32 devices in a mesh: stream: 4 (over y, x), tm: 8 (over z, core).
Axes of the slice: x: 2, y: 2, z: 4, core: 2. Of those that a mesh axis runs over, the one named last changes fastest.
Arguments:
- frames: bfloat16 [16, 8, 256, 512], P('stream', 'tm'), may hold values from -6 to 6
- space_gain: float32 [512], replicated, may hold values from 0.1 to 1.9
- space_input: bfloat16 [512, 1536], replicated, may hold values from -0.25 to 0.25
- space_output: bfloat16 [512, 512], replicated, may hold values from -2 to 2
- space_scale: float32 [512], replicated, may hold values from 0.1 to 1.9
- space_up: bfloat16 [512, 2048], replicated, may hold values from -0.25 to 0.25
- space_down: bfloat16 [2048, 512], replicated, may hold values from -0.125 to 0.125
- time_gain: float32 [512], replicated, may hold values from 0.1 to 1.9
- time_input: bfloat16 [512, 1536], replicated, may hold values from -0.25 to 0.25
- time_output: bfloat16 [512, 512], replicated, may hold values from -1 to 1
- time_scale: float32 [512], replicated, may hold values from 0.1 to 1.9
- time_up: bfloat16 [512, 2048], replicated, may hold values from -0.25 to 0.25
- time_down: bfloat16 [2048, 512], replicated, may hold values from -0.125 to 0.125
- clip_labels: int32 [16, 8], P('stream'), may hold values from 0 to 7, as said below
- output_grad: bfloat16 [16, 8, 256, 512], P('stream', 'tm'), may hold values from -6 to 6
Outputs:
- block_out: float32 [16, 8, 256, 512], P('stream', 'tm')
- input_grad: float32 [16, 8, 256, 512], P('stream', 'tm')
- space_gain_grad: float32 [512], P('tm')
- space_input_grad: float32 [512, 1536], P('tm')
- space_output_grad: float32 [512, 512], P('tm')
- space_scale_grad: float32 [512], P('tm')
- space_up_grad: float32 [512, 2048], P('tm')
- space_down_grad: float32 [2048, 512], P('tm')
- time_gain_grad: float32 [512], P('tm')
- time_input_grad: float32 [512, 1536], P('tm')
- time_output_grad: float32 [512, 512], P('tm')
- time_scale_grad: float32 [512], P('tm')
- time_up_grad: float32 [512, 2048], P('tm')
- time_down_grad: float32 [2048, 512], P('tm')
The draws below stay inside these ranges and needn't reach their ends.
Inputs may be any that keep to these rules, and one draw needn't show every extreme that they name: `clip_labels`: in every pack the labels start at 0 and rise by 0 or 1 from one frame-slot to the next; frame-slots with one label form a clip. In each aligned group of 4 packs one pack is a single clip over all 8 frame-slots, and another pack has a clip of one frame-slot at every frame-slot.
All inputs are finite; a program needn't handle non-finite values.
Results may differ from the reference program's by a relative error of at most 0.025.
Values may be sent and summed in bfloat16 or wider, within the bound.
No kernel may reach another device: no remote copies, remote signals or barrier semaphores. Data moves between devices by JAX's collectives and lax.ppermute only.
A program may use at most 192 MiB of HBM per device.

```python
import jax
import jax.numpy as jnp
from jax import lax

D = 512
HEADS = 8
HEAD_DIM = 64
FF = 2048
PATCHES = 256
PACKS_DEV = 4
PACKS = 16
FRAMES = 8


def draw_clip_labels(key, part):
    key = jax.random.fold_in(key, 11)
    breaks = jax.random.randint(jax.random.fold_in(key, 1), (PACKS, FRAMES), 0, 4) == 0
    chosen = jax.random.randint(jax.random.fold_in(key, 2), (PACKS // PACKS_DEV, 1), 0, PACKS_DEV)
    member_index = (jnp.arange(PACKS) % PACKS_DEV).reshape(PACKS // PACKS_DEV, PACKS_DEV)
    single_clip = (member_index == chosen).reshape(PACKS, 1)
    every_slot = (member_index == (chosen + 1) % PACKS_DEV).reshape(PACKS, 1) & jnp.logical_not(single_clip)
    leading = jnp.arange(FRAMES)[None, :] == 0
    rises = jnp.where(every_slot, 1, breaks.astype(jnp.int32))
    rises = jnp.where(single_clip | leading, 0, rises)
    return jnp.cumsum(rises, axis=1).astype(jnp.int32)


def steps_of(rng, extent, split, least, largest):
    def one(axis_at, shards_of):
        steps = jax.random.uniform(jax.random.fold_in(jax.random.fold_in(rng, 6), axis_at), (shards_of,), jnp.float32, least / len(split), largest / len(split))
        return jnp.repeat(jnp.exp(steps), extent[axis_at] // shards_of).reshape((-1,) + (1,) * (len(extent) - axis_at - 1))

    factor_of = one(*split[0])
    for cut in split[1:]:
        factor_of = factor_of * one(*cut)
    return factor_of


def scatter_about(stream_key, shape, spread, bound, cuts=(), kind=jnp.bfloat16):
    array = spread * jax.random.normal(stream_key, shape, jnp.float32)
    if cuts:
        array = array * steps_of(stream_key, shape, cuts, -0.22, 0.18)
    return jnp.clip(array, -bound, bound).astype(kind)


def setup_inputs(seed: int = 0) -> dict:
    streams_of = jax.random.split(jax.random.key(seed), 16)
    return {
        "frames": scatter_about(streams_of[0], (PACKS, FRAMES, PATCHES, D), 1.0, 6.0, ((0, 4), (1, 8))),
        "space_gain": jnp.clip(1.0 + 0.18 * jax.random.normal(streams_of[1], (D,), jnp.float32), 0.1, 1.9),
        "space_input": scatter_about(streams_of[2], (D, 3 * D), D ** -0.5, 0.25),
        "space_output": scatter_about(streams_of[3], (D, D), (D // 64) ** -0.5, 2.0),
        "space_scale": jnp.clip(1.0 + 0.18 * jax.random.normal(streams_of[4], (D,), jnp.float32), 0.1, 1.9),
        "space_up": scatter_about(streams_of[5], (D, FF), D ** -0.5, 0.25),
        "space_down": scatter_about(streams_of[6], (FF, D), FF ** -0.5, 0.125),
        "time_gain": jnp.clip(1.0 + 0.18 * jax.random.normal(streams_of[7], (D,), jnp.float32), 0.1, 1.9),
        "time_input": scatter_about(streams_of[8], (D, 3 * D), D ** -0.5, 0.25),
        "time_output": scatter_about(streams_of[9], (D, D), (D // 16) ** -0.5, 1.0),
        "time_scale": jnp.clip(1.0 + 0.18 * jax.random.normal(streams_of[10], (D,), jnp.float32), 0.1, 1.9),
        "time_up": scatter_about(streams_of[11], (D, FF), D ** -0.5, 0.25),
        "time_down": scatter_about(streams_of[12], (FF, D), FF ** -0.5, 0.125),
        "clip_labels": draw_clip_labels(jax.random.fold_in(streams_of[15], 71), 0),
        "output_grad": scatter_about(streams_of[14], (PACKS, FRAMES, PATCHES, D), 1.0, 6.0, ((0, 4), (1, 8))),
    }


@jax.custom_vjp
def low(v):
    return lax.optimization_barrier(v.astype(jnp.bfloat16)).astype(jnp.float32)

@jax.custom_vjp
def low_back(v):
    return v

def low_keep(v):
    return (low(v), None)

def low_pass(kept, grad):
    return (grad,)

def back_keep(v):
    return (v, None)

def back_low(kept, grad):
    return (low(grad),)
low.defvjp(low_keep, low_pass)
low_back.defvjp(back_keep, back_low)
highest = lax.Precision.HIGHEST
space_forms = ('fphe,frhe->fhpr', 'fhpr,frhe->fphe')
time_forms = ('fphe,gphe->phfg', 'phfg,gphe->fphe')

def layer_norm(values, gain_vector):
    average = lax.optimization_barrier(jnp.mean(values, axis=-1, keepdims=True))
    centered = values - average
    variance = lax.optimization_barrier(jnp.mean(centered * centered, axis=-1, keepdims=True))
    return centered * lax.rsqrt(variance + 1e-05) * gain_vector

def attend(packed, allowed, einsum_forms):
    queries = packed[:, :, 0]
    key_rows = packed[:, :, 1]
    value_rows = packed[:, :, 2]
    scores = low_back(jnp.einsum(einsum_forms[0], queries, key_rows, precision=highest) * HEAD_DIM ** (-0.5))
    if allowed is not None:
        scores = jnp.where(allowed, scores, -1e+30)
    weights = low(jax.nn.softmax(scores, axis=-1))
    return jnp.einsum(einsum_forms[1], weights, value_rows, precision=highest)

def block(residual, params, allowed, einsum_forms):
    gain_vector, input_weight, output_weight, scale_vector, up_weight, down_weight = params
    frame_count, patch_count, model_width = residual.shape
    stacked = residual.reshape(frame_count * patch_count, model_width)
    normed = low(layer_norm(stacked, gain_vector))
    packed = low(low_back(jnp.dot(normed, input_weight, precision=highest)))
    mixed = attend(packed.reshape(frame_count, patch_count, 3, HEADS, model_width // HEADS), allowed, einsum_forms)
    mixed = low(low_back(mixed.reshape(frame_count * patch_count, model_width)))
    middle = stacked + low_back(jnp.dot(mixed, output_weight, precision=highest))
    second = low(layer_norm(middle, scale_vector))
    before = low_back(jnp.dot(second, up_weight, precision=highest))
    hidden = low(jax.nn.gelu(before, approximate=True))
    result = middle + low_back(jnp.dot(hidden, down_weight, precision=highest))
    return result.reshape(residual.shape)

def forward(sequence, labels, params):
    positions = jnp.arange(sequence.shape[0])
    allowed = (labels[:, None] == labels[None, :]) & (positions[None, :] <= positions[:, None])
    middle = block(sequence, params[:6], None, space_forms)
    return block(middle, params[6:], allowed, time_forms)

def reference(frames, space_gain, space_input, space_output, space_scale, space_up, space_down, time_gain, time_input, time_output, time_scale, time_up, time_down, clip_labels, output_grad):
    params = tuple((partial_item.astype(jnp.float32) for partial_item in (space_gain, space_input, space_output, space_scale, space_up, space_down, time_gain, time_input, time_output, time_scale, time_up, time_down)))

    def one_sequence(running, scanned):
        sequence, labels, cotangent = scanned

        def sequence_forward(sequence_in, *weights):
            return forward(sequence_in, labels, weights)
        result, pullback = jax.vjp(sequence_forward, sequence.astype(jnp.float32), *params)
        gradients = pullback(cotangent.astype(jnp.float32))
        updated = tuple((total_sum + new_term for total_sum, new_term in zip(running, gradients[1:])))
        return (updated, (result, gradients[0]))
    initial_sums = tuple((jnp.zeros_like(partial_item) for partial_item in params))
    totals, (outputs, input_grads) = lax.scan(one_sequence, initial_sums, (frames, clip_labels, output_grad))
    return (outputs, input_grads, totals[0], totals[1], totals[2], totals[3], totals[4], totals[5], totals[6], totals[7], totals[8], totals[9], totals[10], totals[11])
```

```python
import functools

import jax
import jax.numpy as jnp
from jax import lax
from jax.experimental import pallas as pl
from jax.experimental.pallas import tpu as pltpu
from jax.sharding import PartitionSpec as P

HEADS = 8
EPS = 1e-05
GELU_A = 0.7978845608028654
GELU_B = 0.044715
BF = jnp.bfloat16
F32 = jnp.float32
CHUNK = 512
VMEM = 44 * 1024 * 1024


def nn(a, b):
    return jnp.dot(a, b, preferred_element_type=F32)


def nt(a, b):
    return lax.dot_general(a, b, (((1,), (1,)), ((), ())), preferred_element_type=F32)


def tn(a, b):
    return lax.dot_general(a, b, (((0,), (0,)), ((), ())), preferred_element_type=F32)


def unit(values):
    average = jnp.mean(values, axis=-1, keepdims=True)
    centered = values - average
    inverse = lax.rsqrt(jnp.mean(centered * centered, axis=-1, keepdims=True) + EPS)
    return centered * inverse, inverse


def unit_backward(grad, unit_rows, inverse):
    first = jnp.mean(grad, axis=-1, keepdims=True)
    second = jnp.mean(grad * unit_rows, axis=-1, keepdims=True)
    return inverse * (grad - first - unit_rows * second)


def gelu_parts(u):
    square = u * u
    tangent = jnp.tanh(u * (GELU_A + (GELU_A * GELU_B) * square))
    half = 0.5 * u
    value = half + half * tangent
    slope = (0.5 + 0.5 * tangent) + half * (1.0 - tangent * tangent) * (
        GELU_A + (3.0 * GELU_A * GELU_B) * square
    )
    return value, slope


def head_masks(width):
    lane = lax.broadcasted_iota(jnp.int32, (1, 2 * width), 1)
    low = lane < width
    return low, (low.astype(F32).astype(BF), (1.0 - low.astype(F32)).astype(BF))


def attend(qkv_ref, p_ref, o_ref, bias_ref):
    width = qkv_ref.shape[1] // 3
    size = width // HEADS
    low, masks = head_masks(size)
    for pair in range(HEADS // 2):
        at = pair * 2 * size
        q = qkv_ref[:, at : at + 2 * size] * BF(size**-0.5)
        k = qkv_ref[:, width + at : width + at + 2 * size]
        v = qkv_ref[:, 2 * width + at : 2 * width + at + 2 * size]
        both = []
        for side in range(2):
            scores = nt(k * masks[side], q)
            if bias_ref is not None:
                scores = scores + bias_ref[...]
            top = jnp.max(scores, axis=0, keepdims=True)
            e = jnp.exp(scores - top)
            total = jnp.sum(e, axis=0, keepdims=True)
            p = (e * (1.0 / total)).astype(BF)
            p_ref[2 * pair + side] = p
            both.append(tn(p, v))
        o_ref[:, at : at + 2 * size] = jnp.where(low, both[0], both[1]).astype(BF)


def attend_backward(qkv_ref, p_ref, go_ref, out_ref):
    width = qkv_ref.shape[1] // 3
    size = width // HEADS
    low, masks = head_masks(size)
    for pair in range(HEADS // 2):
        at = pair * 2 * size
        q = qkv_ref[:, at : at + 2 * size] * BF(size**-0.5)
        k = qkv_ref[:, width + at : width + at + 2 * size] * BF(size**-0.5)
        v = qkv_ref[:, 2 * width + at : 2 * width + at + 2 * size]
        go = go_ref[:, at : at + 2 * size]
        gq, gk, gv = [], [], []
        for side in range(2):
            p = p_ref[2 * pair + side]
            gv.append(nn(p, go))
            gp = nt(v * masks[side], go)
            p32 = p.astype(F32)
            weighted = p32 * gp
            gs = (weighted - p32 * jnp.sum(weighted, axis=0, keepdims=True)).astype(BF)
            gk.append(nn(gs, q))
            gq.append(tn(gs, k))
        out_ref[:, at : at + 2 * size] = jnp.where(low, gq[0], gq[1]).astype(BF)
        out_ref[:, width + at : width + at + 2 * size] = jnp.where(low, gk[0], gk[1]).astype(BF)
        out_ref[:, 2 * width + at : 2 * width + at + 2 * size] = jnp.where(
            low, gv[0], gv[1]
        ).astype(BF)


def feed_up(m, up_ref, down_ref, h_ref, slope_ref):
    total = None
    for at in range(0, up_ref.shape[1], CHUNK):
        value, slope = gelu_parts(nn(m, up_ref[:, at : at + CHUNK]))
        h = value.astype(BF)
        h_ref[:, at : at + CHUNK] = h
        slope_ref[:, at : at + CHUNK] = slope.astype(BF)
        term = nn(h, down_ref[at : at + CHUNK, :])
        total = term if total is None else total + term
    return total


def feed_back(e2, up_ref, down_ref, slope_ref, eu_ref):
    total = None
    for at in range(0, up_ref.shape[1], CHUNK):
        gh = nt(e2, down_ref[at : at + CHUNK, :])
        eu = (gh * slope_ref[:, at : at + CHUNK].astype(F32)).astype(BF)
        eu_ref[:, at : at + CHUNK] = eu
        term = nt(eu, up_ref[:, at : at + CHUNK])
        total = term if total is None else total + term
    return total


def rows_of(block):
    slots, _, patches, width = block.shape
    return block[:, 0].astype(F32).reshape(slots * patches, width)


def block_of(rows, ref):
    slots, _, patches, width = ref.shape
    ref[:, 0] = rows.reshape(slots, patches, width).astype(ref.dtype)


def space_forward(
    local, order, frames, gain, w_in, w_out, scale, w_up, w_down, *rest
):
    x2, z0, inv0, qkv, p, o, z1, inv1, h, slope = rest[-10:]
    x = frames[0, 0].astype(F32)
    unit0, inverse0 = unit(x)
    z0[0] = unit0.astype(BF)
    inv0[0] = inverse0
    qkv[0] = nn((unit0 * gain[...]).astype(BF), w_in[...]).astype(BF)
    attend(qkv.at[0], p.at[0], o.at[0], None)
    r1 = x + nn(o[0], w_out[...])
    unit1, inverse1 = unit(r1)
    z1[0] = unit1.astype(BF)
    inv1[0] = inverse1
    m = (unit1 * scale[...]).astype(BF)
    r2 = r1 + feed_up(m, w_up, w_down, h.at[0], slope.at[0])
    if local:
        x2[0] = r2
    else:
        block_of(r2, x2)


def build_bias(labels, pack, slots, patches, bias):
    tokens = slots * patches
    row = lax.broadcasted_iota(jnp.int32, (1, tokens), 1)
    column = lax.broadcasted_iota(jnp.int32, (tokens, 1), 0)

    def label_of(position):
        slot = position // patches
        value = jnp.zeros_like(position)
        for f in range(slots):
            value = jnp.where(slot == f, labels[pack, f], value)
        return value

    same_patch = (row % patches) == (column % patches)
    allowed = same_patch & (column <= row) & (label_of(column) == label_of(row))
    bias[...] = jnp.where(allowed, 0.0, -1e30)


def time_both(
    order, labels, x2, grad, gain, w_in, w_out, scale, w_up, w_down, *rest
):
    g0, out, z0, gqkv, o, e1, z1, eu, h, e2 = rest[-14:-4]
    qkv, p, slope, bias = rest[-4:]
    slots, _, patches, _ = x2.shape
    build_bias(labels, order[pl.program_id(0)], slots, patches, bias)
    x = rows_of(x2[...])
    unit0, inverse0 = unit(x)
    z0[0] = unit0.astype(BF)
    qkv[...] = nn((unit0 * gain[...]).astype(BF), w_in[...]).astype(BF)
    attend(qkv, p, o.at[0], bias)
    r1 = x + nn(o[0], w_out[...])
    unit1, inverse1 = unit(r1)
    z1[0] = unit1.astype(BF)
    m = (unit1 * scale[...]).astype(BF)
    block_of(r1 + feed_up(m, w_up, w_down, h.at[0], slope), out)
    g2 = rows_of(grad[...])
    e2[0] = g2.astype(BF)
    gm = feed_back(e2[0], w_up, w_down, slope, eu.at[0])
    g1 = g2 + unit_backward(gm * scale[...], unit1, inverse1)
    e1[0] = g1.astype(BF)
    slope[:, : g1.shape[1]] = nt(e1[0], w_out[...]).astype(BF)
    attend_backward(qkv, p, slope, gqkv.at[0])
    gn = nt(gqkv[0], w_in[...])
    block_of(g1 + unit_backward(gn * gain[...], unit0, inverse0), g0)


def time_alone(
    order, x2, grad, gain, w_in, w_out, scale, w_up, w_down, *rest
):
    g0, out, z0, gqkv, o, e1, z1, eu, h, e2 = rest[-11:-1]
    slope = rest[-1]
    x = x2[0]
    width = x.shape[1]
    unit0, inverse0 = unit(x)
    z0[0] = unit0.astype(BF)
    o[0] = nn((unit0 * gain[...]).astype(BF), w_in[:, 2 * width :]).astype(BF)
    r1 = x + nn(o[0], w_out[...])
    unit1, inverse1 = unit(r1)
    z1[0] = unit1.astype(BF)
    m = (unit1 * scale[...]).astype(BF)
    out[0, 0] = r1 + feed_up(m, w_up, w_down, h.at[0], slope)
    e2[0] = grad[0, 0]
    g2 = grad[0, 0].astype(F32)
    gm = feed_back(e2[0], w_up, w_down, slope, eu.at[0])
    g1 = g2 + unit_backward(gm * scale[...], unit1, inverse1)
    e1[0] = g1.astype(BF)
    gv = nt(e1[0], w_out[...]).astype(BF)
    gqkv[0, :, : 2 * width] = jnp.zeros((x.shape[0], 2 * width), BF)
    gqkv[0, :, 2 * width :] = gv
    gn = nt(gv, w_in[:, 2 * width :])
    g0[0] = g1 + unit_backward(gn * gain[...], unit0, inverse0)


def space_back_feed(
    local, order, grad, z1, inv1, slope, w_out, scale, w_up, w_down, *rest
):
    eu, e2, e1, go, g1 = rest[-5:]
    g2 = grad[0] if local else rows_of(grad[...])
    e2[0] = g2.astype(BF)
    gm = feed_back(e2[0], w_up, w_down, slope.at[0], eu.at[0])
    total = g2 + unit_backward(gm * scale[...], z1[0].astype(F32), inv1[0])
    g1[0] = total
    e1[0] = total.astype(BF)
    go[0] = nt(e1[0], w_out[...]).astype(BF)


def space_back_attend(order, qkv, p, go, *rest):
    attend_backward(qkv.at[0], p.at[0], go.at[0], rest[-1].at[0])


def space_back_in(order, gqkv, w_in, gain, z0, inv0, g1, *rest):
    gn = nt(gqkv[0], w_in[...])
    rest[-1][0, 0] = g1[0] + unit_backward(gn * gain[...], z0[0].astype(F32), inv0[0])


def to_send(order, grad, out):
    block_of(grad[0, 0].astype(F32), out)


def from_received(order, block, before, out):
    out[0, 0] = rows_of(block[...])


class Packs:
    def __init__(self, order, labels, first, count, slots, patches):
        self.scalars = (order, labels)
        self.first, self.count = first, count
        self.slots, self.patches = slots, patches

    def call(self, kernel, args, outs, scratch=(), labels=False, flops=0):
        first = self.first
        scalars = self.scalars if labels else self.scalars[:1]

        def spec(kind, shape):
            rank = len(shape)
            if kind == "whole":
                return pl.BlockSpec(shape, lambda i, *s: (0,) * rank)
            if kind == "pack":
                return pl.BlockSpec(
                    (1,) + tuple(shape[1:]), lambda i, *s: (s[0][first + i],) + (0,) * (rank - 1)
                )
            if kind == "place":
                return pl.BlockSpec(
                    (1,) + tuple(shape[1:]), lambda i, *s: (first + i,) + (0,) * (rank - 1)
                )
            if kind == "step":
                return pl.BlockSpec(
                    (1,) + tuple(shape[1:]), lambda i, *s: (i,) + (0,) * (rank - 1)
                )
            if kind == "moved":
                return pl.BlockSpec(
                    (shape[0], 1, shape[2], shape[3]), lambda i, *s: (0, i, 0, 0)
                )
            return pl.BlockSpec(memory_space=pl.ANY)

        in_specs = [spec(kind, array.shape) for kind, array in args]
        operands = [array for _, array in args]
        aliases = {}
        for index, (kind, shape, dtype, into) in enumerate(outs):
            if into is not None:
                aliases[len(scalars) + len(operands)] = index
                operands.append(into)
                in_specs.append(pl.BlockSpec(memory_space=pl.ANY))
        moved = sum(a.size * a.dtype.itemsize for a in operands)
        return pl.pallas_call(
            kernel,
            out_shape=[jax.ShapeDtypeStruct(shape, dtype) for _, shape, dtype, _ in outs],
            grid_spec=pltpu.PrefetchScalarGridSpec(
                num_scalar_prefetch=len(scalars),
                grid=(self.count,),
                in_specs=in_specs,
                out_specs=[spec(kind, shape) for kind, shape, _, _ in outs],
                scratch_shapes=list(scratch),
            ),
            input_output_aliases=aliases,
            compiler_params=pltpu.CompilerParams(
                vmem_limit_bytes=VMEM, dimension_semantics=("arbitrary",)
            ),
            cost_estimate=pl.CostEstimate(
                flops=int(flops * self.count), bytes_accessed=int(moved), transcendentals=0
            ),
        )(*scalars, *operands)


def feed_weights_kernel(ids, z1, e2, eu, h, mine, other, left):
    step = pl.program_id(0)
    core, z_at, s_at = ids[0], ids[1], ids[2]
    first = core == 0

    def put(at, rows, even, odd):
        mine[at[0], at[1], rows] = jnp.where(first, even, odd)
        other[at[0], at[1], rows] = jnp.where(first, odd, even)

    @pl.when(step == 0)
    def _():
        left[...] = z1[...].T

    @pl.when(step == 4)
    def _():
        left[...] = e2[...].T

    @pl.when(step < 4)
    def _():
        tile = nn(left[...], eu[...]).astype(BF)
        for z in range(4):
            even, odd = tile[128 * z : 128 * z + 64], tile[128 * z + 64 : 128 * z + 128]
            put((step ^ s_at, z ^ z_at), slice(0, 64), even, odd)

    @pl.when(step >= 4)
    def _():
        tile = nn(left[...], h[...]).astype(BF)
        z = step - 4
        for s in range(4):
            upper, lower = tile[128 * s : 128 * s + 64], tile[128 * s + 64 : 128 * s + 128]
            even = jnp.concatenate([upper[:, :256], lower[:, :256]], axis=1)
            odd = jnp.concatenate([upper[:, 256:], lower[:, 256:]], axis=1)
            put((s ^ s_at, z ^ z_at), slice(64, 128), even, odd)


def attend_weights_kernel(ids, z0, o, gqkv, e1, mine, other, left):
    step = pl.program_id(0)
    core, z_at, s_at = ids[0], ids[1], ids[2]
    first = core == 0

    def put_all(tile, index):
        for z in range(4):
            for s in range(4):
                at = 128 * z + 16 * s
                even, odd = tile[at : at + 16], tile[at + 64 : at + 80]
                rows = slice(16 * index, 16 * index + 16)
                mine[s ^ s_at, z ^ z_at, rows] = jnp.where(first, even, odd)
                other[s ^ s_at, z ^ z_at, rows] = jnp.where(first, odd, even)

    @pl.when(step == 0)
    def _():
        left[...] = z0[...].T

    @pl.when(step == 3)
    def _():
        left[...] = o[...].T

    for index in range(4):

        @pl.when(step == index)
        def _():
            right = gqkv if index < 3 else e1
            put_all(nn(left[...], right[...]).astype(BF), index)


def weights_call(kernel, ids, steps, rows, args):
    def spec(kind, shape):
        if kind == "whole":
            return pl.BlockSpec(shape, lambda i, *s: (0, 0))
        low, high = kind
        return pl.BlockSpec(
            (shape[0], CHUNK), lambda i, *s: (0, jnp.clip(i - low, 0, high - low))
        )

    tokens = args[0][1].shape[0]
    out = jax.ShapeDtypeStruct((4, 4, rows, CHUNK), BF)
    out_spec = pl.BlockSpec((4, 4, rows, CHUNK), lambda i, *s: (0, 0, 0, 0))
    return pl.pallas_call(
        kernel,
        out_shape=[out, out],
        grid_spec=pltpu.PrefetchScalarGridSpec(
            num_scalar_prefetch=1,
            grid=(steps,),
            in_specs=[spec(kind, array.shape) for kind, array in args],
            out_specs=[out_spec, out_spec],
            scratch_shapes=[pltpu.VMEM((CHUNK, tokens), BF)],
        ),
        compiler_params=pltpu.CompilerParams(
            vmem_limit_bytes=VMEM, dimension_semantics=("arbitrary",)
        ),
        cost_estimate=pl.CostEstimate(
            flops=steps * 2 * tokens * CHUNK * CHUNK,
            bytes_accessed=sum(a.size * 2 for _, a in args),
            transcendentals=0,
        ),
    )(ids, *[array for _, array in args])


def swap(array, axis, size, mask):
    return lax.ppermute(array, axis, [(i, i ^ mask) for i in range(size)])


def add(*terms):
    total = terms[0].astype(F32)
    for term in terms[1:]:
        total = total + term.astype(F32)
    return total.astype(BF)


def reduce_parts(mine, other):
    got = swap(other, "tm", 8, 1)
    parts = [add(mine[d], got[d]) for d in range(4)]
    got = [swap(parts[d], "stream", 4, d) for d in range(1, 4)]
    rows = [add(parts[0][d], got[0][d], got[1][d], got[2][d]) for d in range(4)]
    got = [swap(rows[d], "tm", 8, 2 * d) for d in range(1, 4)]
    final = add(rows[0], *got)
    return [final] + [swap(final, "stream", 4, d) for d in range(1, 4)]


def column(row):
    size = row.shape[1]
    eye = lax.broadcasted_iota(jnp.int32, (size, size), 0) == lax.broadcasted_iota(
        jnp.int32, (size, size), 1
    )
    return jnp.sum(jnp.where(eye, row, 0.0), axis=1, keepdims=True)


def as_row(col):
    size = col.shape[0]
    eye = lax.broadcasted_iota(jnp.int32, (size, size), 0) == lax.broadcasted_iota(
        jnp.int32, (size, size), 1
    )
    return jnp.sum(jnp.where(eye, col, 0.0), axis=0, keepdims=True)


def own_rows(ids, vector):
    rank = 2 * ids[1] + ids[0]
    return column(vector[pl.ds(rank, 1), :])


def finish_feed_kernel(ids, p0, p1, p2, p3, w_up, scale, scale_grad, up_grad, down_grad):
    s_at = ids[2]
    factor = own_rows(ids, scale)
    for d, piece in enumerate((p0, p1, p2, p3)):
        s = s_at ^ d
        up_grad[:, pl.ds(pl.multiple_of(512 * s, 512), 512)] = piece[:64].astype(F32)
        lower = piece[64:].astype(F32)
        whole = jnp.concatenate([lower[:, :256], lower[:, 256:]], axis=0)
        down_grad[:, pl.ds(pl.multiple_of(128 * s, 128), 128)] = whole.T
    total = up_grad[...]
    scale_grad[...] = as_row(jnp.sum(total * w_up[...].astype(F32), axis=1, keepdims=True))
    up_grad[...] = total * factor


def finish_attend_kernel(ids, p0, p1, p2, p3, w_in, gain, gain_grad, in_grad, out_grad):
    s_at = ids[2]
    factor = own_rows(ids, gain)
    for d, piece in enumerate((p0, p1, p2, p3)):
        rows = pl.ds(pl.multiple_of(16 * (s_at ^ d), 16), 16)
        for third in range(3):
            in_grad[rows, 512 * third : 512 * third + 512] = piece[
                16 * third : 16 * third + 16
            ].astype(F32)
        out_grad[rows, :] = piece[48:].astype(F32)
    total = in_grad[...]
    gain_grad[...] = as_row(jnp.sum(total * w_in[...].astype(F32), axis=1, keepdims=True))
    in_grad[...] = total * factor


def finish_call(kernel, ids, pieces, weight, vector, outs):
    height = weight.shape[0] // 8
    whole = pl.BlockSpec(pieces[0].shape, lambda i, *s: (0, 0))
    results = pl.pallas_call(
        kernel,
        out_shape=[jax.ShapeDtypeStruct(shape, F32) for shape in outs],
        grid_spec=pltpu.PrefetchScalarGridSpec(
            num_scalar_prefetch=1,
            grid=(1,),
            in_specs=[whole] * 4
            + [
                pl.BlockSpec((height, weight.shape[1]), lambda i, s: (2 * s[1] + s[0], 0)),
                pl.BlockSpec((8, height), lambda i, *s: (0, 0)),
            ],
            out_specs=[pl.BlockSpec(shape, lambda i, *s: (0, 0)) for shape in outs],
        ),
        compiler_params=pltpu.CompilerParams(vmem_limit_bytes=VMEM),
    )(ids, *pieces, weight, vector.reshape(8, height))
    return [results[0].reshape(-1)] + list(results[1:])


def plain_weights(z, grads, weight, vector):
    product = tn(z, grads)
    vector_grad = jnp.sum(product * weight.astype(F32), axis=1)
    return vector_grad, product * vector[:, None]


def plain_reduce(array):
    share = lax.psum_scatter(array.astype(BF), "tm", scatter_dimension=0, tiled=True)
    return lax.psum(share, "stream").astype(F32)


def per_device(
    ranks,
    streams,
    frames,
    space_gain,
    space_input,
    space_output,
    space_scale,
    space_up,
    space_down,
    time_gain,
    time_input,
    time_output,
    time_scale,
    time_up,
    time_down,
    clip_labels,
    output_grad,
):
    packs, _, tokens, width = frames.shape
    slots = clip_labels.shape[1]
    patches = tokens // ranks
    hidden = space_up.shape[1]
    some = packs - 1
    hierarchical = (ranks, streams) == (8, 4)
    tm = lax.axis_index("tm")
    ids = jnp.stack([tm % 2, tm // 2, lax.axis_index("stream")]).astype(jnp.int32)

    alone = jnp.argmax(clip_labels[:, -1] == slots - 1).astype(jnp.int32)
    place = jnp.arange(packs, dtype=jnp.int32)
    order = jnp.where(place == packs - 1, alone, place + (place >= alone))
    shared = Packs(order, clip_labels, 0, some, slots, patches)
    single = Packs(order, clip_labels, some, 1, slots, patches)

    row = lambda vector: vector.reshape(1, -1)
    moved = ("moved", (slots, some, patches, width), BF, None)

    def kept(*widths):
        return [("place", (packs, tokens) + w, t, None) for *w, t in [tuple(w) for w in widths]]

    def into(specs, arrays):
        return [(kind, shape, dtype, a) for (kind, shape, dtype, _), a in zip(specs, arrays)]

    def exchange(array):
        return lax.all_to_all(array, "tm", split_axis=0, concat_axis=0, tiled=True)

    def place_spec(*tail, dtype=BF):
        return ("place", (packs,) + tail, dtype, None)

    (sent,) = shared.call(to_send, [("pack", output_grad)], [moved])
    grad_moved = exchange(sent)

    space_args = [
        ("pack", frames),
        ("whole", row(space_gain)),
        ("whole", space_input),
        ("whole", space_output),
        ("whole", row(space_scale)),
        ("whole", space_up),
        ("whole", space_down),
    ]
    state = [
        place_spec(tokens, width),
        place_spec(tokens, 1, dtype=F32),
        place_spec(tokens, 3 * width),
        place_spec(HEADS, tokens, tokens),
        place_spec(tokens, width),
        place_spec(tokens, width),
        place_spec(tokens, 1, dtype=F32),
        place_spec(tokens, hidden),
        place_spec(tokens, hidden),
    ]
    flops = 2 * tokens * width * (4 * width + 2 * hidden)
    x2, *held = shared.call(
        functools.partial(space_forward, False), space_args, [moved] + state, flops=flops
    )
    x2_moved = exchange(x2)
    local = ("step", (1, tokens, width), F32, None)
    x2_alone, *held = single.call(
        functools.partial(space_forward, True),
        space_args,
        [local] + into(state, held),
        flops=flops,
    )
    sz0, sinv0, sqkv, sp, so, sz1, sinv1, sh, sslope = held

    time_args = [
        ("whole", row(time_gain)),
        ("whole", time_input),
        ("whole", time_output),
        ("whole", row(time_scale)),
        ("whole", time_up),
        ("whole", time_down),
    ]
    state = [
        place_spec(tokens, width),
        place_spec(tokens, 3 * width),
        place_spec(tokens, width),
        place_spec(tokens, width),
        place_spec(tokens, width),
        place_spec(tokens, hidden),
        place_spec(tokens, hidden),
        place_spec(tokens, width),
    ]
    g0_alone, result, *held = single.call(
        time_alone,
        [("step", x2_alone), ("pack", output_grad)] + time_args,
        [local, ("pack", frames.shape, F32, None)] + state,
        scratch=[pltpu.VMEM((tokens, hidden), BF)],
        flops=3 * flops,
    )
    g0, out, *held = shared.call(
        time_both,
        [("moved", x2_moved), ("moved", grad_moved)] + time_args,
        [moved, moved] + into(state, held),
        scratch=[
            pltpu.VMEM((tokens, 3 * width), BF),
            pltpu.VMEM((HEADS, tokens, tokens), BF),
            pltpu.VMEM((tokens, hidden), BF),
            pltpu.VMEM((tokens, tokens), F32),
        ],
        labels=True,
        flops=3 * flops,
    )
    tz0, tgqkv, to, te1, tz1, teu, th, te2 = held
    g0_moved = exchange(g0)
    out_moved = exchange(out)

    def flat(array):
        return array.reshape(packs * tokens, array.shape[-1])

    def feed_weights(z1, eu, h, e2):
        return weights_call(
            feed_weights_kernel,
            ids,
            8,
            128,
            [("whole", flat(z1)), ("whole", flat(e2)), ((0, 3), flat(eu)), ((4, 7), flat(h))],
        )

    def attend_weights(z0, gqkv, o, e1):
        return weights_call(
            attend_weights_kernel,
            ids,
            4,
            64,
            [("whole", flat(z0)), ("whole", flat(o)), ((0, 2), flat(gqkv)), ("whole", flat(e1))],
        )

    def feed_grads(z1, eu, h, e2, scale, up):
        if hierarchical:
            pieces = reduce_parts(*feed_weights(z1, eu, h, e2))
            return finish_call(
                finish_feed_kernel,
                ids,
                pieces,
                up,
                scale,
                [(1, width // 8), (width // 8, hidden), (hidden // 8, width)],
            )
        scale_grad, up_grad = plain_weights(flat(z1), flat(eu), up, scale)
        return [plain_reduce(a) for a in (scale_grad, up_grad, tn(flat(h), flat(e2)))]

    def attend_grads(z0, gqkv, o, e1, gain, w_in):
        if hierarchical:
            pieces = reduce_parts(*attend_weights(z0, gqkv, o, e1))
            return finish_call(
                finish_attend_kernel,
                ids,
                pieces,
                w_in,
                gain,
                [(1, width // 8), (width // 8, 3 * width), (width // 8, width)],
            )
        gain_grad, in_grad = plain_weights(flat(z0), flat(gqkv), w_in, gain)
        return [plain_reduce(a) for a in (gain_grad, in_grad, tn(flat(o), flat(e1)))]

    time_feed = feed_grads(tz1, teu, th, te2, time_scale, time_up)
    time_attend = attend_grads(tz0, tgqkv, to, te1, time_gain, time_input)

    back = [
        place_spec(tokens, hidden),
        place_spec(tokens, width),
        place_spec(tokens, width),
        place_spec(tokens, width),
        place_spec(tokens, width, dtype=F32),
    ]
    feed_args = [
        ("place", sz1),
        ("place", sinv1),
        ("place", sslope),
        ("whole", space_output),
        ("whole", row(space_scale)),
        ("whole", space_up),
        ("whole", space_down),
    ]
    held = single.call(
        functools.partial(space_back_feed, True), [("step", g0_alone)] + feed_args, back, flops=flops
    )
    held = shared.call(
        functools.partial(space_back_feed, False),
        [("moved", g0_moved)] + feed_args,
        into(back, held),
        flops=flops,
    )
    seu, se2, se1, sgo, sg1 = held
    space_feed = feed_grads(sz1, seu, sh, se2, space_scale, space_up)
    whole_packs = Packs(order, clip_labels, 0, packs, slots, patches)
    (sgqkv,) = whole_packs.call(
        space_back_attend,
        [("place", sqkv), ("place", sp), ("place", sgo)],
        [place_spec(tokens, 3 * width)],
        flops=flops,
    )
    space_attend = attend_grads(sz0, sgqkv, so, se1, space_gain, space_input)
    (input_grad,) = whole_packs.call(
        space_back_in,
        [
            ("place", sgqkv),
            ("whole", space_input),
            ("whole", row(space_gain)),
            ("place", sz0),
            ("place", sinv0),
            ("place", sg1),
        ],
        [("pack", frames.shape, F32, None)],
        flops=flops // 4,
    )
    (result,) = shared.call(
        from_received, [("moved", out_moved)], [("pack", frames.shape, F32, result)]
    )
    return (
        result,
        input_grad,
        space_attend[0],
        space_attend[1],
        space_attend[2],
        space_feed[0],
        space_feed[1],
        space_feed[2],
        time_attend[0],
        time_attend[1],
        time_attend[2],
        time_feed[0],
        time_feed[1],
        time_feed[2],
    )


def solution(mesh):
    tokens = P("stream", "tm", None, None)
    vector, matrix = P("tm"), P("tm", None)
    return jax.shard_map(
        functools.partial(per_device, mesh.shape["tm"], mesh.shape["stream"]),
        mesh=mesh,
        in_specs=(tokens,) + (P(),) * 12 + (P("stream", None), tokens),
        out_specs=(tokens, tokens) + (vector, matrix, matrix, vector, matrix, matrix) * 2,
        check_vma=False,
    )
```

```python
import functools

import jax
import jax.numpy as jnp
from jax import lax
from jax.experimental import pallas as pl
from jax.experimental.pallas import tpu as pltpu
from jax.sharding import PartitionSpec as P

HEADS = 8
EPS = 1e-05
GELU_A = 0.7978845608028654
GELU_B = 0.044715
BF = jnp.bfloat16
F32 = jnp.float32
CHUNK = 512
LANES = 128
VMEM = 60 * 1024 * 1024


def nn(a, b):
    return jnp.dot(a, b, preferred_element_type=F32)


def nt(a, b):
    return lax.dot_general(a, b, (((1,), (1,)), ((), ())), preferred_element_type=F32)


def tn(a, b):
    return lax.dot_general(a, b, (((0,), (0,)), ((), ())), preferred_element_type=F32)


def unit(values):
    average = jnp.mean(values, axis=-1, keepdims=True)
    centered = values - average
    inverse = lax.rsqrt(jnp.mean(centered * centered, axis=-1, keepdims=True) + EPS)
    return centered * inverse, inverse


def unit_backward(grad, unit_rows, inverse):
    first = jnp.mean(grad, axis=-1, keepdims=True)
    second = jnp.mean(grad * unit_rows, axis=-1, keepdims=True)
    return inverse * (grad - first - unit_rows * second)


def gelu_parts(u):
    square = u * u
    tangent = jnp.tanh(u * (BF(GELU_A) + BF(GELU_A * GELU_B) * square))
    half = BF(0.5) * u
    value = half + half * tangent
    slope = (BF(0.5) + BF(0.5) * tangent) + half * (BF(1.0) - tangent * tangent) * (
        BF(GELU_A) + BF(3.0 * GELU_A * GELU_B) * square
    )
    return value, slope


def head_masks(width):
    lane = lax.broadcasted_iota(jnp.int32, (1, 2 * width), 1)
    low = lane < width
    return low, (low.astype(F32).astype(BF), (1.0 - low.astype(F32)).astype(BF))


def attend(qkv_ref, p_ref, o_ref, bias_ref, s_ref):
    width = qkv_ref.shape[1] // 3
    size = width // HEADS
    _, masks = head_masks(size)

    def lanes(part, head):
        at = part * width + (head // 2) * 2 * size
        return qkv_ref[:, at : at + 2 * size]

    def score(head):
        s_ref[head % 4] = nt(lanes(1, head) * masks[head % 2], lanes(0, head) * BF(size**-0.5))

    def soften(head):
        scores = s_ref[head % 4]
        if bias_ref is not None:
            scores = scores + bias_ref[...]
        e = jnp.exp(scores - jnp.max(scores, axis=0, keepdims=True))
        p_ref[head] = (e * (1.0 / jnp.sum(e, axis=0, keepdims=True))).astype(BF)

    for head in range(0, HEADS, 2):
        if head == 0:
            score(0)
            score(1)
        if head + 2 < HEADS:
            score(head + 2)
            score(head + 3)
        soften(head)
        soften(head + 1)
    for head in range(0, HEADS, 2):
        v = lanes(2, head).T
        both = jnp.concatenate([nn(v[:size], p_ref[head]), nn(v[size:], p_ref[head + 1])], axis=0)
        o_ref[:, head * size : (head + 2) * size] = both.T.astype(BF)


def attend_backward(qkv_ref, p_ref, go_ref, out_ref, gp_ref, gs_ref):
    width = qkv_ref.shape[1] // 3
    size = width // HEADS
    _, masks = head_masks(size)

    def lanes(part, head):
        at = part * width + (head // 2) * 2 * size
        return qkv_ref[:, at : at + 2 * size]

    def gos(head):
        return go_ref[:, (head // 2) * 2 * size : (head // 2 + 1) * 2 * size]

    def put(part, head, value):
        at = part * width + head * size
        out_ref[:, at : at + 2 * size] = value.astype(BF)

    def start(head):
        for h in (head, head + 1):
            gp_ref[h % 4] = nt(lanes(2, h) * masks[h % 2], gos(h)).astype(BF)
        g = gos(head)
        put(2, head, nn(p_ref[head], g * masks[0]) + nn(p_ref[head + 1], g * masks[1]))

    def middle(head):
        p = p_ref[head]
        weighted = p * gp_ref[head % 4]
        total = jnp.sum(weighted.astype(F32), axis=0, keepdims=True).astype(BF)
        gs_ref[head] = weighted - p * total

    def finish(head):
        q = lanes(0, head) * BF(size**-0.5)
        k = (lanes(1, head) * BF(size**-0.5)).T
        put(1, head, nn(gs_ref[head], q * masks[0]) + nn(gs_ref[head + 1], q * masks[1]))
        both = jnp.concatenate([nn(k[:size], gs_ref[head]), nn(k[size:], gs_ref[head + 1])], axis=0)
        put(0, head, both.T)

    start(0)
    for head in range(0, HEADS, 2):
        middle(head)
        middle(head + 1)
        if head + 2 < HEADS:
            start(head + 2)
        if head > 0:
            finish(head - 2)
    finish(HEADS - 2)


def feed_up(m, up_ref, down_ref, h_ref, slope_ref, u_ref):
    steps = up_ref.shape[1] // CHUNK

    def before(step):
        u_ref[step % 2] = nn(m, up_ref[:, step * CHUNK : (step + 1) * CHUNK]).astype(BF)

    before(0)
    for step in range(steps):
        if step + 1 < steps:
            before(step + 1)
        at = step * CHUNK
        h_ref[:, at : at + CHUNK], slope_ref[:, at : at + CHUNK] = gelu_parts(u_ref[step % 2])
    return nn(h_ref[...], down_ref[...])


def feed_back(e2, up_ref, down_ref, slope_ref, eu_ref):
    for at in range(0, up_ref.shape[1], CHUNK):
        gh = nt(e2, down_ref[at : at + CHUNK, :]).astype(BF)
        eu_ref[:, at : at + CHUNK] = gh * slope_ref[:, at : at + CHUNK]
    return nt(eu_ref[...], up_ref[...])


def rows_of(block):
    slots, _, patches, width = block.shape
    return block[:, 0].astype(F32).reshape(slots * patches, width)


def block_of(rows, ref):
    slots, _, patches, width = ref.shape
    ref[:, 0] = rows.reshape(slots, patches, width).astype(ref.dtype)


def work_shapes(tokens):
    return [
        pltpu.VMEM((4, tokens, tokens), F32),
        pltpu.VMEM((2, tokens, CHUNK), BF),
        pltpu.VMEM((4, tokens, tokens), BF),
        pltpu.VMEM((HEADS, tokens, tokens), BF),
    ]


def wide(column):
    return jnp.broadcast_to(column, (column.shape[0], LANES))


def space_rows(x, weights, state, work):
    gain, w_in, w_out, scale, w_up, w_down = weights
    z0, inv0, qkv, p, o, z1, inv1, h, slope = state
    unit0, inverse0 = unit(x)
    z0[...] = unit0.astype(BF)
    inv0[...] = wide(inverse0)
    qkv[...] = nn((unit0 * gain[...]).astype(BF), w_in[...]).astype(BF)
    attend(qkv, p, o, None, work[0])
    r1 = x + nn(o[...], w_out[...])
    unit1, inverse1 = unit(r1)
    z1[...] = unit1.astype(BF)
    inv1[...] = wide(inverse1)
    m = (unit1 * scale[...]).astype(BF)
    return r1 + feed_up(m, w_up, w_down, h, slope, work[1])


def space_forward(labels, frames, *rest):
    weights, x2, state, work = rest[:6], rest[6], rest[7:16], rest[16:]
    rows = space_rows(frames[0, 0].astype(F32), weights, [ref.at[0] for ref in state], work)
    block_of(rows, x2)


def build_bias(labels, pack, slots, patches, bias):
    tokens = slots * patches
    row = lax.broadcasted_iota(jnp.int32, (1, tokens), 1)
    column = lax.broadcasted_iota(jnp.int32, (tokens, 1), 0)

    def label_of(position):
        slot = position // patches
        value = jnp.zeros_like(position)
        for f in range(slots):
            value = jnp.where(slot == f, labels[pack, f], value)
        return value

    same_patch = (row % patches) == (column % patches)
    allowed = same_patch & (column <= row) & (label_of(column) == label_of(row))
    bias[...] = jnp.where(allowed, 0.0, -1e30)


def time_both(labels, x2, grad, *rest):
    gain, w_in, w_out, scale, w_up, w_down = rest[:6]
    g0, out, z0, gqkv, o, e1, z1, eu, h, e2 = rest[6:16]
    qkv, p, slope, bias, *work = rest[16:]
    slots, _, patches, _ = x2.shape
    build_bias(labels, pack_at(labels, pl.program_id(0)), slots, patches, bias)
    x = rows_of(x2[...])
    unit0, inverse0 = unit(x)
    z0[0] = unit0.astype(BF)
    qkv[...] = nn((unit0 * gain[...]).astype(BF), w_in[...]).astype(BF)
    attend(qkv, p, o.at[0], bias, work[0])
    r1 = x + nn(o[0], w_out[...])
    unit1, inverse1 = unit(r1)
    z1[0] = unit1.astype(BF)
    m = (unit1 * scale[...]).astype(BF)
    block_of(r1 + feed_up(m, w_up, w_down, h.at[0], slope, work[1]), out)
    g2 = rows_of(grad[...])
    e2[0] = g2.astype(BF)
    gm = feed_back(e2[0], w_up, w_down, slope, eu.at[0])
    g1 = g2 + unit_backward(gm * scale[...], unit1, inverse1)
    e1[0] = g1.astype(BF)
    slope[:, : g1.shape[1]] = nt(e1[0], w_out[...]).astype(BF)
    attend_backward(qkv, p, slope, gqkv.at[0], work[2], work[3])
    gn = nt(gqkv[0], w_in[...])
    block_of(g1 + unit_backward(gn * gain[...], unit0, inverse0), g0)


def alone_both(labels, frames, grad, *rest):
    space, (gain, w_in, w_out, scale, w_up, w_down) = rest[:6], rest[6:12]
    input_grad, out = rest[12:14]
    sz0, so, se1, sgqkv, sz1, seu, sh, se2 = [ref.at[0] for ref in rest[14:22]]
    z0, o, e1, gv, z1, eu, h, e2 = [ref.at[0] for ref in rest[22:30]]
    inv0, inv1, qkv, p, sslope, slope, go, *work = rest[30:]
    state = sz0, inv0, qkv, p, so, sz1, inv1, sh, sslope
    x = space_rows(frames[0, 0].astype(F32), space, state, work)
    width = x.shape[1]
    unit0, inverse0 = unit(x)
    z0[...] = unit0.astype(BF)
    o[...] = nn((unit0 * gain[...]).astype(BF), w_in[:, 2 * width :]).astype(BF)
    r1 = x + nn(o[...], w_out[...])
    unit1, inverse1 = unit(r1)
    z1[...] = unit1.astype(BF)
    m = (unit1 * scale[...]).astype(BF)
    out[0, 0] = r1 + feed_up(m, w_up, w_down, h, slope, work[1])
    e2[...] = grad[0, 0]
    g2 = grad[0, 0].astype(F32)
    gm = feed_back(e2[...], w_up, w_down, slope, eu)
    g1 = g2 + unit_backward(gm * scale[...], unit1, inverse1)
    e1[...] = g1.astype(BF)
    gv[...] = nt(e1[...], w_out[...]).astype(BF)
    gn = nt(gv[...], w_in[:, 2 * width :])
    g2 = g1 + unit_backward(gn * gain[...], unit0, inverse0)
    gain, w_in, w_out, scale, w_up, w_down = space
    se2[...] = g2.astype(BF)
    gm = feed_back(se2[...], w_up, w_down, sslope, seu)
    g1 = g2 + unit_backward(gm * scale[...], sz1[...].astype(F32), inv1[:, :1])
    se1[...] = g1.astype(BF)
    go[...] = nt(se1[...], w_out[...]).astype(BF)
    attend_backward(qkv, p, go, sgqkv, work[2], work[3])
    gn = nt(sgqkv[...], w_in[...])
    input_grad[0, 0] = g1 + unit_backward(gn * gain[...], sz0[...].astype(F32), inv0[:, :1])


def space_back_in(labels, gqkv, w_in, gain, z0, inv0, g1, moved, *rest):
    input_grad, result = rest[-2:]
    gn = nt(gqkv[0], w_in[...])
    grad = unit_backward(gn * gain[...], z0[0].astype(F32), inv0[0, :, :1])
    input_grad[0, 0] = g1[0] + grad
    result[0, 0] = rows_of(moved[...])


class Copies:
    def __init__(self, semaphores):
        self.semaphores, self.count, self.sent = semaphores, 0, []

    def fetch(self, source, target):
        copy = pltpu.make_async_copy(source, target, self.semaphores.at[self.count])
        self.count += 1
        copy.start()
        return copy

    def send(self, source, target):
        self.sent.append(self.fetch(source, target))

    def finish(self):
        for copy in self.sent:
            copy.wait()


def wait(*copies):
    for copy in copies:
        copy.wait()


def space_feed_kernel(
    hierarchical, ids, scale, inv1, g2_in, slope_in, z1_in, w_out_in, w_up_in, w_down_in, h_in, z1_one, h_one, eu_one, e2_one, *rest
):
    outs, scratch = rest[: 5], rest[5:]
    e1_out, go_out, g1_out = outs[:3]
    g2, slope, z1, w_out, w_up, w_down, h, eu, e2, e1, go, g1 = scratch[:12]
    copies = Copies(scratch[-1])
    packs, tokens, _ = e1.shape
    have = packs * tokens
    got_g2 = copies.fetch(g2_in, g2)
    got_down = [
        copies.fetch(w_down_in.at[pl.ds(at, CHUNK)], w_down.at[pl.ds(at, CHUNK)])
        for at in range(0, w_down.shape[0], CHUNK)
    ]
    got_slope = [copies.fetch(slope_in.at[pack], slope.at[pack]) for pack in range(packs)]
    got_up = copies.fetch(w_up_in, w_up)
    got_z1 = [
        copies.fetch(z1_in.at[pack], z1.at[pl.ds(pack * tokens, tokens)]) for pack in range(packs)
    ]
    got_out = copies.fetch(w_out_in, w_out)
    if hierarchical:
        got_rest = [
            copies.fetch(z1_one.at[0], z1.at[pl.ds(have, tokens)]),
            copies.fetch(eu_one.at[0], eu.at[pl.ds(have, tokens)]),
            copies.fetch(e2_one.at[0], e2.at[pl.ds(have, tokens)]),
            copies.fetch(h_one.at[0], h.at[pl.ds(have, tokens)]),
        ] + [
            copies.fetch(h_in.at[pack], h.at[pl.ds(pack * tokens, tokens)]) for pack in range(packs)
        ]
    wait(got_g2)
    for pack in range(packs):
        rows = slice(pack * tokens, (pack + 1) * tokens)
        e2[rows] = rows_of(g2[:, pack : pack + 1]).astype(BF)
        wait(got_slope[pack])
        if pack == 0:
            wait(*got_down, got_up)
        gm = feed_back(e2[rows], w_up, w_down, slope.at[pack], eu.at[rows])
        if pack == 0:
            wait(*got_z1, got_out)
        grad = unit_backward(gm * scale[...], z1[rows].astype(F32), inv1[pack, :, :1])
        total = rows_of(g2[:, pack : pack + 1]) + grad
        g1[pack] = total
        e1[pack] = total.astype(BF)
        go[pack] = nt(e1[pack], w_out[...]).astype(BF)
        copies.send(g1.at[pack], g1_out.at[pack])
        copies.send(e1.at[pack], e1_out.at[pack])
        copies.send(go.at[pack], go_out.at[pack])
    if hierarchical:
        wait(*got_rest)
        feed_tiles(copies, ids, z1, e2, eu, h, 0, scratch[12:14], outs[3:])
    else:
        copies.send(eu, outs[3])
        copies.send(e2, outs[4])
    copies.finish()


def space_attend_kernel(
    hierarchical, ids, qkv_in, p_in, go_in, z0_in, o_in, e1_in, z0_one, o_one, e1_one, gqkv_one, *rest
):
    outs, scratch = rest[: 3 if hierarchical else 1], rest[3 if hierarchical else 1 :]
    qkv, p, go, z0, o, e1, gqkv, gp, gs = scratch[:9]
    copies = Copies(scratch[-1])
    packs, tokens, _ = qkv.shape
    have = packs * tokens
    got = [
        [
            copies.fetch(qkv_in.at[pack], qkv.at[pack]),
            copies.fetch(go_in.at[pack], go.at[pack]),
            copies.fetch(p_in.at[pack], p.at[pack]),
        ]
        for pack in range(packs)
    ]
    if hierarchical:
        pairs = (z0_in, z0_one, z0), (o_in, o_one, o), (e1_in, e1_one, e1)
        got_rest = [
            copies.fetch(source.at[pack], target.at[pl.ds(pack * tokens, tokens)])
            for source, _, target in pairs
            for pack in range(packs)
        ]
        got_rest += [copies.fetch(one.at[0], target.at[pl.ds(have, tokens)]) for _, one, target in pairs]
        got_rest.append(copies.fetch(gqkv_one.at[0], gqkv.at[pl.ds(have, tokens)]))
    for pack in range(packs):
        wait(*got[pack])
        rows = pl.ds(pack * tokens, tokens)
        attend_backward(qkv.at[pack], p.at[pack], go.at[pack], gqkv.at[rows], gp, gs)
        copies.send(gqkv.at[rows], outs[0].at[pack])
    if hierarchical:
        wait(*got_rest)
        attend_tiles(copies, ids, z0, o, gqkv, e1, 0, scratch[9:11], outs[1:], gqkv.shape[0])
    copies.finish()


def to_send(labels, grad, out):
    for place in range(out.shape[1]):
        rows = grad[pack_at(labels, place), 0].astype(F32)
        out[:, place] = rows.reshape(out.shape[0], out.shape[2], out.shape[3]).astype(BF)


def pack_at(labels, place):
    packs, slots = labels.shape
    alone = packs - 1
    for pack in range(packs - 2, -1, -1):
        alone = jnp.where(labels[pack, slots - 1] == slots - 1, pack, alone)
    return jnp.where(place == packs - 1, alone, place + (place >= alone).astype(jnp.int32))


def without(kernel, first, count):
    def call(*refs):
        return kernel(*refs[:first], *refs[first + count :])

    return call


class Packs:
    def __init__(self, labels, first, count):
        self.labels, self.first, self.count = labels, first, count

    def call(self, kernel, args, outs, scratch=(), flops=0, after=()):
        first, last = self.first, self.labels.shape[0] - 2
        scalars = (self.labels,)

        def spec(kind, shape):
            rank = len(shape)
            if kind == "whole":
                return pl.BlockSpec(shape, lambda i, *s: (0,) * rank)
            if kind == "pack":
                return pl.BlockSpec(
                    (1,) + tuple(shape[1:]), lambda i, s: (pack_at(s, first + i),) + (0,) * (rank - 1)
                )
            if kind == "place":
                return pl.BlockSpec(
                    (1,) + tuple(shape[1:]), lambda i, *s: (first + i,) + (0,) * (rank - 1)
                )
            if kind == "step":
                return pl.BlockSpec(
                    (1,) + tuple(shape[1:]), lambda i, *s: (i,) + (0,) * (rank - 1)
                )
            if kind == "moved":
                return pl.BlockSpec(
                    (shape[0], 1, shape[2], shape[3]),
                    lambda i, *s: (0, jnp.minimum(i, last), 0, 0),
                )
            return pl.BlockSpec(memory_space=pl.ANY)

        in_specs = [spec(kind, array.shape) for kind, array in args]
        operands = [array for _, array in args]
        aliases = {}
        for index, (kind, shape, dtype, into) in enumerate(outs):
            if into is not None:
                aliases[len(scalars) + len(operands)] = index
                operands.append(into)
                in_specs.append(pl.BlockSpec(memory_space=pl.ANY))
        for array in after:
            operands.append(array)
            in_specs.append(pl.BlockSpec(memory_space=pl.ANY))
        moved = sum(a.size * a.dtype.itemsize for a in operands)
        unread = len(operands) - len(args)
        return pl.pallas_call(
            without(kernel, len(scalars) + len(args), unread),
            out_shape=[jax.ShapeDtypeStruct(shape, dtype) for _, shape, dtype, _ in outs],
            grid_spec=pltpu.PrefetchScalarGridSpec(
                num_scalar_prefetch=len(scalars),
                grid=(self.count,),
                in_specs=in_specs,
                out_specs=[spec(kind, shape) for kind, shape, _, _ in outs],
                scratch_shapes=list(scratch),
            ),
            input_output_aliases=aliases,
            compiler_params=pltpu.CompilerParams(
                vmem_limit_bytes=VMEM, dimension_semantics=("arbitrary",)
            ),
            cost_estimate=pl.CostEstimate(
                flops=int(flops * self.count), bytes_accessed=int(moved), transcendentals=0
            ),
        )(*scalars, *operands)


def feed_tiles(copies, ids, z1, e2, eu, h, at, held, outs):
    first = ids[0] == 0
    for step in range(4):
        tile = tn(z1[...], eu[:, step * CHUNK : (step + 1) * CHUNK]).astype(BF)
        s = step ^ ids[2]
        for z in range(4):
            even, odd = tile[128 * z : 128 * z + 64], tile[128 * z + 64 : 128 * z + 128]
            held[0][s, z ^ ids[1], at : at + 64] = jnp.where(first, even, odd)
            held[1][s, z ^ ids[1], at : at + 64] = jnp.where(first, odd, even)
        for ref, out in zip(held, outs):
            copies.send(ref.at[s, :, pl.ds(at, 64)], out.at[s, :, pl.ds(at, 64)])
    at = at + 64
    for step in range(4):
        tile = tn(e2[...], h[:, step * CHUNK : (step + 1) * CHUNK]).astype(BF)
        z = step ^ ids[1]
        for s in range(4):
            upper, lower = tile[128 * s : 128 * s + 64], tile[128 * s + 64 : 128 * s + 128]
            even = jnp.concatenate([upper[:, :256], lower[:, :256]], axis=1)
            odd = jnp.concatenate([upper[:, 256:], lower[:, 256:]], axis=1)
            held[0][s ^ ids[2], z, at : at + 64] = jnp.where(first, even, odd)
            held[1][s ^ ids[2], z, at : at + 64] = jnp.where(first, odd, even)
        for ref, out in zip(held, outs):
            copies.send(ref.at[:, z, pl.ds(at, 64)], out.at[:, z, pl.ds(at, 64)])


def attend_tiles(copies, ids, z0, o, gqkv, e1, at, held, outs, depth):
    first = ids[0] == 0
    for step in range(4):
        if step == 3:
            tile = tn(o[...], e1[...])
        else:
            rows = gqkv.shape[0] if step == 2 else depth
            tile = tn(z0[:rows], gqkv[:rows, step * CHUNK : (step + 1) * CHUNK])
        tile = tile.astype(BF)
        here = at + 16 * step
        for z in range(4):
            for s in range(4):
                row = 128 * z + 16 * s
                even, odd = tile[row : row + 16], tile[row + 64 : row + 80]
                held[0][s ^ ids[2], z ^ ids[1], here : here + 16] = jnp.where(first, even, odd)
                held[1][s ^ ids[2], z ^ ids[1], here : here + 16] = jnp.where(first, odd, even)
    for ref, out in zip(held, outs):
        copies.send(ref.at[:, :, pl.ds(at, 64)], out.at[:, :, pl.ds(at, 64)])


def time_weights_kernel(ids, *rest):
    names = 8
    shared, one, outs, scratch = rest[:names], rest[names : 2 * names], rest[16:18], rest[18:]
    z1, eu, e2, h, z0, gqkv, o, e1 = scratch[:names]
    held, copies = scratch[8:10], Copies(scratch[-1])
    packs, tokens, _ = shared[0].shape
    have = packs * tokens
    got = []
    for source, single, target in zip(shared, one, scratch):
        wide_target = target.at[pl.ds(have, tokens)]
        if single.shape[2] < target.shape[1]:
            wide_target = target.at[pl.ds(have, tokens), pl.ds(target.shape[1] - single.shape[2], single.shape[2])]
        got.append(
            [copies.fetch(source.at[pack], target.at[pl.ds(pack * tokens, tokens)]) for pack in range(packs)]
            + [copies.fetch(single.at[0], wide_target)]
        )
    wait(*got[0], *got[1], *got[2], *got[3])
    feed_tiles(copies, ids, z1, e2, eu, h, 0, held, outs)
    wait(*got[4], *got[5], *got[6], *got[7])
    attend_tiles(copies, ids, z0, o, gqkv, e1, 128, held, outs, have)
    copies.finish()


def manual_call(kernel, ids, args, outs, scratch, semaphores, small=0, after=(), flops=0):
    anywhere = pl.BlockSpec(memory_space=pl.ANY)
    return pl.pallas_call(
        without(kernel, 1 + len(args), len(after)),
        out_shape=[jax.ShapeDtypeStruct(shape, dtype) for shape, dtype in outs],
        in_specs=[pl.BlockSpec(memory_space=pltpu.SMEM)]
        + [pl.BlockSpec(memory_space=pltpu.VMEM)] * small
        + [anywhere] * (len(args) - small + len(after)),
        out_specs=[anywhere] * len(outs),
        scratch_shapes=[pltpu.VMEM(shape, dtype) for shape, dtype in scratch]
        + [pltpu.SemaphoreType.DMA((semaphores,))],
        compiler_params=pltpu.CompilerParams(vmem_limit_bytes=VMEM),
        cost_estimate=pl.CostEstimate(
            flops=int(flops), bytes_accessed=sum(a.size * 2 for a in args), transcendentals=0
        ),
    )(ids, *args, *after)


def swap(array, axis, size, mask):
    return lax.ppermute(array, axis, [(i, i ^ mask) for i in range(size)])


def add(*terms):
    total = terms[0].astype(F32)
    for term in terms[1:]:
        total = total + term.astype(F32)
    return total.astype(BF)


def core_sum(mine, other):
    got = swap(other, "tm", 8, 1)
    return [add(mine[d], got[d]) for d in range(1, 4)], (mine[0], got[0])


def rest_sum(parts, own):
    got = [swap(part, "stream", 4, d + 1) for d, part in enumerate(parts)]
    rows = [add(*[term[d] for term in (*own, *got)]) for d in range(4)]
    got = [swap(rows[d], "tm", 8, 2 * d) for d in range(1, 4)]
    final = add(rows[0], *got)
    return [final] + [swap(final, "stream", 4, d) for d in range(1, 4)]


def column(row):
    size = row.shape[1]
    eye = lax.broadcasted_iota(jnp.int32, (size, size), 0) == lax.broadcasted_iota(
        jnp.int32, (size, size), 1
    )
    return jnp.sum(jnp.where(eye, row, 0.0), axis=1, keepdims=True)


def as_row(col):
    size = col.shape[0]
    eye = lax.broadcasted_iota(jnp.int32, (size, size), 0) == lax.broadcasted_iota(
        jnp.int32, (size, size), 1
    )
    return jnp.sum(jnp.where(eye, col, 0.0), axis=0, keepdims=True)


def own_rows(ids, vector):
    rank = 2 * ids[1] + ids[0]
    return column(vector[pl.ds(rank, 1), :])


def finish_feed(ids, pieces, at, w_up, scale, scale_grad, up_grad, down_grad):
    factor = own_rows(ids, scale)
    for d, piece in enumerate(pieces):
        s = ids[2] ^ d
        up_grad[:, pl.ds(pl.multiple_of(512 * s, 512), 512)] = piece[at : at + 64].astype(F32)
        lower = piece[at + 64 : at + 128].astype(F32)
        whole = jnp.concatenate([lower[:, :256], lower[:, 256:]], axis=0)
        down_grad[:, pl.ds(pl.multiple_of(128 * s, 128), 128)] = whole.T
    total = up_grad[...]
    scale_grad[...] = as_row(jnp.sum(total * w_up[...].astype(F32), axis=1, keepdims=True))
    up_grad[...] = total * factor


def finish_attend(ids, pieces, at, w_in, gain, gain_grad, in_grad, out_grad):
    factor = own_rows(ids, gain)
    for d, piece in enumerate(pieces):
        rows = pl.ds(pl.multiple_of(16 * (ids[2] ^ d), 16), 16)
        for third in range(3):
            in_grad[rows, 512 * third : 512 * third + 512] = piece[
                at + 16 * third : at + 16 * third + 16
            ].astype(F32)
        out_grad[rows, :] = piece[at + 48 : at + 64].astype(F32)
    total = in_grad[...]
    gain_grad[...] = as_row(jnp.sum(total * w_in[...].astype(F32), axis=1, keepdims=True))
    in_grad[...] = total * factor


def finish_feed_kernel(ids, p0, p1, p2, p3, w_up, scale, *outs):
    finish_feed(ids, (p0, p1, p2, p3), 0, w_up, scale, *outs)


def finish_attend_kernel(ids, p0, p1, p2, p3, w_in, gain, *outs):
    finish_attend(ids, (p0, p1, p2, p3), 0, w_in, gain, *outs)


def finish_all_kernel(ids, p0, p1, p2, p3, w_up, scale, w_in, gain, *outs):
    finish_feed(ids, (p0, p1, p2, p3), 0, w_up, scale, *outs[:3])
    finish_attend(ids, (p0, p1, p2, p3), 128, w_in, gain, *outs[3:])


def finish_call(kernel, ids, pieces, pairs, outs):
    whole = pl.BlockSpec(pieces[0].shape, lambda i, *s: (0, 0))
    specs, operands = [], []
    for weight, vector in pairs:
        height = weight.shape[0] // 8
        specs += [
            pl.BlockSpec((height, weight.shape[1]), lambda i, s: (2 * s[1] + s[0], 0)),
            pl.BlockSpec((8, height), lambda i, *s: (0, 0)),
        ]
        operands += [weight, vector.reshape(8, height)]
    results = pl.pallas_call(
        kernel,
        out_shape=[jax.ShapeDtypeStruct(shape, F32) for shape in outs],
        grid_spec=pltpu.PrefetchScalarGridSpec(
            num_scalar_prefetch=1,
            grid=(1,),
            in_specs=[whole] * 4 + specs,
            out_specs=[pl.BlockSpec(shape, lambda i, *s: (0, 0)) for shape in outs],
        ),
        compiler_params=pltpu.CompilerParams(vmem_limit_bytes=VMEM),
    )(ids, *pieces, *operands)
    return [a.reshape(-1) if a.shape[0] == 1 else a for a in results]


def plain_grads(z, grads, left, right, weight, vector):
    product = tn(z, grads)
    vector_grad = jnp.sum(product * weight.astype(F32), axis=1)
    sums = []
    for term in (vector_grad, product * vector[:, None], tn(left, right)):
        share = lax.psum_scatter(term.astype(BF), "tm", scatter_dimension=0, tiled=True)
        sums.append(lax.psum(share, "stream").astype(F32))
    return sums


def everyone_once(labels, grad, moved):
    _, shape, dtype, _ = moved
    return pl.pallas_call(
        to_send,
        out_shape=[jax.ShapeDtypeStruct(shape, dtype)],
        grid_spec=pltpu.PrefetchScalarGridSpec(
            num_scalar_prefetch=1,
            grid=(1,),
            in_specs=[pl.BlockSpec(grad.shape, lambda i, s: (0, 0, 0, 0))],
            out_specs=[pl.BlockSpec(shape, lambda i, s: (0, 0, 0, 0))],
        ),
        compiler_params=pltpu.CompilerParams(vmem_limit_bytes=VMEM),
    )(labels, grad)


def per_device(
    ranks,
    streams,
    frames,
    space_gain,
    space_input,
    space_output,
    space_scale,
    space_up,
    space_down,
    time_gain,
    time_input,
    time_output,
    time_scale,
    time_up,
    time_down,
    clip_labels,
    output_grad,
):
    packs, _, tokens, width = frames.shape
    slots = clip_labels.shape[1]
    patches = tokens // ranks
    hidden = space_up.shape[1]
    some = packs - 1
    hierarchical = (ranks, streams) == (8, 4)
    tm = lax.axis_index("tm")
    ids = jnp.stack([tm % 2, tm // 2, lax.axis_index("stream")]).astype(jnp.int32)
    shared = Packs(clip_labels, 0, some)
    single = Packs(clip_labels, some, 1)

    def row(vector):
        return vector.reshape(1, -1)

    def exchange(array):
        return lax.all_to_all(array, "tm", split_axis=0, concat_axis=0, tiled=True)

    def steps(count, *tails):
        return [("step", (count,) + tail, BF, None) for tail in tails]

    moved = ("moved", (slots, some, patches, width), BF, None)
    whole = ("pack", frames.shape, F32, None)
    flops = 2 * tokens * width * (4 * width + 2 * hidden)

    (sent,) = everyone_once(clip_labels, output_grad, moved)
    grad_moved = exchange(sent)

    space_args = [
        ("whole", row(space_gain)),
        ("whole", space_input),
        ("whole", space_output),
        ("whole", row(space_scale)),
        ("whole", space_up),
        ("whole", space_down),
    ]
    time_args = [
        ("whole", row(time_gain)),
        ("whole", time_input),
        ("whole", time_output),
        ("whole", row(time_scale)),
        ("whole", time_up),
        ("whole", time_down),
    ]
    rows_w, rows_3, rows_h = (tokens, width), (tokens, 3 * width), (tokens, hidden)
    spread = ("step", (some, tokens, LANES), F32, None)
    x2, sz0, sinv0, sqkv, sp, so, sz1, sinv1, sh, sslope = shared.call(
        space_forward,
        [("pack", frames)] + space_args,
        [moved]
        + steps(some, rows_w)
        + [spread]
        + steps(some, rows_3, (HEADS, tokens, tokens), rows_w, rows_w)
        + [spread]
        + steps(some, rows_h, rows_h),
        scratch=work_shapes(tokens),
        flops=flops,
        after=(sent,),
    )
    x2, grad_moved = lax.optimization_barrier((x2, grad_moved))
    x2_moved = exchange(x2)

    block_tails = [rows_w, rows_w, rows_w, rows_3, rows_w, rows_h, rows_h, rows_w]
    time_tails = [rows_w, rows_w, rows_w, rows_w, rows_w, rows_h, rows_h, rows_w]
    input_grad, result, *alone = single.call(
        alone_both,
        [("pack", frames), ("pack", output_grad)] + space_args + time_args,
        [whole, whole] + steps(1, *block_tails) + steps(1, *time_tails),
        scratch=[
            pltpu.VMEM((tokens, LANES), F32),
            pltpu.VMEM((tokens, LANES), F32),
            pltpu.VMEM(rows_3, BF),
            pltpu.VMEM((HEADS, tokens, tokens), BF),
            pltpu.VMEM(rows_h, BF),
            pltpu.VMEM(rows_h, BF),
            pltpu.VMEM(rows_w, BF),
        ]
        + work_shapes(tokens),
        flops=6 * flops,
        after=(x2,),
    )
    sz0_one, so_one, se1_one, sgqkv_one, sz1_one, seu_one, sh_one, se2_one = alone[:8]
    tz0_one, to_one, te1_one, tgv_one, tz1_one, teu_one, th_one, te2_one = alone[8:]

    g0, out, tz0, tgqkv, to, te1, tz1, teu, th, te2 = shared.call(
        time_both,
        [("moved", x2_moved), ("moved", grad_moved)] + time_args,
        [moved, moved] + steps(some, rows_w, rows_3, rows_w, rows_w, rows_w, rows_h, rows_h, rows_w),
        scratch=[
            pltpu.VMEM(rows_3, BF),
            pltpu.VMEM((HEADS, tokens, tokens), BF),
            pltpu.VMEM(rows_h, BF),
            pltpu.VMEM((tokens, tokens), F32),
        ]
        + work_shapes(tokens),
        flops=3 * flops,
        after=(sz0_one,),
    )
    g0_moved = exchange(g0)
    out, g0_moved = lax.optimization_barrier((out, g0_moved))
    out_moved = exchange(out)

    everything = packs * tokens
    feed_shapes = [(1, width // 8), (width // 8, hidden), (hidden // 8, width)]
    attend_shapes = [(1, width // 8), (width // 8, 3 * width), (width // 8, width)]
    time_shared = [tz1, teu, te2, th, tz0, tgqkv, to, te1]
    time_one = [tz1_one, teu_one, te2_one, th_one, tz0_one, tgv_one, to_one, te1_one]
    time_parts = ()
    if hierarchical:
        parts_shape = ((4, 4, 192, CHUNK), BF)
        mine, other = manual_call(
            time_weights_kernel,
            ids,
            time_shared + time_one,
            [parts_shape] * 2,
            [((everything, a.shape[2]), BF) for a in time_shared] + [parts_shape] * 2,
            8 * packs + 18,
            flops=packs * flops,
        )
        time_parts, own = core_sum(mine, other)
        time_grads = finish_call(
            finish_all_kernel,
            ids,
            rest_sum(time_parts, own),
            [(time_up, time_scale), (time_input, time_gain)],
            feed_shapes + attend_shapes,
        )
    else:
        grad_one = jnp.pad(tgv_one, ((0, 0), (0, 0), (2 * width, 0)))
        joined = [joint(a, b) for a, b in zip(time_shared, time_one[:5] + [grad_one] + time_one[6:])]
        time_grads = plain_grads(joined[0], joined[1], joined[3], joined[2], time_up, time_scale)
        time_grads += plain_grads(joined[4], joined[5], joined[6], joined[7], time_input, time_gain)

    shared_w, shared_h = (some,) + rows_w, (some,) + rows_h
    feed_args = [row(space_scale), sinv1, g0_moved, sslope, sz1, space_output, space_up, space_down]
    feed_args += [sh, sz1_one, sh_one, seu_one, se2_one]
    parts_shape = ((4, 4, 128, CHUNK), BF)
    state_shapes = [((everything, hidden), BF), ((everything, width), BF)]
    se1, sgo, sg1, *weights = manual_call(
        functools.partial(space_feed_kernel, hierarchical),
        ids,
        feed_args,
        [(shared_w, BF), (shared_w, BF), (shared_w, F32)]
        + ([parts_shape] * 2 if hierarchical else state_shapes),
        [
            (g0_moved.shape, BF),
            (shared_h, BF),
            ((everything, width), BF),
            (space_output.shape, BF),
            (space_up.shape, BF),
            (space_down.shape, BF),
            ((everything, hidden), BF),
            *state_shapes,
            (shared_w, BF),
            (shared_w, BF),
            (shared_w, F32),
        ]
        + ([parts_shape] * 2 if hierarchical else []),
        64,
        small=2,
        after=time_parts,
        flops=packs * flops,
    )
    parts = ()
    if hierarchical:
        parts, own = core_sum(*weights)
        feed_grads = finish_call(
            finish_feed_kernel, ids, rest_sum(parts, own), [(space_up, space_scale)], feed_shapes
        )
    else:
        have = some * tokens
        seu, se2 = [a[:have].reshape(some, tokens, -1) for a in weights]
        feed_grads = plain_grads(
            joint(sz1, sz1_one),
            joint(seu, seu_one),
            joint(sh, sh_one),
            joint(se2, se2_one),
            space_up,
            space_scale,
        )
    parts_shape = ((4, 4, 64, CHUNK), BF)
    sgqkv, *weights = manual_call(
        functools.partial(space_attend_kernel, hierarchical),
        ids,
        [sqkv, sp, sgo, sz0, so, se1, sz0_one, so_one, se1_one, sgqkv_one],
        [((some,) + rows_3, BF)] + ([parts_shape] * 2 if hierarchical else []),
        [
            ((some,) + rows_3, BF),
            (sp.shape, BF),
            (shared_w, BF),
            ((everything, width), BF),
            ((everything, width), BF),
            ((everything, width), BF),
            ((everything, 3 * width), BF),
            ((4, tokens, tokens), BF),
            ((HEADS, tokens, tokens), BF),
        ]
        + ([parts_shape] * 2 if hierarchical else []),
        64,
        after=parts,
        flops=packs * flops,
    )
    if hierarchical:
        attend_grads = finish_call(
            finish_attend_kernel,
            ids,
            rest_sum(*core_sum(*weights)),
            [(space_input, space_gain)],
            attend_shapes,
        )
    else:
        attend_grads = plain_grads(
            joint(sz0, sz0_one),
            joint(sgqkv, sgqkv_one),
            joint(so, so_one),
            joint(se1, se1_one),
            space_input,
            space_gain,
        )
    input_grad, result = shared.call(
        space_back_in,
        [
            ("step", sgqkv),
            ("whole", space_input),
            ("whole", row(space_gain)),
            ("step", sz0),
            ("step", sinv0),
            ("step", sg1),
            ("moved", out_moved),
        ],
        [("pack", frames.shape, F32, input_grad), ("pack", frames.shape, F32, result)],
        flops=flops // 4,
    )
    grads = attend_grads + feed_grads + time_grads[3:] + time_grads[:3]
    return (result, input_grad, *grads)


def joint(shared, one):
    return jnp.concatenate([shared, one]).reshape(-1, shared.shape[-1])


def solution(mesh):
    tokens = P("stream", "tm", None, None)
    vector, matrix = P("tm"), P("tm", None)
    return jax.shard_map(
        functools.partial(per_device, mesh.shape["tm"], mesh.shape["stream"]),
        mesh=mesh,
        in_specs=(tokens,) + (P(),) * 12 + (P("stream", None), tokens),
        out_specs=(tokens, tokens) + (vector, matrix, matrix, vector, matrix, matrix) * 2,
        check_vma=False,
    )
```

```python
import functools

import jax
import jax.numpy as jnp
from jax import lax
from jax.experimental import pallas as pl
from jax.experimental.pallas import tpu as pltpu
from jax.sharding import PartitionSpec as P

HEADS = 8
EPS = 1e-05
GELU_A = 0.7978845608028654
GELU_B = 0.044715
BF = jnp.bfloat16
F32 = jnp.float32
CHUNK = 512
LANES = 128
COST = 1
VMEM = 60 * 1024 * 1024
SMALL_VMEM = 24 * 1024 * 1024


def nn(a, b):
    return jnp.dot(a, b, preferred_element_type=F32)


def nt(a, b):
    return lax.dot_general(a, b, (((1,), (1,)), ((), ())), preferred_element_type=F32)


def tn(a, b):
    return lax.dot_general(a, b, (((0,), (0,)), ((), ())), preferred_element_type=F32)


def unit(values):
    average = jnp.mean(values, axis=-1, keepdims=True)
    centered = values - average
    inverse = lax.rsqrt(jnp.mean(centered * centered, axis=-1, keepdims=True) + EPS)
    return centered * inverse, inverse


def unit_backward(grad, unit_rows, inverse):
    first = jnp.mean(grad, axis=-1, keepdims=True)
    second = jnp.mean(grad * unit_rows, axis=-1, keepdims=True)
    return inverse * (grad - first - unit_rows * second)


def gelu_parts(u):
    square = u * u
    tangent = jnp.tanh(u * (BF(GELU_A) + BF(GELU_A * GELU_B) * square))
    half = BF(0.5) * u
    value = half + half * tangent
    slope = (BF(0.5) + BF(0.5) * tangent) + half * (BF(1.0) - tangent * tangent) * (
        BF(GELU_A) + BF(3.0 * GELU_A * GELU_B) * square
    )
    return value, slope


def head_masks(width):
    lane = lax.broadcasted_iota(jnp.int32, (1, 2 * width), 1)
    low = lane < width
    return low, (low.astype(F32).astype(BF), (1.0 - low.astype(F32)).astype(BF))


def attend(qkv_ref, p_ref, o_ref, bias_ref, s_ref):
    width = qkv_ref.shape[1] // 3
    size = width // HEADS
    _, masks = head_masks(size)

    def lanes(part, head):
        at = part * width + (head // 2) * 2 * size
        return qkv_ref[:, at : at + 2 * size]

    def score(head):
        s_ref[head % 4] = nt(lanes(1, head) * masks[head % 2], lanes(0, head) * BF(size**-0.5))

    def soften(head):
        scores = s_ref[head % 4]
        if bias_ref is not None:
            scores = scores + bias_ref[...]
        e = jnp.exp(scores - jnp.max(scores, axis=0, keepdims=True))
        p_ref[head] = (e * (1.0 / jnp.sum(e, axis=0, keepdims=True))).astype(BF)

    for head in range(0, HEADS, 2):
        if head == 0:
            score(0)
            score(1)
        if head + 2 < HEADS:
            score(head + 2)
            score(head + 3)
        soften(head)
        soften(head + 1)
    for head in range(0, HEADS, 2):
        v = lanes(2, head).T
        both = jnp.concatenate([nn(v[:size], p_ref[head]), nn(v[size:], p_ref[head + 1])], axis=0)
        o_ref[:, head * size : (head + 2) * size] = both.T.astype(BF)


def attend_backward(qkv_ref, p_ref, go_ref, out_ref, gp_ref, gs_ref):
    width = qkv_ref.shape[1] // 3
    size = width // HEADS
    _, masks = head_masks(size)

    def lanes(part, head):
        at = part * width + (head // 2) * 2 * size
        return qkv_ref[:, at : at + 2 * size]

    def gos(head):
        return go_ref[:, (head // 2) * 2 * size : (head // 2 + 1) * 2 * size]

    def put(part, head, value):
        at = part * width + head * size
        out_ref[:, at : at + 2 * size] = value.astype(BF)

    def start(head):
        for h in (head, head + 1):
            gp_ref[h % 4] = nt(lanes(2, h) * masks[h % 2], gos(h)).astype(BF)
        g = gos(head)
        put(2, head, nn(p_ref[head], g * masks[0]) + nn(p_ref[head + 1], g * masks[1]))

    def middle(head):
        p = p_ref[head]
        weighted = p * gp_ref[head % 4]
        total = jnp.sum(weighted.astype(F32), axis=0, keepdims=True).astype(BF)
        gs_ref[head] = weighted - p * total

    def finish(head):
        q = lanes(0, head) * BF(size**-0.5)
        k = (lanes(1, head) * BF(size**-0.5)).T
        put(1, head, nn(gs_ref[head], q * masks[0]) + nn(gs_ref[head + 1], q * masks[1]))
        both = jnp.concatenate([nn(k[:size], gs_ref[head]), nn(k[size:], gs_ref[head + 1])], axis=0)
        put(0, head, both.T)

    start(0)
    for head in range(0, HEADS, 2):
        middle(head)
        middle(head + 1)
        if head + 2 < HEADS:
            start(head + 2)
        if head > 0:
            finish(head - 2)
    finish(HEADS - 2)


def feed_up(m, up_ref, down_ref, h_ref, slope_ref, u_ref):
    steps = up_ref.shape[1] // CHUNK

    def before(step):
        u_ref[step % 2] = nn(m, up_ref[:, step * CHUNK : (step + 1) * CHUNK]).astype(BF)

    before(0)
    for step in range(steps):
        if step + 1 < steps:
            before(step + 1)
        at = step * CHUNK
        h_ref[:, at : at + CHUNK], slope_ref[:, at : at + CHUNK] = gelu_parts(u_ref[step % 2])
    return nn(h_ref[...], down_ref[...])


def feed_back(e2, up_ref, down_ref, slope_ref, eu_ref):
    for at in range(0, up_ref.shape[1], CHUNK):
        gh = nt(e2, down_ref[at : at + CHUNK, :]).astype(BF)
        eu_ref[:, at : at + CHUNK] = gh * slope_ref[:, at : at + CHUNK]
    return nt(eu_ref[...], up_ref[...])


def rows_of(block):
    slots, _, patches, width = block.shape
    return block[:, 0].astype(F32).reshape(slots * patches, width)


def block_of(rows, ref):
    slots, _, patches, width = ref.shape
    ref[:, 0] = rows.reshape(slots, patches, width).astype(ref.dtype)


def work_shapes(tokens):
    return [
        pltpu.VMEM((4, tokens, tokens), F32),
        pltpu.VMEM((2, tokens, CHUNK), BF),
        pltpu.VMEM((4, tokens, tokens), BF),
        pltpu.VMEM((HEADS, tokens, tokens), BF),
    ]


def wide(column):
    return jnp.broadcast_to(column, (column.shape[0], LANES))


def space_rows(x, weights, state, work):
    gain, w_in, w_out, scale, w_up, w_down = weights
    z0, inv0, qkv, p, o, z1, inv1, h, slope = state
    unit0, inverse0 = unit(x)
    z0[...] = unit0.astype(BF)
    inv0[...] = wide(inverse0)
    qkv[...] = nn((unit0 * gain[...]).astype(BF), w_in[...]).astype(BF)
    attend(qkv, p, o, None, work[0])
    r1 = x + nn(o[...], w_out[...])
    unit1, inverse1 = unit(r1)
    z1[...] = unit1.astype(BF)
    inv1[...] = wide(inverse1)
    m = (unit1 * scale[...]).astype(BF)
    return r1 + feed_up(m, w_up, w_down, h, slope, work[1])


def space_forward(labels, frames, *rest):
    weights, x2, state, work = rest[:6], rest[6], rest[7:16], rest[16:]
    rows = space_rows(frames[0, 0].astype(F32), weights, [ref.at[0] for ref in state], work)
    block_of(rows, x2)


def build_bias(labels, pack, slots, patches, bias):
    tokens = slots * patches
    row = lax.broadcasted_iota(jnp.int32, (1, tokens), 1)
    column = lax.broadcasted_iota(jnp.int32, (tokens, 1), 0)

    def label_of(position):
        slot = position // patches
        value = jnp.zeros_like(position)
        for f in range(slots):
            value = jnp.where(slot == f, labels[pack, f], value)
        return value

    same_patch = (row % patches) == (column % patches)
    allowed = same_patch & (column <= row) & (label_of(column) == label_of(row))
    bias[...] = jnp.where(allowed, 0.0, -1e30)


def time_both(labels, x2, grad, *rest):
    gain, w_in, w_out, scale, w_up, w_down = rest[:6]
    g0, out, z0, gqkv, o, e1, z1, eu, h, e2 = rest[6:16]
    qkv, p, slope, bias, *work = rest[16:]
    slots, _, patches, _ = x2.shape
    build_bias(labels, pack_at(labels, pl.program_id(0)), slots, patches, bias)
    x = rows_of(x2[...])
    unit0, inverse0 = unit(x)
    z0[0] = unit0.astype(BF)
    qkv[...] = nn((unit0 * gain[...]).astype(BF), w_in[...]).astype(BF)
    attend(qkv, p, o.at[0], bias, work[0])
    r1 = x + nn(o[0], w_out[...])
    unit1, inverse1 = unit(r1)
    z1[0] = unit1.astype(BF)
    m = (unit1 * scale[...]).astype(BF)
    block_of(r1 + feed_up(m, w_up, w_down, h.at[0], slope, work[1]), out)
    g2 = rows_of(grad[...])
    e2[0] = g2.astype(BF)
    gm = feed_back(e2[0], w_up, w_down, slope, eu.at[0])
    g1 = g2 + unit_backward(gm * scale[...], unit1, inverse1)
    e1[0] = g1.astype(BF)
    slope[:, : g1.shape[1]] = nt(e1[0], w_out[...]).astype(BF)
    attend_backward(qkv, p, slope, gqkv.at[0], work[2], work[3])
    gn = nt(gqkv[0], w_in[...])
    block_of(g1 + unit_backward(gn * gain[...], unit0, inverse0), g0)


def alone_both(labels, frames, grad, *rest):
    space, (gain, w_in, w_out, scale, w_up, w_down) = rest[:6], rest[6:12]
    input_grad, out = rest[12:14]
    sz0, so, se1, sgqkv, sz1, seu, sh, se2 = [ref.at[0] for ref in rest[14:22]]
    z0, o, e1, gv, z1, eu, h, e2 = [ref.at[0] for ref in rest[22:30]]
    inv0, inv1, qkv, p, sslope, slope, go, *work = rest[30:]
    state = sz0, inv0, qkv, p, so, sz1, inv1, sh, sslope
    x = space_rows(frames[0, 0].astype(F32), space, state, work)
    width = x.shape[1]
    unit0, inverse0 = unit(x)
    z0[...] = unit0.astype(BF)
    o[...] = nn((unit0 * gain[...]).astype(BF), w_in[:, 2 * width :]).astype(BF)
    r1 = x + nn(o[...], w_out[...])
    unit1, inverse1 = unit(r1)
    z1[...] = unit1.astype(BF)
    m = (unit1 * scale[...]).astype(BF)
    out[0, 0] = r1 + feed_up(m, w_up, w_down, h, slope, work[1])
    e2[...] = grad[0, 0]
    g2 = grad[0, 0].astype(F32)
    gm = feed_back(e2[...], w_up, w_down, slope, eu)
    g1 = g2 + unit_backward(gm * scale[...], unit1, inverse1)
    e1[...] = g1.astype(BF)
    gv[...] = nt(e1[...], w_out[...]).astype(BF)
    gn = nt(gv[...], w_in[:, 2 * width :])
    g2 = g1 + unit_backward(gn * gain[...], unit0, inverse0)
    gain, w_in, w_out, scale, w_up, w_down = space
    se2[...] = g2.astype(BF)
    gm = feed_back(se2[...], w_up, w_down, sslope, seu)
    g1 = g2 + unit_backward(gm * scale[...], sz1[...].astype(F32), inv1[:, :1])
    se1[...] = g1.astype(BF)
    go[...] = nt(se1[...], w_out[...]).astype(BF)
    attend_backward(qkv, p, go, sgqkv, work[2], work[3])
    gn = nt(sgqkv[...], w_in[...])
    input_grad[0, 0] = g1 + unit_backward(gn * gain[...], sz0[...].astype(F32), inv0[:, :1])


def space_back_in(labels, gqkv, w_in, gain, z0, inv0, g1, moved, input_grad, result):
    gn = nt(gqkv[0], w_in[...])
    grad = unit_backward(gn * gain[...], z0[0].astype(F32), inv0[0, :, :1])
    input_grad[0, 0] = g1[0] + grad
    result[0, 0] = rows_of(moved[...])


class Copies:
    def __init__(self, semaphores):
        self.semaphores, self.count, self.sent = semaphores, 0, []

    def fetch(self, source, target):
        copy = pltpu.make_async_copy(source, target, self.semaphores.at[self.count])
        self.count += 1
        copy.start()
        return copy

    def send(self, source, target):
        self.sent.append(self.fetch(source, target))

    def finish(self):
        for copy in self.sent:
            copy.wait()


def wait(*copies):
    for copy in copies:
        copy.wait()


def space_kernel(hierarchical, ids, scale, inv1, *rest):
    (g2_in, slope_in, z1_in, w_out_in, w_up_in, w_down_in, qkv_in, p_in), rest = rest[:8], rest[8:]
    shared, one, rest = rest[:3], rest[3:11], rest[11:]
    (g1_out, gqkv_out), outs, scratch = rest[:2], rest[2 : 6 if hierarchical else 5], rest[6 if hierarchical else 5 :]
    g2, slope, w_out, w_up, w_down, qkv, p, go, g1, gp, gs = scratch[:11]
    z1, eu, h, e2, z0, gqkv, o, e1 = whole = scratch[11:19]
    copies = Copies(scratch[-1])
    packs, tokens, _ = g1.shape
    have = packs * tokens
    got_g2 = copies.fetch(g2_in, g2)
    got_down = copies.fetch(w_down_in, w_down)
    got_slope = [copies.fetch(slope_in.at[pack], slope.at[pack]) for pack in range(packs)]
    got_up = copies.fetch(w_up_in, w_up)
    got_z1 = [
        copies.fetch(z1_in.at[pack], z1.at[pl.ds(pack * tokens, tokens)]) for pack in range(packs)
    ]
    got_out = copies.fetch(w_out_in, w_out)
    got_attend = [
        (copies.fetch(qkv_in.at[pack], qkv.at[pack]), copies.fetch(p_in.at[pack], p.at[pack]))
        for pack in range(packs)
    ]
    got_rest = []
    if hierarchical:
        for source, target in zip(shared, (h, z0, o)):
            for pack in range(packs):
                rows = pl.ds(pack * tokens, tokens)
                got_rest.append(copies.fetch(source.at[pack], target.at[rows]))
        for source, target in zip(one, whole):
            got_rest.append(copies.fetch(source.at[0], target.at[pl.ds(have, tokens)]))
    wait(got_g2)
    for pack in range(packs):
        rows = slice(pack * tokens, (pack + 1) * tokens)
        e2[rows] = rows_of(g2[:, pack : pack + 1]).astype(BF)
        wait(got_slope[pack])
        if pack == 0:
            wait(got_down, got_up)
        gm = feed_back(e2[rows], w_up, w_down, slope.at[pack], eu.at[rows])
        if pack == 0:
            wait(*got_z1, got_out)
        grad = unit_backward(gm * scale[...], z1[rows].astype(F32), inv1[pack, :, :1])
        total = rows_of(g2[:, pack : pack + 1]) + grad
        g1[pack] = total
        e1[rows] = total.astype(BF)
        go[pack] = nt(e1[rows], w_out[...]).astype(BF)
        copies.send(g1.at[pack], g1_out.at[pack])
    for pack in range(packs):
        wait(*got_attend[pack])
        rows = pl.ds(pack * tokens, tokens)
        attend_backward(qkv.at[pack], p.at[pack], go.at[pack], gqkv.at[rows], gp, gs)
        copies.send(gqkv.at[rows], gqkv_out.at[pack])
    if hierarchical:
        wait(*got_rest)
        feed_tiles(Halves(copies, ids, scratch[19:21], outs[:2]), z1, e2, eu, h, 0)
        place = Halves(copies, ids, scratch[21:23], outs[2:])
        attend_tiles(place, z0, o, gqkv, e1, 0, gqkv.shape[0])
    else:
        for source, target in zip((eu, e2, e1), outs):
            copies.send(source, target)
    copies.finish()


def to_send(labels, grad, out):
    for place in range(out.shape[1]):
        rows = grad[pack_at(labels, place), 0].astype(F32)
        out[:, place] = rows.reshape(out.shape[0], out.shape[2], out.shape[3]).astype(BF)


def pack_at(labels, place):
    packs, slots = labels.shape
    alone = packs - 1
    for pack in range(packs - 2, -1, -1):
        alone = jnp.where(labels[pack, slots - 1] == slots - 1, pack, alone)
    return jnp.where(place == packs - 1, alone, place + (place >= alone).astype(jnp.int32))


def without(kernel, first, count):
    def call(*refs):
        return kernel(*refs[:first], *refs[first + count :])

    return call


class Packs:
    def __init__(self, labels, first, count):
        self.labels, self.first, self.count = labels, first, count

    def call(self, kernel, args, outs, scratch=(), flops=0, after=()):
        first, last = self.first, self.labels.shape[0] - 2
        scalars = (self.labels,)

        def spec(kind, shape):
            rank = len(shape)
            if kind == "whole":
                return pl.BlockSpec(shape, lambda i, *s: (0,) * rank)
            if kind == "pack":
                return pl.BlockSpec(
                    (1,) + tuple(shape[1:]), lambda i, s: (pack_at(s, first + i),) + (0,) * (rank - 1)
                )
            if kind == "place":
                return pl.BlockSpec(
                    (1,) + tuple(shape[1:]), lambda i, *s: (first + i,) + (0,) * (rank - 1)
                )
            if kind == "step":
                return pl.BlockSpec(
                    (1,) + tuple(shape[1:]), lambda i, *s: (i,) + (0,) * (rank - 1)
                )
            if kind == "moved":
                return pl.BlockSpec(
                    (shape[0], 1, shape[2], shape[3]),
                    lambda i, *s: (0, jnp.minimum(i, last), 0, 0),
                )
            return pl.BlockSpec(memory_space=pl.ANY)

        in_specs = [spec(kind, array.shape) for kind, array in args]
        operands = [array for _, array in args]
        aliases = {}
        for index, (kind, shape, dtype, into) in enumerate(outs):
            if into is not None:
                aliases[len(scalars) + len(operands)] = index
                operands.append(into)
                in_specs.append(pl.BlockSpec(memory_space=pl.ANY))
        for array in after:
            operands.append(array)
            in_specs.append(pl.BlockSpec(memory_space=pl.ANY))
        moved = sum(a.size * a.dtype.itemsize for a in operands)
        unread = len(operands) - len(args)
        return pl.pallas_call(
            without(kernel, len(scalars) + len(args), unread),
            out_shape=[jax.ShapeDtypeStruct(shape, dtype) for _, shape, dtype, _ in outs],
            grid_spec=pltpu.PrefetchScalarGridSpec(
                num_scalar_prefetch=len(scalars),
                grid=(self.count,),
                in_specs=in_specs,
                out_specs=[spec(kind, shape) for kind, shape, _, _ in outs],
                scratch_shapes=list(scratch),
            ),
            input_output_aliases=aliases,
            compiler_params=pltpu.CompilerParams(
                vmem_limit_bytes=VMEM, dimension_semantics=("arbitrary",)
            ),
            cost_estimate=pl.CostEstimate(
                flops=int(flops * self.count * COST), bytes_accessed=int(moved * COST), transcendentals=0
            ),
        )(*scalars, *operands)


class Halves:
    def __init__(self, copies, ids, held, outs, z_first=False):
        self.copies, self.held, self.outs = copies, held, outs
        self.first, self.z, self.s, self.z_first = ids[0] == 0, ids[1], ids[2], z_first

    def at(self, s, z):
        s = slice(None) if s is None else s ^ self.s
        z = slice(None) if z is None else z ^ self.z
        return (z, s) if self.z_first else (s, z)

    def put(self, s, z, at, even, odd):
        rows = slice(at, at + even.shape[0])
        self.held[0][*self.at(s, z), rows] = jnp.where(self.first, even, odd)
        self.held[1][*self.at(s, z), rows] = jnp.where(self.first, odd, even)

    def send(self, s, z, at):
        for ref, out in zip(self.held, self.outs):
            index = *self.at(s, z), pl.ds(at, 64)
            self.copies.send(ref.at[index], out.at[index])


def feed_tiles(place, z1, e2, eu, h, at):
    for step in range(4):
        tile = tn(z1[...], eu[:, step * CHUNK : (step + 1) * CHUNK]).astype(BF)
        for z in range(4):
            row = 128 * z
            place.put(step, z, at, tile[row : row + 64], tile[row + 64 : row + 128])
        place.send(step, None, at)
    at = at + 64
    for step in range(4):
        tile = tn(e2[...], h[:, step * CHUNK : (step + 1) * CHUNK]).astype(BF)
        for s in range(4):
            upper, lower = tile[128 * s : 128 * s + 64], tile[128 * s + 64 : 128 * s + 128]
            even = jnp.concatenate([upper[:, :256], lower[:, :256]], axis=1)
            odd = jnp.concatenate([upper[:, 256:], lower[:, 256:]], axis=1)
            place.put(s, step, at, even, odd)
        place.send(None, step, at)


def attend_tiles(place, z0, o, gqkv, e1, at, depth):
    for step in range(4):
        if step == 3:
            tile = tn(o[...], e1[...])
        else:
            rows = gqkv.shape[0] if step == 2 else depth
            tile = tn(z0[:rows], gqkv[:rows, step * CHUNK : (step + 1) * CHUNK])
        tile = tile.astype(BF)
        for z in range(4):
            for s in range(4):
                row = 128 * z + 16 * s
                even, odd = tile[row : row + 16], tile[row + 64 : row + 80]
                place.put(s, z, at + 16 * step, even, odd)
    place.send(None, None, at)


def time_weights_kernel(ids, *rest):
    names = 8
    shared, one, outs, scratch = rest[:names], rest[names : 2 * names], rest[16:18], rest[18:]
    z1, eu, e2, h, z0, gqkv, o, e1 = scratch[:names]
    copies = Copies(scratch[-1])
    place = Halves(copies, ids, scratch[8:10], outs)
    packs, tokens, _ = shared[0].shape
    have = packs * tokens
    got = []
    for source, single, target in zip(shared, one, scratch):
        wide_target = target.at[pl.ds(have, tokens)]
        if single.shape[2] < target.shape[1]:
            wide_target = target.at[pl.ds(have, tokens), pl.ds(target.shape[1] - single.shape[2], single.shape[2])]
        got.append(
            [copies.fetch(source.at[pack], target.at[pl.ds(pack * tokens, tokens)]) for pack in range(packs)]
            + [copies.fetch(single.at[0], wide_target)]
        )
    wait(*got[0], *got[1], *got[2], *got[3])
    feed_tiles(place, z1, e2, eu, h, 0)
    wait(*got[4], *got[5], *got[6], *got[7])
    attend_tiles(place, z0, o, gqkv, e1, 128, have)
    copies.finish()


def manual_call(kernel, ids, args, outs, scratch, semaphores, small=0, after=(), flops=0):
    anywhere = pl.BlockSpec(memory_space=pl.ANY)
    return pl.pallas_call(
        without(kernel, 1 + len(args), len(after)),
        out_shape=[jax.ShapeDtypeStruct(shape, dtype) for shape, dtype in outs],
        in_specs=[pl.BlockSpec(memory_space=pltpu.SMEM)]
        + [pl.BlockSpec(memory_space=pltpu.VMEM)] * small
        + [anywhere] * (len(args) - small + len(after)),
        out_specs=[anywhere] * len(outs),
        scratch_shapes=[pltpu.VMEM(shape, dtype) for shape, dtype in scratch]
        + [pltpu.SemaphoreType.DMA((semaphores,))],
        compiler_params=pltpu.CompilerParams(vmem_limit_bytes=VMEM),
        cost_estimate=pl.CostEstimate(
            flops=int(flops * COST), bytes_accessed=0, transcendentals=0
        ),
    )(ids, *args, *after)


def swap(array, axis, size, mask):
    return lax.ppermute(array, axis, [(i, i ^ mask) for i in range(size)])


def add(*terms):
    total = terms[0].astype(F32)
    for term in terms[1:]:
        total = total + term.astype(F32)
    return total.astype(BF)


def core_sum(mine, got, *note):
    return [add(mine[d], got[d], *note) for d in range(1, 4)], (mine[0], got[0])


def stream_total(parts, own):
    return add(*own, *[swap(part, "stream", 4, d + 1) for d, part in enumerate(parts)])


def stream_sum(parts, own):
    got = [swap(part, "stream", 4, d + 1) for d, part in enumerate(parts)]
    return [add(*[term[d] for term in (*own, *got)]) for d in range(4)]


def z_sum(rows):
    return add(rows[0], *[swap(rows[d], "tm", 8, 2 * d) for d in range(1, 4)])


def gather_parts(final):
    return [final] + [swap(final, "stream", 4, d) for d in range(1, 4)]


def marker(array):
    def kernel(source, out):
        out[...] = jnp.zeros_like(out)

    return pl.pallas_call(
        kernel,
        out_shape=jax.ShapeDtypeStruct((1, CHUNK), F32),
        in_specs=[pl.BlockSpec(memory_space=pl.ANY)],
        out_specs=pl.BlockSpec(memory_space=pltpu.VMEM),
        cost_estimate=pl.CostEstimate(flops=10**12, bytes_accessed=10**8, transcendentals=0),
    )(array)


def z_scatter(rows):
    groups = [[0, 2, 4, 6], [1, 3, 5, 7]]
    got = lax.all_to_all(
        rows, "tm", split_axis=0, concat_axis=0, tiled=True, axis_index_groups=groups
    )
    return add(*[got[z] for z in range(4)])


def stream_total(parts, own):
    return add(*own, *[swap(part, "stream", 4, d + 1) for d, part in enumerate(parts)])


def stream_sum(parts, own):
    got = [swap(part, "stream", 4, d + 1) for d, part in enumerate(parts)]
    return [add(*[term[d] for term in (*own, *got)]) for d in range(4)]


def z_sum(rows):
    return add(rows[0], *[swap(rows[d], "tm", 8, 2 * d) for d in range(1, 4)])


def gather_parts(final):
    return [final] + [swap(final, "stream", 4, d) for d in range(1, 4)]


def marker(array):
    def kernel(source, out):
        out[...] = jnp.zeros_like(out)

    return pl.pallas_call(
        kernel,
        out_shape=jax.ShapeDtypeStruct((1, CHUNK), F32),
        in_specs=[pl.BlockSpec(memory_space=pl.ANY)],
        out_specs=pl.BlockSpec(memory_space=pltpu.VMEM),
        cost_estimate=pl.CostEstimate(flops=10**12, bytes_accessed=10**8, transcendentals=0),
    )(array)


def stream_total(parts, own):
    return add(*own, *[swap(part, "stream", 4, d + 1) for d, part in enumerate(parts)])


def stream_total(parts, own):
    return add(*own, *[swap(part, "stream", 4, d + 1) for d, part in enumerate(parts)])


def stream_sum(parts, own):
    got = [swap(part, "stream", 4, d + 1) for d, part in enumerate(parts)]
    return [add(*[term[d] for term in (*own, *got)]) for d in range(4)]


def z_sum(rows):
    return add(rows[0], *[swap(rows[d], "tm", 8, 2 * d) for d in range(1, 4)])


def gather_parts(final):
    return [final] + [swap(final, "stream", 4, d) for d in range(1, 4)]


def marker(array):
    def kernel(source, out):
        out[...] = jnp.zeros_like(out)

    return pl.pallas_call(
        kernel,
        out_shape=jax.ShapeDtypeStruct((1, CHUNK), F32),
        in_specs=[pl.BlockSpec(memory_space=pl.ANY)],
        out_specs=pl.BlockSpec(memory_space=pltpu.VMEM),
        cost_estimate=pl.CostEstimate(flops=10**12, bytes_accessed=10**8, transcendentals=0),
    )(array)


def add_call(mine, got, after):
    def kernel(a, b, out):
        out[...] = (a[...].astype(F32) + b[...].astype(F32)).astype(BF)

    block = pl.BlockSpec((1,) + mine.shape[1:], lambda i: (i,) + (0,) * (mine.ndim - 1))
    return pl.pallas_call(
        without(kernel, 2, len(after)),
        out_shape=jax.ShapeDtypeStruct(mine.shape, BF),
        grid=(mine.shape[0],),
        in_specs=[block, block] + [pl.BlockSpec(memory_space=pl.ANY)] * len(after),
        out_specs=block,
        compiler_params=pltpu.CompilerParams(vmem_limit_bytes=VMEM),
    )(mine, got, *after)


def scatter_sum(total):
    share = lax.psum_scatter(total, "stream", scatter_dimension=0)
    groups = [[0, 2, 4, 6], [1, 3, 5, 7]]
    return lax.psum_scatter(share, "tm", scatter_dimension=0, axis_index_groups=groups)


def as_row(col):
    size = col.shape[0]
    eye = lax.broadcasted_iota(jnp.int32, (size, size), 0) == lax.broadcasted_iota(
        jnp.int32, (size, size), 1
    )
    return jnp.sum(jnp.where(eye, col, 0.0), axis=0, keepdims=True)


def own_rows(ids, vector):
    shape = 64, vector.shape[1]
    row = lax.broadcasted_iota(jnp.int32, shape, 0) + 64 * (2 * ids[1] + ids[0])
    lane = lax.broadcasted_iota(jnp.int32, shape, 1)
    return jnp.sum(jnp.where(row == lane, vector[...], 0.0), axis=1, keepdims=True)


def finish_feed(ids, pieces, at, w_up, scale, scale_grad, up_grad, down_grad):
    factor = own_rows(ids, scale)
    for d, piece in enumerate(pieces):
        s = ids[2] ^ d
        up_grad[:, pl.ds(pl.multiple_of(512 * s, 512), 512)] = piece[at : at + 64].astype(F32)
        lower = piece[at + 64 : at + 128].astype(F32)
        whole = jnp.concatenate([lower[:, :256], lower[:, 256:]], axis=0)
        down_grad[:, pl.ds(pl.multiple_of(128 * s, 128), 128)] = whole.T
    total = up_grad[...]
    scale_grad[...] = as_row(jnp.sum(total * w_up[...].astype(F32), axis=1, keepdims=True))
    up_grad[...] = total * factor


def finish_attend(ids, pieces, at, w_in, gain, gain_grad, in_grad, out_grad):
    factor = own_rows(ids, gain)
    for d, piece in enumerate(pieces):
        rows = pl.ds(pl.multiple_of(16 * (ids[2] ^ d), 16), 16)
        for third in range(3):
            in_grad[rows, 512 * third : 512 * third + 512] = piece[
                at + 16 * third : at + 16 * third + 16
            ].astype(F32)
        out_grad[rows, :] = piece[at + 48 : at + 64].astype(F32)
    total = in_grad[...]
    gain_grad[...] = as_row(jnp.sum(total * w_in[...].astype(F32), axis=1, keepdims=True))
    in_grad[...] = total * factor


def finish_space_kernel(ids, p0, p1, p2, p3, *rest):
    pieces, outs = (p0, p1, p2, p3), rest[4:]
    finish_feed(ids, pieces, 0, *rest[0:2], *outs[0:3])
    finish_attend(ids, pieces, 128, *rest[2:4], *outs[3:6])


def finish_time_kernel(ids, p0, p1, p2, p3, *rest):
    finish_space_kernel(ids, p0, p1, p2, p3, *rest)


def finish_call(kernel, ids, pieces, pairs, outs):
    whole = pl.BlockSpec(pieces[0].shape, lambda i, *s: (0, 0))
    specs, operands = [], []
    for weight, vector in pairs:
        height = weight.shape[0] // 8
        specs += [
            pl.BlockSpec((height, weight.shape[1]), lambda i, s: (2 * s[1] + s[0], 0)),
            pl.BlockSpec((1, vector.size), lambda i, *s: (0, 0)),
        ]
        operands += [weight, vector.reshape(1, -1)]
    results = pl.pallas_call(
        kernel,
        out_shape=[jax.ShapeDtypeStruct(shape, F32) for shape in outs],
        grid_spec=pltpu.PrefetchScalarGridSpec(
            num_scalar_prefetch=1,
            grid=(1,),
            in_specs=[whole] * 4 + specs,
            out_specs=[pl.BlockSpec(shape, lambda i, *s: (0, 0)) for shape in outs],
        ),
        compiler_params=pltpu.CompilerParams(vmem_limit_bytes=SMALL_VMEM),
    )(ids, *pieces, *operands)
    return [a.reshape(-1) if a.shape[0] == 1 else a for a in results]


def plain_grads(z, grads, left, right, weight, vector):
    product = tn(z, grads)
    vector_grad = jnp.sum(product * weight.astype(F32), axis=1)
    sums = []
    for term in (vector_grad, product * vector[:, None], tn(left, right)):
        share = lax.psum_scatter(term.astype(BF), "tm", scatter_dimension=0, tiled=True)
        sums.append(lax.psum(share, "stream").astype(F32))
    return sums


def everyone_once(labels, grad, moved):
    _, shape, dtype, _ = moved
    return pl.pallas_call(
        to_send,
        out_shape=[jax.ShapeDtypeStruct(shape, dtype)],
        grid_spec=pltpu.PrefetchScalarGridSpec(
            num_scalar_prefetch=1,
            grid=(1,),
            in_specs=[pl.BlockSpec(grad.shape, lambda i, s: (0, 0, 0, 0))],
            out_specs=[pl.BlockSpec(shape, lambda i, s: (0, 0, 0, 0))],
        ),
        compiler_params=pltpu.CompilerParams(vmem_limit_bytes=VMEM),
    )(labels, grad)


def per_device(
    ranks,
    streams,
    frames,
    space_gain,
    space_input,
    space_output,
    space_scale,
    space_up,
    space_down,
    time_gain,
    time_input,
    time_output,
    time_scale,
    time_up,
    time_down,
    clip_labels,
    output_grad,
):
    packs, _, tokens, width = frames.shape
    slots = clip_labels.shape[1]
    patches = tokens // ranks
    hidden = space_up.shape[1]
    some = packs - 1
    hierarchical = (ranks, streams) == (8, 4)
    tm = lax.axis_index("tm")
    ids = jnp.stack([tm % 2, tm // 2, lax.axis_index("stream")]).astype(jnp.int32)
    shared = Packs(clip_labels, 0, some)
    single = Packs(clip_labels, some, 1)

    def row(vector):
        return vector.reshape(1, -1)

    def exchange(array):
        return lax.all_to_all(array, "tm", split_axis=0, concat_axis=0, tiled=True)

    def steps(count, *tails):
        return [("step", (count,) + tail, BF, None) for tail in tails]

    moved = ("moved", (slots, some, patches, width), BF, None)
    whole = ("pack", frames.shape, F32, None)
    flops = 2 * tokens * width * (4 * width + 2 * hidden)

    (sent,) = everyone_once(clip_labels, output_grad, moved)
    grad_moved = exchange(sent)

    space_args = [
        ("whole", row(space_gain)),
        ("whole", space_input),
        ("whole", space_output),
        ("whole", row(space_scale)),
        ("whole", space_up),
        ("whole", space_down),
    ]
    time_args = [
        ("whole", row(time_gain)),
        ("whole", time_input),
        ("whole", time_output),
        ("whole", row(time_scale)),
        ("whole", time_up),
        ("whole", time_down),
    ]
    rows_w, rows_3, rows_h = (tokens, width), (tokens, 3 * width), (tokens, hidden)
    spread = ("step", (some, tokens, LANES), F32, None)
    x2, sz0, sinv0, sqkv, sp, so, sz1, sinv1, sh, sslope = shared.call(
        space_forward,
        [("pack", frames)] + space_args,
        [moved]
        + steps(some, rows_w)
        + [spread]
        + steps(some, rows_3, (HEADS, tokens, tokens), rows_w, rows_w)
        + [spread]
        + steps(some, rows_h, rows_h),
        scratch=work_shapes(tokens),
        flops=flops,
        after=(sent,),
    )
    x2, grad_moved = lax.optimization_barrier((x2, grad_moved))
    x2_moved = exchange(x2)

    block_tails = [rows_w, rows_w, rows_w, rows_3, rows_w, rows_h, rows_h, rows_w]
    time_tails = [rows_w, rows_w, rows_w, rows_w, rows_w, rows_h, rows_h, rows_w]
    input_grad, result, *alone = single.call(
        alone_both,
        [("pack", frames), ("pack", output_grad)] + space_args + time_args,
        [whole, whole] + steps(1, *block_tails) + steps(1, *time_tails),
        scratch=[
            pltpu.VMEM((tokens, LANES), F32),
            pltpu.VMEM((tokens, LANES), F32),
            pltpu.VMEM(rows_3, BF),
            pltpu.VMEM((HEADS, tokens, tokens), BF),
            pltpu.VMEM(rows_h, BF),
            pltpu.VMEM(rows_h, BF),
            pltpu.VMEM(rows_w, BF),
        ]
        + work_shapes(tokens),
        flops=6 * flops,
        after=(x2,),
    )
    sz0_one, so_one, se1_one, sgqkv_one, sz1_one, seu_one, sh_one, se2_one = alone[:8]
    tz0_one, to_one, te1_one, tgv_one, tz1_one, teu_one, th_one, te2_one = alone[8:]

    g0, out, tz0, tgqkv, to, te1, tz1, teu, th, te2 = shared.call(
        time_both,
        [("moved", x2_moved), ("moved", grad_moved)] + time_args,
        [moved, moved] + steps(some, rows_w, rows_3, rows_w, rows_w, rows_w, rows_h, rows_h, rows_w),
        scratch=[
            pltpu.VMEM(rows_3, BF),
            pltpu.VMEM((HEADS, tokens, tokens), BF),
            pltpu.VMEM(rows_h, BF),
            pltpu.VMEM((tokens, tokens), F32),
        ]
        + work_shapes(tokens),
        flops=3 * flops,
        after=(sz0_one,),
    )
    g0_moved = exchange(g0)
    out, g0_moved = lax.optimization_barrier((out, g0_moved))
    out_moved = exchange(out)

    held_back = ()
    everything = packs * tokens
    feed_shapes = [(1, width // 8), (width // 8, hidden), (hidden // 8, width)]
    attend_shapes = [(1, width // 8), (width // 8, 3 * width), (width // 8, width)]
    time_shared = [tz1, teu, te2, th, tz0, tgqkv, to, te1]
    time_one = [tz1_one, teu_one, te2_one, th_one, tz0_one, tgv_one, to_one, te1_one]
    if hierarchical:
        parts_shape = ((4, 4, 192, CHUNK), BF)
        mine, other = manual_call(
            time_weights_kernel,
            jnp.stack([ids[0], jnp.int32(0), ids[2]]),
            time_shared + time_one,
            [parts_shape] * 2,
            [((everything, a.shape[2]), BF) for a in time_shared] + [parts_shape] * 2,
            8 * packs + 18,
            flops=packs * flops,
        )
        time_parts, time_own = core_sum(mine, swap(other, "tm", 8, 1), marker(g0_moved))
        held_back = tuple(time_parts)
    else:
        grad_one = jnp.pad(tgv_one, ((0, 0), (0, 0), (2 * width, 0)))
        joined = [joint(a, b) for a, b in zip(time_shared, time_one[:5] + [grad_one] + time_one[6:])]
        time_grads = plain_grads(joined[0], joined[1], joined[3], joined[2], time_up, time_scale)
        time_grads += plain_grads(joined[4], joined[5], joined[6], joined[7], time_input, time_gain)

    shared_w, shared_3 = (some,) + rows_w, (some,) + rows_3
    space_one = [sz1_one, seu_one, sh_one, se2_one, sz0_one, sgqkv_one, so_one, se1_one]
    whole_shapes = [((everything, a.shape[2]), BF) for a in space_one]
    parts_shapes = [((4, 4, 128, CHUNK), BF)] * 2 + [((4, 4, 64, CHUNK), BF)] * 2
    sg1, sgqkv, *weights = manual_call(
        functools.partial(space_kernel, hierarchical),
        ids,
        [row(space_scale), sinv1, g0_moved, sslope, sz1, space_output, space_up, space_down]
        + [sqkv, sp, sh, sz0, so]
        + space_one,
        [(shared_w, F32), (shared_3, BF)]
        + (parts_shapes if hierarchical else [whole_shapes[i] for i in (1, 3, 7)]),
        [
            (g0_moved.shape, BF),
            (sslope.shape, BF),
            (space_output.shape, BF),
            (space_up.shape, BF),
            (space_down.shape, BF),
            (sqkv.shape, BF),
            (sp.shape, BF),
            (shared_w, BF),
            (shared_w, F32),
            ((4, tokens, tokens), BF),
            ((HEADS, tokens, tokens), BF),
        ]
        + whole_shapes
        + (parts_shapes if hierarchical else []),
        80,
        small=2,
        after=held_back,
        flops=2 * packs * flops,
    )
    input_grad, result = shared.call(
        space_back_in,
        [
            ("step", sgqkv),
            ("whole", space_input),
            ("whole", row(space_gain)),
            ("step", sz0),
            ("step", sinv0),
            ("step", sg1),
            ("moved", out_moved),
        ],
        [("pack", frames.shape, F32, input_grad), ("pack", frames.shape, F32, result)],
        flops=flops // 4,
    )
    if hierarchical:
        feed, feed_other, attend_mine, attend_other = weights
        feed_got = swap(feed_other, "tm", 8, 1)
        attend_got = swap(attend_other, "tm", 8, 1)
        time_own, input_grad = lax.optimization_barrier((time_own, input_grad))
        time_rows = stream_total(time_parts, time_own)
        note = marker(time_rows)
        feed_parts = [add(feed[d], feed_got[d], note) for d in range(1, 4)]
        attend_got, feed_parts[0] = lax.optimization_barrier((attend_got, feed_parts[0]))
        attend_part = add(attend_mine[2:], attend_got[2:])
        rows = stream_sum(feed_parts, (feed[0], feed_got[0]))
        half = swap(attend_part, "stream", 4, 2)
        got, rows[1] = lax.optimization_barrier((attend_got[1], rows[1]))
        near = swap(add(attend_mine[1], got, half[1]), "stream", 4, 1)
        feed_final = z_sum(rows)
        own, feed_final = lax.optimization_barrier(((attend_mine[0], attend_got[0]), feed_final))
        attend_rows = [add(*[term[d] for term in (*own, half[0], near)]) for d in range(4)]
        final = jnp.concatenate([feed_final, z_sum(attend_rows)])
        grads = finish_call(
            finish_space_kernel,
            ids,
            gather_parts(final),
            [(space_up, space_scale), (space_input, space_gain)],
            feed_shapes + attend_shapes,
        )
        feed_grads, attend_grads = grads[:3], grads[3:]
        time_grads = finish_call(
            finish_time_kernel,
            ids,
            gather_parts(z_scatter(time_rows)),
            [(time_up, time_scale), (time_input, time_gain)],
            feed_shapes + attend_shapes,
        )
    else:
        have = some * tokens
        seu, se2, se1 = [a[:have].reshape(some, tokens, -1) for a in weights]
        feed_grads = plain_grads(
            joint(sz1, sz1_one),
            joint(seu, seu_one),
            joint(sh, sh_one),
            joint(se2, se2_one),
            space_up,
            space_scale,
        )
        attend_grads = plain_grads(
            joint(sz0, sz0_one),
            joint(sgqkv, sgqkv_one),
            joint(so, so_one),
            joint(se1, se1_one),
            space_input,
            space_gain,
        )
    grads = attend_grads + feed_grads + time_grads[3:] + time_grads[:3]
    return (result, input_grad, *grads)


def joint(shared, one):
    return jnp.concatenate([shared, one]).reshape(-1, shared.shape[-1])


def solution(mesh):
    tokens = P("stream", "tm", None, None)
    vector, matrix = P("tm"), P("tm", None)
    return jax.shard_map(
        functools.partial(per_device, mesh.shape["tm"], mesh.shape["stream"]),
        mesh=mesh,
        in_specs=(tokens,) + (P(),) * 12 + (P("stream", None), tokens),
        out_specs=(tokens, tokens) + (vector, matrix, matrix, vector, matrix, matrix) * 2,
        check_vma=False,
    )
```

```python
import functools

import jax
import jax.numpy as jnp
from jax import lax
from jax.experimental import pallas as pl
from jax.experimental.pallas import tpu as pltpu
from jax.sharding import PartitionSpec as P

HEADS = 8
EPS = 1e-05
GELU_A = 0.7978845608028654
GELU_B = 0.044715
BF = jnp.bfloat16
F32 = jnp.float32
CHUNK = 512
LANES = 128
COST = 1
ROWS = (0, 96, 64, 80, 160, 176)
VMEM = 60 * 1024 * 1024
SMALL_VMEM = 24 * 1024 * 1024


def nn(a, b):
    return jnp.dot(a, b, preferred_element_type=F32)


def nt(a, b):
    return lax.dot_general(a, b, (((1,), (1,)), ((), ())), preferred_element_type=F32)


def tn(a, b):
    return lax.dot_general(a, b, (((0,), (0,)), ((), ())), preferred_element_type=F32)


def unit(values):
    average = jnp.mean(values, axis=-1, keepdims=True)
    centered = values - average
    inverse = lax.rsqrt(jnp.mean(centered * centered, axis=-1, keepdims=True) + EPS)
    return centered * inverse, inverse


def unit_backward(grad, unit_rows, inverse):
    first = jnp.mean(grad, axis=-1, keepdims=True)
    second = jnp.mean(grad * unit_rows, axis=-1, keepdims=True)
    return inverse * (grad - first - unit_rows * second)


def gelu_parts(u):
    square = u * u
    tangent = jnp.tanh(u * (BF(GELU_A) + BF(GELU_A * GELU_B) * square))
    half = BF(0.5) * u
    value = half + half * tangent
    slope = (BF(0.5) + BF(0.5) * tangent) + half * (BF(1.0) - tangent * tangent) * (
        BF(GELU_A) + BF(3.0 * GELU_A * GELU_B) * square
    )
    return value, slope


def head_masks(width):
    lane = lax.broadcasted_iota(jnp.int32, (1, 2 * width), 1)
    low = lane < width
    return low, (low.astype(F32).astype(BF), (1.0 - low.astype(F32)).astype(BF))


def attend(qkv_ref, p_ref, o_ref, bias_ref, s_ref):
    width = qkv_ref.shape[1] // 3
    size = width // HEADS
    _, masks = head_masks(size)

    def lanes(part, head):
        at = part * width + (head // 2) * 2 * size
        return qkv_ref[:, at : at + 2 * size]

    def score(head):
        s_ref[head % 4] = nt(lanes(1, head) * masks[head % 2], lanes(0, head) * BF(size**-0.5))

    def soften(head):
        scores = s_ref[head % 4]
        if bias_ref is not None:
            scores = scores + bias_ref[...]
        e = jnp.exp(scores - jnp.max(scores, axis=0, keepdims=True))
        p_ref[head] = (e * (1.0 / jnp.sum(e, axis=0, keepdims=True))).astype(BF)

    for head in range(0, HEADS, 2):
        if head == 0:
            score(0)
            score(1)
        if head + 2 < HEADS:
            score(head + 2)
            score(head + 3)
        soften(head)
        soften(head + 1)
    for head in range(0, HEADS, 2):
        v = lanes(2, head).T
        both = jnp.concatenate([nn(v[:size], p_ref[head]), nn(v[size:], p_ref[head + 1])], axis=0)
        o_ref[:, head * size : (head + 2) * size] = both.T.astype(BF)


def attend_backward(qkv_ref, p_ref, go_ref, out_ref, gp_ref, gs_ref):
    width = qkv_ref.shape[1] // 3
    size = width // HEADS
    _, masks = head_masks(size)

    def lanes(part, head):
        at = part * width + (head // 2) * 2 * size
        return qkv_ref[:, at : at + 2 * size]

    def gos(head):
        return go_ref[:, (head // 2) * 2 * size : (head // 2 + 1) * 2 * size]

    def put(part, head, value):
        at = part * width + head * size
        out_ref[:, at : at + 2 * size] = value.astype(BF)

    def start(head):
        for h in (head, head + 1):
            gp_ref[h % 4] = nt(lanes(2, h) * masks[h % 2], gos(h)).astype(BF)
        g = gos(head)
        put(2, head, nn(p_ref[head], g * masks[0]) + nn(p_ref[head + 1], g * masks[1]))

    def middle(head):
        p = p_ref[head]
        weighted = p * gp_ref[head % 4]
        total = jnp.sum(weighted.astype(F32), axis=0, keepdims=True).astype(BF)
        gs_ref[head] = weighted - p * total

    def finish(head):
        q = lanes(0, head) * BF(size**-0.5)
        k = (lanes(1, head) * BF(size**-0.5)).T
        put(1, head, nn(gs_ref[head], q * masks[0]) + nn(gs_ref[head + 1], q * masks[1]))
        both = jnp.concatenate([nn(k[:size], gs_ref[head]), nn(k[size:], gs_ref[head + 1])], axis=0)
        put(0, head, both.T)

    start(0)
    for head in range(0, HEADS, 2):
        middle(head)
        middle(head + 1)
        if head + 2 < HEADS:
            start(head + 2)
        if head > 0:
            finish(head - 2)
    finish(HEADS - 2)


def feed_up(m, up_ref, down_ref, h_ref, slope_ref, u_ref):
    steps = up_ref.shape[1] // CHUNK

    def before(step):
        u_ref[step % 2] = nn(m, up_ref[:, step * CHUNK : (step + 1) * CHUNK]).astype(BF)

    before(0)
    for step in range(steps):
        if step + 1 < steps:
            before(step + 1)
        at = step * CHUNK
        h_ref[:, at : at + CHUNK], slope_ref[:, at : at + CHUNK] = gelu_parts(u_ref[step % 2])
    return nn(h_ref[...], down_ref[...])


def feed_back(e2, up_ref, down_ref, slope_ref, eu_ref):
    for at in range(0, up_ref.shape[1], CHUNK):
        gh = nt(e2, down_ref[at : at + CHUNK, :]).astype(BF)
        eu_ref[:, at : at + CHUNK] = gh * slope_ref[:, at : at + CHUNK]
    return nt(eu_ref[...], up_ref[...])


def rows_of(block):
    slots, _, patches, width = block.shape
    return block[:, 0].astype(F32).reshape(slots * patches, width)


def block_of(rows, ref):
    slots, _, patches, width = ref.shape
    ref[:, 0] = rows.reshape(slots, patches, width).astype(ref.dtype)


def work_shapes(tokens):
    return [
        pltpu.VMEM((4, tokens, tokens), F32),
        pltpu.VMEM((2, tokens, CHUNK), BF),
        pltpu.VMEM((4, tokens, tokens), BF),
        pltpu.VMEM((HEADS, tokens, tokens), BF),
    ]


def wide(column):
    return jnp.broadcast_to(column, (column.shape[0], LANES))


def space_rows(x, weights, state, work):
    gain, w_in, w_out, scale, w_up, w_down = weights
    z0, inv0, qkv, p, o, z1, inv1, h, slope = state
    unit0, inverse0 = unit(x)
    z0[...] = unit0.astype(BF)
    inv0[...] = wide(inverse0)
    qkv[...] = nn((unit0 * gain[...]).astype(BF), w_in[...]).astype(BF)
    attend(qkv, p, o, None, work[0])
    r1 = x + nn(o[...], w_out[...])
    unit1, inverse1 = unit(r1)
    z1[...] = unit1.astype(BF)
    inv1[...] = wide(inverse1)
    m = (unit1 * scale[...]).astype(BF)
    return r1 + feed_up(m, w_up, w_down, h, slope, work[1])


def space_forward(labels, frames, *rest):
    weights, x2, state, work = rest[:6], rest[6], rest[7:16], rest[16:]
    rows = space_rows(frames[0, 0].astype(F32), weights, [ref.at[0] for ref in state], work)
    block_of(rows, x2)


def build_bias(labels, pack, slots, patches, bias):
    tokens = slots * patches
    row = lax.broadcasted_iota(jnp.int32, (1, tokens), 1)
    column = lax.broadcasted_iota(jnp.int32, (tokens, 1), 0)

    def label_of(position):
        slot = position // patches
        value = jnp.zeros_like(position)
        for f in range(slots):
            value = jnp.where(slot == f, labels[pack, f], value)
        return value

    same_patch = (row % patches) == (column % patches)
    allowed = same_patch & (column <= row) & (label_of(column) == label_of(row))
    bias[...] = jnp.where(allowed, 0.0, -1e30)


def time_both(labels, x2, grad, *rest):
    gain, w_in, w_out, scale, w_up, w_down = rest[:6]
    g0, out, z0, gqkv, o, e1, z1, eu, h, e2 = rest[6:16]
    qkv, p, slope, bias, *work = rest[16:]
    slots, _, patches, _ = x2.shape
    build_bias(labels, pack_at(labels, pl.program_id(0)), slots, patches, bias)
    x = rows_of(x2[...])
    unit0, inverse0 = unit(x)
    z0[0] = unit0.astype(BF)
    qkv[...] = nn((unit0 * gain[...]).astype(BF), w_in[...]).astype(BF)
    attend(qkv, p, o.at[0], bias, work[0])
    r1 = x + nn(o[0], w_out[...])
    unit1, inverse1 = unit(r1)
    z1[0] = unit1.astype(BF)
    m = (unit1 * scale[...]).astype(BF)
    block_of(r1 + feed_up(m, w_up, w_down, h.at[0], slope, work[1]), out)
    g2 = rows_of(grad[...])
    e2[0] = g2.astype(BF)
    gm = feed_back(e2[0], w_up, w_down, slope, eu.at[0])
    g1 = g2 + unit_backward(gm * scale[...], unit1, inverse1)
    e1[0] = g1.astype(BF)
    slope[:, : g1.shape[1]] = nt(e1[0], w_out[...]).astype(BF)
    attend_backward(qkv, p, slope, gqkv.at[0], work[2], work[3])
    gn = nt(gqkv[0], w_in[...])
    block_of(g1 + unit_backward(gn * gain[...], unit0, inverse0), g0)


def alone_both(labels, frames, grad, *rest):
    space, (gain, w_in, w_out, scale, w_up, w_down) = rest[:6], rest[6:12]
    input_grad, out = rest[12:14]
    sz0, so, se1, sgqkv, sz1, seu, sh, se2 = [ref.at[0] for ref in rest[14:22]]
    z0, o, e1, gv, z1, eu, h, e2 = [ref.at[0] for ref in rest[22:30]]
    inv0, inv1, qkv, p, sslope, slope, go, *work = rest[30:]
    state = sz0, inv0, qkv, p, so, sz1, inv1, sh, sslope
    x = space_rows(frames[0, 0].astype(F32), space, state, work)
    width = x.shape[1]
    unit0, inverse0 = unit(x)
    z0[...] = unit0.astype(BF)
    o[...] = nn((unit0 * gain[...]).astype(BF), w_in[:, 2 * width :]).astype(BF)
    r1 = x + nn(o[...], w_out[...])
    unit1, inverse1 = unit(r1)
    z1[...] = unit1.astype(BF)
    m = (unit1 * scale[...]).astype(BF)
    out[0, 0] = r1 + feed_up(m, w_up, w_down, h, slope, work[1])
    e2[...] = grad[0, 0]
    g2 = grad[0, 0].astype(F32)
    gm = feed_back(e2[...], w_up, w_down, slope, eu)
    g1 = g2 + unit_backward(gm * scale[...], unit1, inverse1)
    e1[...] = g1.astype(BF)
    gv[...] = nt(e1[...], w_out[...]).astype(BF)
    gn = nt(gv[...], w_in[:, 2 * width :])
    g2 = g1 + unit_backward(gn * gain[...], unit0, inverse0)
    gain, w_in, w_out, scale, w_up, w_down = space
    se2[...] = g2.astype(BF)
    gm = feed_back(se2[...], w_up, w_down, sslope, seu)
    g1 = g2 + unit_backward(gm * scale[...], sz1[...].astype(F32), inv1[:, :1])
    se1[...] = g1.astype(BF)
    go[...] = nt(se1[...], w_out[...]).astype(BF)
    attend_backward(qkv, p, go, sgqkv, work[2], work[3])
    gn = nt(sgqkv[...], w_in[...])
    input_grad[0, 0] = g1 + unit_backward(gn * gain[...], sz0[...].astype(F32), inv0[:, :1])


def space_back_in(labels, gqkv, w_in, gain, z0, inv0, g1, moved, input_grad, result):
    gn = nt(gqkv[0], w_in[...])
    grad = unit_backward(gn * gain[...], z0[0].astype(F32), inv0[0, :, :1])
    input_grad[0, 0] = g1[0] + grad
    result[0, 0] = rows_of(moved[...])


class Copies:
    def __init__(self, semaphores):
        self.semaphores, self.count, self.sent = semaphores, 0, []

    def fetch(self, source, target):
        copy = pltpu.make_async_copy(source, target, self.semaphores.at[self.count])
        self.count += 1
        copy.start()
        return copy

    def send(self, source, target):
        self.sent.append(self.fetch(source, target))

    def finish(self):
        for copy in self.sent:
            copy.wait()


def wait(*copies):
    for copy in copies:
        copy.wait()


def space_kernel(hierarchical, ids, scale, inv1, *rest):
    (g2_in, slope_in, z1_in, w_out_in, w_up_in, w_down_in, qkv_in, p_in), rest = rest[:8], rest[8:]
    shared, one, rest = rest[:3], rest[3:11], rest[11:]
    (g1_out, gqkv_out), outs, scratch = rest[:2], rest[2 : 6 if hierarchical else 5], rest[6 if hierarchical else 5 :]
    g2, slope, w_out, w_up, w_down, qkv, p, go, g1, gp, gs = scratch[:11]
    z1, eu, h, e2, z0, gqkv, o, e1 = whole = scratch[11:19]
    copies = Copies(scratch[-1])
    packs, tokens, _ = g1.shape
    have = packs * tokens
    got_g2 = copies.fetch(g2_in, g2)
    got_down = copies.fetch(w_down_in, w_down)
    got_slope = [copies.fetch(slope_in.at[pack], slope.at[pack]) for pack in range(packs)]
    got_up = copies.fetch(w_up_in, w_up)
    got_z1 = [
        copies.fetch(z1_in.at[pack], z1.at[pl.ds(pack * tokens, tokens)]) for pack in range(packs)
    ]
    got_out = copies.fetch(w_out_in, w_out)
    got_attend = [
        (copies.fetch(qkv_in.at[pack], qkv.at[pack]), copies.fetch(p_in.at[pack], p.at[pack]))
        for pack in range(packs)
    ]
    got_rest = []
    if hierarchical:
        for source, target in zip(shared, (h, z0, o)):
            for pack in range(packs):
                rows = pl.ds(pack * tokens, tokens)
                got_rest.append(copies.fetch(source.at[pack], target.at[rows]))
        for source, target in zip(one, whole):
            got_rest.append(copies.fetch(source.at[0], target.at[pl.ds(have, tokens)]))
    wait(got_g2)
    for pack in range(packs):
        rows = slice(pack * tokens, (pack + 1) * tokens)
        e2[rows] = rows_of(g2[:, pack : pack + 1]).astype(BF)
        wait(got_slope[pack])
        if pack == 0:
            wait(got_down, got_up)
        gm = feed_back(e2[rows], w_up, w_down, slope.at[pack], eu.at[rows])
        if pack == 0:
            wait(*got_z1, got_out)
        grad = unit_backward(gm * scale[...], z1[rows].astype(F32), inv1[pack, :, :1])
        total = rows_of(g2[:, pack : pack + 1]) + grad
        g1[pack] = total
        e1[rows] = total.astype(BF)
        go[pack] = nt(e1[rows], w_out[...]).astype(BF)
        copies.send(g1.at[pack], g1_out.at[pack])
    for pack in range(packs):
        wait(*got_attend[pack])
        rows = pl.ds(pack * tokens, tokens)
        attend_backward(qkv.at[pack], p.at[pack], go.at[pack], gqkv.at[rows], gp, gs)
        copies.send(gqkv.at[rows], gqkv_out.at[pack])
    if hierarchical:
        wait(*got_rest)
        one = Halves(copies, ids, scratch[19:21], outs[:2], x_high=True)
        two = Halves(copies, ids, scratch[21:23], outs[2:])
        up_tiles(one, z1, eu, 0)
        down_tiles(two, e2, h, 0)
        attend_tiles([one, one, two, two], z0, o, gqkv, e1, [64, 80, 64, 80], gqkv.shape[0])
    else:
        for source, target in zip((eu, e2, e1), outs):
            copies.send(source, target)
    copies.finish()


def to_send(labels, grad, out):
    for place in range(out.shape[1]):
        rows = grad[pack_at(labels, place), 0].astype(F32)
        out[:, place] = rows.reshape(out.shape[0], out.shape[2], out.shape[3]).astype(BF)


def pack_at(labels, place):
    packs, slots = labels.shape
    alone = packs - 1
    for pack in range(packs - 2, -1, -1):
        alone = jnp.where(labels[pack, slots - 1] == slots - 1, pack, alone)
    return jnp.where(place == packs - 1, alone, place + (place >= alone).astype(jnp.int32))


def without(kernel, first, count):
    def call(*refs):
        return kernel(*refs[:first], *refs[first + count :])

    return call


class Packs:
    def __init__(self, labels, first, count):
        self.labels, self.first, self.count = labels, first, count

    def call(self, kernel, args, outs, scratch=(), flops=0, after=()):
        first, last = self.first, self.labels.shape[0] - 2
        scalars = (self.labels,)

        def spec(kind, shape):
            rank = len(shape)
            if kind == "whole":
                return pl.BlockSpec(shape, lambda i, *s: (0,) * rank)
            if kind == "pack":
                return pl.BlockSpec(
                    (1,) + tuple(shape[1:]), lambda i, s: (pack_at(s, first + i),) + (0,) * (rank - 1)
                )
            if kind == "place":
                return pl.BlockSpec(
                    (1,) + tuple(shape[1:]), lambda i, *s: (first + i,) + (0,) * (rank - 1)
                )
            if kind == "step":
                return pl.BlockSpec(
                    (1,) + tuple(shape[1:]), lambda i, *s: (i,) + (0,) * (rank - 1)
                )
            if kind == "moved":
                return pl.BlockSpec(
                    (shape[0], 1, shape[2], shape[3]),
                    lambda i, *s: (0, jnp.minimum(i, last), 0, 0),
                )
            return pl.BlockSpec(memory_space=pl.ANY)

        in_specs = [spec(kind, array.shape) for kind, array in args]
        operands = [array for _, array in args]
        aliases = {}
        for index, (kind, shape, dtype, into) in enumerate(outs):
            if into is not None:
                aliases[len(scalars) + len(operands)] = index
                operands.append(into)
                in_specs.append(pl.BlockSpec(memory_space=pl.ANY))
        for array in after:
            operands.append(array)
            in_specs.append(pl.BlockSpec(memory_space=pl.ANY))
        moved = sum(a.size * a.dtype.itemsize for a in operands)
        unread = len(operands) - len(args)
        return pl.pallas_call(
            without(kernel, len(scalars) + len(args), unread),
            out_shape=[jax.ShapeDtypeStruct(shape, dtype) for _, shape, dtype, _ in outs],
            grid_spec=pltpu.PrefetchScalarGridSpec(
                num_scalar_prefetch=len(scalars),
                grid=(self.count,),
                in_specs=in_specs,
                out_specs=[spec(kind, shape) for kind, shape, _, _ in outs],
                scratch_shapes=list(scratch),
            ),
            input_output_aliases=aliases,
            compiler_params=pltpu.CompilerParams(
                vmem_limit_bytes=VMEM, dimension_semantics=("arbitrary",)
            ),
            cost_estimate=pl.CostEstimate(
                flops=int(flops * self.count * COST), bytes_accessed=int(moved * COST), transcendentals=0
            ),
        )(*scalars, *operands)


class Halves:
    def __init__(self, copies, ids, held, outs, x_high=False):
        self.copies, self.held, self.outs = copies, held, outs
        self.first, self.z, self.s, self.x_high = ids[0] == 0, ids[1], ids[2], x_high

    def part(self, s):
        if s is None:
            return slice(None)
        part = s ^ self.s
        return (part & 1) * 2 + (part >> 1) if self.x_high else part

    def put(self, s, z, at, even, odd):
        rows = slice(at, at + even.shape[0])
        self.held[0][self.part(s), z ^ self.z, rows] = jnp.where(self.first, even, odd)
        self.held[1][self.part(s), z ^ self.z, rows] = jnp.where(self.first, odd, even)

    def send(self, s, z, at, rows):
        index = self.part(s), slice(None) if z is None else z ^ self.z, pl.ds(at, rows)
        for ref, out in zip(self.held, self.outs):
            self.copies.send(ref.at[index], out.at[index])


def up_tiles(place, z1, eu, at):
    for step in range(4):
        tile = tn(z1[...], eu[:, step * CHUNK : (step + 1) * CHUNK]).astype(BF)
        for z in range(4):
            row = 128 * z
            place.put(step, z, at, tile[row : row + 64], tile[row + 64 : row + 128])
        place.send(step, None, at, 64)


def down_tiles(place, e2, h, at):
    for step in range(4):
        tile = tn(e2[...], h[:, step * CHUNK : (step + 1) * CHUNK]).astype(BF)
        for s in range(4):
            upper, lower = tile[128 * s : 128 * s + 64], tile[128 * s + 64 : 128 * s + 128]
            even = jnp.concatenate([upper[:, :256], lower[:, :256]], axis=1)
            odd = jnp.concatenate([upper[:, 256:], lower[:, 256:]], axis=1)
            place.put(s, step, at, even, odd)
        place.send(None, step, at, 64)


def attend_tiles(places, z0, o, gqkv, e1, ats, depth):
    for step, (place, at) in enumerate(zip(places, ats)):
        if step == 3:
            tile = tn(o[...], e1[...])
        else:
            rows = gqkv.shape[0] if step == 2 else depth
            tile = tn(z0[:rows], gqkv[:rows, step * CHUNK : (step + 1) * CHUNK])
        tile = tile.astype(BF)
        for z in range(4):
            for s in range(4):
                row = 128 * z + 16 * s
                place.put(s, z, at, tile[row : row + 16], tile[row + 64 : row + 80])
        if step % 2:
            place.send(None, None, at - 16, 32)


def time_weights_kernel(ids, *rest):
    names = 8
    shared, single, outs, scratch = rest[:names], rest[names : 2 * names], rest[16:20], rest[20:]
    z1, eu, e2, h, z0, gqkv, o, e1 = scratch[:names]
    copies = Copies(scratch[-1])
    one = Halves(copies, ids, scratch[8:10], outs[:2], x_high=True)
    two = Halves(copies, ids, scratch[10:12], outs[2:])
    packs, tokens, _ = shared[0].shape
    have = packs * tokens
    got = []
    for source, last, target in zip(shared, single, scratch):
        wide_target = target.at[pl.ds(have, tokens)]
        if last.shape[2] < target.shape[1]:
            wide_target = target.at[pl.ds(have, tokens), pl.ds(target.shape[1] - last.shape[2], last.shape[2])]
        got.append(
            [copies.fetch(source.at[pack], target.at[pl.ds(pack * tokens, tokens)]) for pack in range(packs)]
            + [copies.fetch(last.at[0], wide_target)]
        )
    wait(*got[0], *got[1], *got[2], *got[3])
    up_tiles(one, z1, eu, 0)
    down_tiles(two, e2, h, 0)
    wait(*got[4], *got[5], *got[6], *got[7])
    attend_tiles([one, one, two, two], z0, o, gqkv, e1, [64, 80, 64, 80], have)
    copies.finish()


def manual_call(kernel, ids, args, outs, scratch, semaphores, small=0, after=(), flops=0):
    anywhere = pl.BlockSpec(memory_space=pl.ANY)
    return pl.pallas_call(
        without(kernel, 1 + len(args), len(after)),
        out_shape=[jax.ShapeDtypeStruct(shape, dtype) for shape, dtype in outs],
        in_specs=[pl.BlockSpec(memory_space=pltpu.SMEM)]
        + [pl.BlockSpec(memory_space=pltpu.VMEM)] * small
        + [anywhere] * (len(args) - small + len(after)),
        out_specs=[anywhere] * len(outs),
        scratch_shapes=[pltpu.VMEM(shape, dtype) for shape, dtype in scratch]
        + [pltpu.SemaphoreType.DMA((semaphores,))],
        compiler_params=pltpu.CompilerParams(vmem_limit_bytes=VMEM),
        cost_estimate=pl.CostEstimate(
            flops=int(flops * COST), bytes_accessed=0, transcendentals=0
        ),
    )(ids, *args, *after)


def swap(array, axis, size, mask):
    return lax.ppermute(array, axis, [(i, i ^ mask) for i in range(size)])


def add(*terms):
    total = terms[0].astype(F32)
    for term in terms[1:]:
        total = total + term.astype(F32)
    return total.astype(BF)


def far_parts(mine, got, note):
    return [add(a[2:], b[2:], note) for a, b in zip(mine, got)]


def near_parts(mine, got, far):
    halves = [swap(far[0], "stream", 4, 1), swap(far[1], "stream", 4, 2)]
    return halves, [add(a[1], b[1], half[1]) for a, b, half in zip(mine, got, halves)]


def stream_rows(mine, got, halves, near):
    last = [swap(near[0], "stream", 4, 2), swap(near[1], "stream", 4, 1)]
    terms = list(zip(mine, got, halves, last))
    return [
        jnp.concatenate([add(a[0][d], b[0][d], half[0][d], end[d]) for a, b, half, end in terms])
        for d in range(4)
    ]


def z_sum(rows):
    return add(rows[0], *[swap(rows[d], "tm", 8, 2 * d) for d in range(1, 4)])


def gather_parts(final):
    return [final] + [swap(final, "stream", 4, d) for d in range(1, 4)]


def marker(array):
    def kernel(source, out):
        out[...] = jnp.zeros_like(out)

    return pl.pallas_call(
        kernel,
        out_shape=jax.ShapeDtypeStruct((1, CHUNK), F32),
        in_specs=[pl.BlockSpec(memory_space=pl.ANY)],
        out_specs=pl.BlockSpec(memory_space=pltpu.VMEM),
        cost_estimate=pl.CostEstimate(flops=10**12, bytes_accessed=10**8, transcendentals=0),
    )(array)


def stream_total(parts, own):
    return add(*own, *[swap(part, "stream", 4, d + 1) for d, part in enumerate(parts)])


def stream_total(parts, own):
    return add(*own, *[swap(part, "stream", 4, d + 1) for d, part in enumerate(parts)])


def stream_sum(parts, own):
    got = [swap(part, "stream", 4, d + 1) for d, part in enumerate(parts)]
    return [add(*[term[d] for term in (*own, *got)]) for d in range(4)]


def halved_sum(mine, got, far, first, second):
    half = swap(far, "stream", 4, first)
    near = swap(add(mine[1], got[1], half[1]), "stream", 4, second)
    return [(mine[0][d], got[0][d], half[0][d], near[d]) for d in range(4)]


def z_sum(rows):
    return add(rows[0], *[swap(rows[d], "tm", 8, 2 * d) for d in range(1, 4)])


def gather_parts(final):
    return [final] + [swap(final, "stream", 4, d) for d in range(1, 4)]


def marker(array):
    def kernel(source, out):
        out[...] = jnp.zeros_like(out)

    return pl.pallas_call(
        kernel,
        out_shape=jax.ShapeDtypeStruct((1, CHUNK), F32),
        in_specs=[pl.BlockSpec(memory_space=pl.ANY)],
        out_specs=pl.BlockSpec(memory_space=pltpu.VMEM),
        cost_estimate=pl.CostEstimate(flops=10**12, bytes_accessed=10**8, transcendentals=0),
    )(array)


def add_call(mine, got, after):
    def kernel(a, b, out):
        out[...] = (a[...].astype(F32) + b[...].astype(F32)).astype(BF)

    block = pl.BlockSpec((1,) + mine.shape[1:], lambda i: (i,) + (0,) * (mine.ndim - 1))
    return pl.pallas_call(
        without(kernel, 2, len(after)),
        out_shape=jax.ShapeDtypeStruct(mine.shape, BF),
        grid=(mine.shape[0],),
        in_specs=[block, block] + [pl.BlockSpec(memory_space=pl.ANY)] * len(after),
        out_specs=block,
        compiler_params=pltpu.CompilerParams(vmem_limit_bytes=VMEM),
    )(mine, got, *after)


def scatter_sum(total):
    share = lax.psum_scatter(total, "stream", scatter_dimension=0)
    groups = [[0, 2, 4, 6], [1, 3, 5, 7]]
    return lax.psum_scatter(share, "tm", scatter_dimension=0, axis_index_groups=groups)


def as_row(col):
    size = col.shape[0]
    eye = lax.broadcasted_iota(jnp.int32, (size, size), 0) == lax.broadcasted_iota(
        jnp.int32, (size, size), 1
    )
    return jnp.sum(jnp.where(eye, col, 0.0), axis=0, keepdims=True)


def own_rows(ids, vector):
    shape = 64, vector.shape[1]
    row = lax.broadcasted_iota(jnp.int32, shape, 0) + 64 * (2 * ids[1] + ids[0])
    lane = lax.broadcasted_iota(jnp.int32, shape, 1)
    return jnp.sum(jnp.where(row == lane, vector[...], 0.0), axis=1, keepdims=True)


def finish_kernel(ids, p0, p1, p2, p3, w_up, scale, w_in, gain, *outs):
    scale_grad, up_grad, down_grad, gain_grad, in_grad, out_grad = outs
    up_at, down_at, *in_at, out_at = ROWS
    for d, piece in enumerate((p0, p1, p2, p3)):
        s = ids[2] ^ d
        up_grad[:, pl.ds(pl.multiple_of(512 * s, 512), 512)] = piece[up_at : up_at + 64].astype(F32)
        lower = piece[down_at : down_at + 64].astype(F32)
        whole = jnp.concatenate([lower[:, :256], lower[:, 256:]], axis=0)
        down_grad[:, pl.ds(pl.multiple_of(128 * s, 128), 128)] = whole.T
        rows = pl.ds(pl.multiple_of(16 * s, 16), 16)
        for third, at in enumerate(in_at):
            in_grad[rows, 512 * third : 512 * third + 512] = piece[at : at + 16].astype(F32)
        out_grad[rows, :] = piece[out_at : out_at + 16].astype(F32)
    for grad, weight, factor, vector_grad in (
        (up_grad, w_up, scale, scale_grad),
        (in_grad, w_in, gain, gain_grad),
    ):
        total = grad[...]
        vector_grad[...] = as_row(jnp.sum(total * weight[...].astype(F32), axis=1, keepdims=True))
        grad[...] = total * own_rows(ids, factor)


def finish_call(kernel, ids, pieces, pairs, outs):
    whole = pl.BlockSpec(pieces[0].shape, lambda i, *s: (0, 0))
    specs, operands = [], []
    for weight, vector in pairs:
        height = weight.shape[0] // 8
        specs += [
            pl.BlockSpec((height, weight.shape[1]), lambda i, s: (2 * s[1] + s[0], 0)),
            pl.BlockSpec((1, vector.size), lambda i, *s: (0, 0)),
        ]
        operands += [weight, vector.reshape(1, -1)]
    results = pl.pallas_call(
        kernel,
        out_shape=[jax.ShapeDtypeStruct(shape, F32) for shape in outs],
        grid_spec=pltpu.PrefetchScalarGridSpec(
            num_scalar_prefetch=1,
            grid=(1,),
            in_specs=[whole] * 4 + specs,
            out_specs=[pl.BlockSpec(shape, lambda i, *s: (0, 0)) for shape in outs],
        ),
        compiler_params=pltpu.CompilerParams(vmem_limit_bytes=SMALL_VMEM),
    )(ids, *pieces, *operands)
    return [a.reshape(-1) if a.shape[0] == 1 else a for a in results]


def plain_grads(z, grads, left, right, weight, vector):
    product = tn(z, grads)
    vector_grad = jnp.sum(product * weight.astype(F32), axis=1)
    sums = []
    for term in (vector_grad, product * vector[:, None], tn(left, right)):
        share = lax.psum_scatter(term.astype(BF), "tm", scatter_dimension=0, tiled=True)
        sums.append(lax.psum(share, "stream").astype(F32))
    return sums


def everyone_once(labels, grad, moved):
    _, shape, dtype, _ = moved
    return pl.pallas_call(
        to_send,
        out_shape=[jax.ShapeDtypeStruct(shape, dtype)],
        grid_spec=pltpu.PrefetchScalarGridSpec(
            num_scalar_prefetch=1,
            grid=(1,),
            in_specs=[pl.BlockSpec(grad.shape, lambda i, s: (0, 0, 0, 0))],
            out_specs=[pl.BlockSpec(shape, lambda i, s: (0, 0, 0, 0))],
        ),
        compiler_params=pltpu.CompilerParams(vmem_limit_bytes=VMEM),
    )(labels, grad)


def per_device(
    ranks,
    streams,
    frames,
    space_gain,
    space_input,
    space_output,
    space_scale,
    space_up,
    space_down,
    time_gain,
    time_input,
    time_output,
    time_scale,
    time_up,
    time_down,
    clip_labels,
    output_grad,
):
    packs, _, tokens, width = frames.shape
    slots = clip_labels.shape[1]
    patches = tokens // ranks
    hidden = space_up.shape[1]
    some = packs - 1
    hierarchical = (ranks, streams) == (8, 4)
    tm = lax.axis_index("tm")
    ids = jnp.stack([tm % 2, tm // 2, lax.axis_index("stream")]).astype(jnp.int32)
    shared = Packs(clip_labels, 0, some)
    single = Packs(clip_labels, some, 1)

    def row(vector):
        return vector.reshape(1, -1)

    def exchange(array):
        return lax.all_to_all(array, "tm", split_axis=0, concat_axis=0, tiled=True)

    def steps(count, *tails):
        return [("step", (count,) + tail, BF, None) for tail in tails]

    moved = ("moved", (slots, some, patches, width), BF, None)
    whole = ("pack", frames.shape, F32, None)
    flops = 2 * tokens * width * (4 * width + 2 * hidden)

    (sent,) = everyone_once(clip_labels, output_grad, moved)
    grad_moved = exchange(sent)

    space_args = [
        ("whole", row(space_gain)),
        ("whole", space_input),
        ("whole", space_output),
        ("whole", row(space_scale)),
        ("whole", space_up),
        ("whole", space_down),
    ]
    time_args = [
        ("whole", row(time_gain)),
        ("whole", time_input),
        ("whole", time_output),
        ("whole", row(time_scale)),
        ("whole", time_up),
        ("whole", time_down),
    ]
    rows_w, rows_3, rows_h = (tokens, width), (tokens, 3 * width), (tokens, hidden)
    spread = ("step", (some, tokens, LANES), F32, None)
    x2, sz0, sinv0, sqkv, sp, so, sz1, sinv1, sh, sslope = shared.call(
        space_forward,
        [("pack", frames)] + space_args,
        [moved]
        + steps(some, rows_w)
        + [spread]
        + steps(some, rows_3, (HEADS, tokens, tokens), rows_w, rows_w)
        + [spread]
        + steps(some, rows_h, rows_h),
        scratch=work_shapes(tokens),
        flops=flops,
        after=(sent,),
    )
    x2, grad_moved = lax.optimization_barrier((x2, grad_moved))
    x2_moved = exchange(x2)

    block_tails = [rows_w, rows_w, rows_w, rows_3, rows_w, rows_h, rows_h, rows_w]
    time_tails = [rows_w, rows_w, rows_w, rows_w, rows_w, rows_h, rows_h, rows_w]
    input_grad, result, *alone = single.call(
        alone_both,
        [("pack", frames), ("pack", output_grad)] + space_args + time_args,
        [whole, whole] + steps(1, *block_tails) + steps(1, *time_tails),
        scratch=[
            pltpu.VMEM((tokens, LANES), F32),
            pltpu.VMEM((tokens, LANES), F32),
            pltpu.VMEM(rows_3, BF),
            pltpu.VMEM((HEADS, tokens, tokens), BF),
            pltpu.VMEM(rows_h, BF),
            pltpu.VMEM(rows_h, BF),
            pltpu.VMEM(rows_w, BF),
        ]
        + work_shapes(tokens),
        flops=6 * flops,
        after=(x2,),
    )
    sz0_one, so_one, se1_one, sgqkv_one, sz1_one, seu_one, sh_one, se2_one = alone[:8]
    tz0_one, to_one, te1_one, tgv_one, tz1_one, teu_one, th_one, te2_one = alone[8:]

    g0, out, tz0, tgqkv, to, te1, tz1, teu, th, te2 = shared.call(
        time_both,
        [("moved", x2_moved), ("moved", grad_moved)] + time_args,
        [moved, moved] + steps(some, rows_w, rows_3, rows_w, rows_w, rows_w, rows_h, rows_h, rows_w),
        scratch=[
            pltpu.VMEM(rows_3, BF),
            pltpu.VMEM((HEADS, tokens, tokens), BF),
            pltpu.VMEM(rows_h, BF),
            pltpu.VMEM((tokens, tokens), F32),
        ]
        + work_shapes(tokens),
        flops=3 * flops,
        after=(sz0_one,),
    )
    g0_moved = exchange(g0)
    out, g0_moved = lax.optimization_barrier((out, g0_moved))
    out_moved = exchange(out)

    held_back = ()
    everything = packs * tokens
    feed_shapes = [(1, width // 8), (width // 8, hidden), (hidden // 8, width)]
    attend_shapes = [(1, width // 8), (width // 8, 3 * width), (width // 8, width)]
    time_shared = [tz1, teu, te2, th, tz0, tgqkv, to, te1]
    time_one = [tz1_one, teu_one, te2_one, th_one, tz0_one, tgv_one, to_one, te1_one]
    if hierarchical:
        parts_shapes = [((4, 4, 96, CHUNK), BF)] * 4
        time_terms = manual_call(
            time_weights_kernel,
            ids,
            time_shared + time_one,
            parts_shapes,
            [((everything, a.shape[2]), BF) for a in time_shared] + parts_shapes,
            8 * packs + 20,
            flops=packs * flops,
        )
        time_got = [swap(other, "tm", 8, 1) for other in time_terms[1::2]]
        time_far = far_parts(time_terms[::2], time_got, marker(g0_moved))
        held_back = time_far
    else:
        grad_one = jnp.pad(tgv_one, ((0, 0), (0, 0), (2 * width, 0)))
        joined = [joint(a, b) for a, b in zip(time_shared, time_one[:5] + [grad_one] + time_one[6:])]
        time_grads = plain_grads(joined[0], joined[1], joined[3], joined[2], time_up, time_scale)
        time_grads += plain_grads(joined[4], joined[5], joined[6], joined[7], time_input, time_gain)

    shared_w, shared_3 = (some,) + rows_w, (some,) + rows_3
    space_one = [sz1_one, seu_one, sh_one, se2_one, sz0_one, sgqkv_one, so_one, se1_one]
    whole_shapes = [((everything, a.shape[2]), BF) for a in space_one]
    parts_shapes = [((4, 4, 96, CHUNK), BF)] * 4
    sg1, sgqkv, *weights = manual_call(
        functools.partial(space_kernel, hierarchical),
        ids,
        [row(space_scale), sinv1, g0_moved, sslope, sz1, space_output, space_up, space_down]
        + [sqkv, sp, sh, sz0, so]
        + space_one,
        [(shared_w, F32), (shared_3, BF)]
        + (parts_shapes if hierarchical else [whole_shapes[i] for i in (1, 3, 7)]),
        [
            (g0_moved.shape, BF),
            (sslope.shape, BF),
            (space_output.shape, BF),
            (space_up.shape, BF),
            (space_down.shape, BF),
            (sqkv.shape, BF),
            (sp.shape, BF),
            (shared_w, BF),
            (shared_w, F32),
            ((4, tokens, tokens), BF),
            ((HEADS, tokens, tokens), BF),
        ]
        + whole_shapes
        + (parts_shapes if hierarchical else []),
        80,
        small=2,
        after=held_back,
        flops=2 * packs * flops,
    )
    held_back = ()
    if hierarchical:
        time_got, sgqkv = lax.optimization_barrier((time_got, sgqkv))
        time_mine = time_terms[::2]
        time_halves, time_near = near_parts(time_mine, time_got, time_far)
        mine = weights[::2]
        got = [swap(other, "tm", 8, 1) for other in weights[1::2]]
        far = far_parts(mine, got, marker(time_near[1]))
        far, time_halves = lax.optimization_barrier((far, time_halves))
        held_back = far
    input_grad, result = shared.call(
        space_back_in,
        [
            ("step", sgqkv),
            ("whole", space_input),
            ("whole", row(space_gain)),
            ("step", sz0),
            ("step", sinv0),
            ("step", sg1),
            ("moved", out_moved),
        ],
        [("pack", frames.shape, F32, input_grad), ("pack", frames.shape, F32, result)],
        flops=flops // 4,
        after=held_back,
    )
    if hierarchical:
        time_rows = stream_rows(time_mine, time_got, time_halves, time_near)
        time_final = z_sum(time_rows)
        got, time_final, input_grad = lax.optimization_barrier((got, time_final, input_grad))
        final = z_sum(stream_rows(mine, got, *near_parts(mine, got, far)))
        grads = finish_call(
            finish_kernel,
            ids,
            gather_parts(final),
            [(space_up, space_scale), (space_input, space_gain)],
            feed_shapes + attend_shapes,
        )
        feed_grads, attend_grads = grads[:3], grads[3:]
        time_grads = finish_call(
            finish_kernel,
            ids,
            gather_parts(time_final),
            [(time_up, time_scale), (time_input, time_gain)],
            feed_shapes + attend_shapes,
        )
    else:
        have = some * tokens
        seu, se2, se1 = [a[:have].reshape(some, tokens, -1) for a in weights]
        feed_grads = plain_grads(
            joint(sz1, sz1_one),
            joint(seu, seu_one),
            joint(sh, sh_one),
            joint(se2, se2_one),
            space_up,
            space_scale,
        )
        attend_grads = plain_grads(
            joint(sz0, sz0_one),
            joint(sgqkv, sgqkv_one),
            joint(so, so_one),
            joint(se1, se1_one),
            space_input,
            space_gain,
        )
    grads = attend_grads + feed_grads + time_grads[3:] + time_grads[:3]
    return (result, input_grad, *grads)


def joint(shared, one):
    return jnp.concatenate([shared, one]).reshape(-1, shared.shape[-1])


def solution(mesh):
    tokens = P("stream", "tm", None, None)
    vector, matrix = P("tm"), P("tm", None)
    return jax.shard_map(
        functools.partial(per_device, mesh.shape["tm"], mesh.shape["stream"]),
        mesh=mesh,
        in_specs=(tokens,) + (P(),) * 12 + (P("stream", None), tokens),
        out_specs=(tokens, tokens) + (vector, matrix, matrix, vector, matrix, matrix) * 2,
        check_vma=False,
    )
```

```python
import functools

import jax
import jax.numpy as jnp
from jax import lax
from jax.experimental import pallas as pl
from jax.experimental.pallas import tpu as pltpu
from jax.sharding import PartitionSpec as P

HEADS = 8
EPS = 1e-05
GELU_A = 0.7978845608028654
GELU_B = 0.044715
BF = jnp.bfloat16
F32 = jnp.float32
CHUNK = 512
LANES = 128
COST = 1
ROWS = (0, 96, 64, 80, 160, 176)
VMEM = 60 * 1024 * 1024
SMALL_VMEM = 24 * 1024 * 1024


def nn(a, b):
    return jnp.dot(a, b, preferred_element_type=F32)


def nt(a, b):
    return lax.dot_general(a, b, (((1,), (1,)), ((), ())), preferred_element_type=F32)


def tn(a, b):
    return lax.dot_general(a, b, (((0,), (0,)), ((), ())), preferred_element_type=F32)


def unit(values):
    average = jnp.mean(values, axis=-1, keepdims=True)
    centered = values - average
    inverse = lax.rsqrt(jnp.mean(centered * centered, axis=-1, keepdims=True) + EPS)
    return centered * inverse, inverse


def unit_backward(grad, unit_rows, inverse):
    first = jnp.mean(grad, axis=-1, keepdims=True)
    second = jnp.mean(grad * unit_rows, axis=-1, keepdims=True)
    return inverse * (grad - first - unit_rows * second)


def gelu_parts(u):
    square = u * u
    tangent = jnp.tanh(u * (BF(GELU_A) + BF(GELU_A * GELU_B) * square))
    half = BF(0.5) * u
    value = half + half * tangent
    slope = (BF(0.5) + BF(0.5) * tangent) + half * (BF(1.0) - tangent * tangent) * (
        BF(GELU_A) + BF(3.0 * GELU_A * GELU_B) * square
    )
    return value, slope


def head_masks(width):
    lane = lax.broadcasted_iota(jnp.int32, (1, 2 * width), 1)
    low = lane < width
    return low, (low.astype(F32).astype(BF), (1.0 - low.astype(F32)).astype(BF))


def attend_steps(qkv_ref, p_ref, o_ref, bias_ref, s_ref):
    width = qkv_ref.shape[1] // 3
    size = width // HEADS
    _, masks = head_masks(size)

    def lanes(part, head):
        at = part * width + (head // 2) * 2 * size
        return qkv_ref[:, at : at + 2 * size]

    def score(head):
        s_ref[head % 4] = nt(lanes(1, head) * masks[head % 2], lanes(0, head) * BF(size**-0.5))

    def soften(head):
        scores = s_ref[head % 4]
        if bias_ref is not None:
            scores = scores + bias_ref[...]
        e = jnp.exp(scores - jnp.max(scores, axis=0, keepdims=True))
        p_ref[head] = (e * (1.0 / jnp.sum(e, axis=0, keepdims=True))).astype(BF)

    for head in range(0, HEADS, 2):
        if head == 0:
            score(0)
            score(1)
        if head + 2 < HEADS:
            score(head + 2)
            score(head + 3)
        soften(head)
        soften(head + 1)
        yield
    for head in range(0, HEADS, 2):
        v = lanes(2, head).T
        both = jnp.concatenate([nn(v[:size], p_ref[head]), nn(v[size:], p_ref[head + 1])], axis=0)
        o_ref[:, head * size : (head + 2) * size] = both.T.astype(BF)
        yield


def attend_backward_steps(qkv_ref, p_ref, go_ref, out_ref, gp_ref, gs_ref):
    width = qkv_ref.shape[1] // 3
    size = width // HEADS
    _, masks = head_masks(size)

    def lanes(part, head):
        at = part * width + (head // 2) * 2 * size
        return qkv_ref[:, at : at + 2 * size]

    def gos(head):
        return go_ref[:, (head // 2) * 2 * size : (head // 2 + 1) * 2 * size]

    def put(part, head, value):
        at = part * width + head * size
        out_ref[:, at : at + 2 * size] = value.astype(BF)

    def start(head):
        for h in (head, head + 1):
            gp_ref[h % 4] = nt(lanes(2, h) * masks[h % 2], gos(h)).astype(BF)
        g = gos(head)
        put(2, head, nn(p_ref[head], g * masks[0]) + nn(p_ref[head + 1], g * masks[1]))

    def middle(head):
        p = p_ref[head]
        weighted = p * gp_ref[head % 4]
        total = jnp.sum(weighted.astype(F32), axis=0, keepdims=True).astype(BF)
        gs_ref[head] = weighted - p * total

    def finish(head):
        q = lanes(0, head) * BF(size**-0.5)
        k = (lanes(1, head) * BF(size**-0.5)).T
        put(1, head, nn(gs_ref[head], q * masks[0]) + nn(gs_ref[head + 1], q * masks[1]))
        both = jnp.concatenate([nn(k[:size], gs_ref[head]), nn(k[size:], gs_ref[head + 1])], axis=0)
        put(0, head, both.T)

    start(0)
    yield
    for head in range(0, HEADS, 2):
        middle(head)
        middle(head + 1)
        if head + 2 < HEADS:
            start(head + 2)
        if head > 0:
            finish(head - 2)
        yield
    finish(HEADS - 2)


def feed_up_steps(m, up_ref, down_ref, h_ref, slope_ref, u_ref):
    steps = up_ref.shape[1] // CHUNK

    def before(step):
        u_ref[step % 2] = nn(m, up_ref[:, step * CHUNK : (step + 1) * CHUNK]).astype(BF)

    before(0)
    for step in range(steps):
        if step + 1 < steps:
            before(step + 1)
        at = step * CHUNK
        h_ref[:, at : at + CHUNK], slope_ref[:, at : at + CHUNK] = gelu_parts(u_ref[step % 2])
        yield
    return nn(h_ref[...], down_ref[...])


def feed_back_steps(e2, up_ref, down_ref, slope_ref, eu_ref, up_copy=None):
    for at in range(0, up_ref.shape[1], CHUNK):
        gh = nt(e2, down_ref[at : at + CHUNK, :]).astype(BF)
        eu_ref[:, at : at + CHUNK] = gh * slope_ref[:, at : at + CHUNK]
        yield
    if up_copy is not None:
        wait(up_copy)
    return nt(eu_ref[...], up_ref[...])


def whole(steps):
    while True:
        try:
            next(steps)
        except StopIteration as end:
            return end.value


def together(runs):
    while runs:
        runs = [run for run in runs if next(run, "end") != "end"]


def attend(*args):
    whole(attend_steps(*args))


def attend_backward(*args):
    whole(attend_backward_steps(*args))


def feed_up(*args):
    return whole(feed_up_steps(*args))


def feed_back(*args):
    return whole(feed_back_steps(*args))


def rows_of(block):
    slots, _, patches, width = block.shape
    return block[:, 0].astype(F32).reshape(slots * patches, width)


def block_of(rows, ref):
    slots, _, patches, width = ref.shape
    ref[:, 0] = rows.reshape(slots, patches, width).astype(ref.dtype)


def work_shapes(tokens):
    return [
        pltpu.VMEM((4, tokens, tokens), F32),
        pltpu.VMEM((2, tokens, CHUNK), BF),
        pltpu.VMEM((4, tokens, tokens), BF),
        pltpu.VMEM((HEADS, tokens, tokens), BF),
    ]


def wide(column):
    return jnp.broadcast_to(column, (column.shape[0], LANES))


def space_rows(x, weights, state, work):
    gain, w_in, w_out, scale, w_up, w_down = weights
    z0, inv0, qkv, p, o, z1, inv1, h, slope = state
    unit0, inverse0 = unit(x)
    z0[...] = unit0.astype(BF)
    inv0[...] = wide(inverse0)
    qkv[...] = nn((unit0 * gain[...]).astype(BF), w_in[...]).astype(BF)
    attend(qkv, p, o, None, work[0])
    r1 = x + nn(o[...], w_out[...])
    unit1, inverse1 = unit(r1)
    z1[...] = unit1.astype(BF)
    inv1[...] = wide(inverse1)
    m = (unit1 * scale[...]).astype(BF)
    return r1 + feed_up(m, w_up, w_down, h, slope, work[1])


def space_forward(labels, frames, *rest):
    weights, x2, state, work = rest[:6], rest[6], rest[7:16], rest[16:]
    rows = space_rows(frames[0, 0].astype(F32), weights, [ref.at[0] for ref in state], work)
    block_of(rows, x2)


def build_bias(labels, pack, slots, patches, bias):
    tokens = slots * patches
    row = lax.broadcasted_iota(jnp.int32, (1, tokens), 1)
    column = lax.broadcasted_iota(jnp.int32, (tokens, 1), 0)

    def label_of(position):
        slot = position // patches
        value = jnp.zeros_like(position)
        for f in range(slots):
            value = jnp.where(slot == f, labels[pack, f], value)
        return value

    same_patch = (row % patches) == (column % patches)
    allowed = same_patch & (column <= row) & (label_of(column) == label_of(row))
    bias[...] = jnp.where(allowed, 0.0, -1e30)


def time_kernel(labels, gain, scale, x2_in, grad_in, w_in_in, w_out_in, w_up_in, w_down_in, *rest):
    outs, rest = rest[:10], rest[10:]
    x2, grad, w_in, w_out, w_up, w_down = rest[:6]
    held = rest[6:16]
    g0, out, z0, gqkv, o, e1, z1, eu, h, e2 = held
    qkv, p, slope, bias, go, scores, u, gp, gs = rest[16:25]
    copies = Copies(rest[-1])
    slots, packs, patches, _ = x2.shape
    got_x2, got_in = copies.fetch(x2_in, x2), copies.fetch(w_in_in, w_in)
    got_out, got_up = copies.fetch(w_out_in, w_out), copies.fetch(w_up_in, w_up)
    got_down, got_grad = copies.fetch(w_down_in, w_down), copies.fetch(grad_in, grad)

    def send(index, pack):
        copies.send(held[index].at[pack], outs[index].at[pack])

    def run(pack):
        if pack == 0:
            wait(got_x2)
        build_bias(labels, pack_at(labels, pack), slots, patches, bias.at[pack])
        x = rows_of(x2[:, pack : pack + 1])
        unit0, inverse0 = unit(x)
        z0[pack] = unit0.astype(BF)
        send(2, pack)
        if pack == 0:
            wait(got_in)
        qkv[pack] = nn((unit0 * gain[...]).astype(BF), w_in[...]).astype(BF)
        yield
        yield from attend_steps(qkv.at[pack], p.at[pack], o.at[pack], bias.at[pack], scores.at[pack])
        send(4, pack)
        if pack == 0:
            wait(got_out)
        r1 = x + nn(o[pack], w_out[...])
        unit1, inverse1 = unit(r1)
        z1[pack] = unit1.astype(BF)
        send(6, pack)
        m = (unit1 * scale[...]).astype(BF)
        yield
        if pack == 0:
            wait(got_up, got_down)
        total = yield from feed_up_steps(m, w_up, w_down, h.at[pack], slope.at[pack], u.at[pack])
        send(8, pack)
        block_of(r1 + total, out.at[:, pl.ds(pack, 1)])
        if pack == 0:
            wait(got_grad)
        g2 = rows_of(grad[:, pack : pack + 1])
        e2[pack] = g2.astype(BF)
        send(9, pack)
        yield
        gm = yield from feed_back_steps(e2[pack], w_up, w_down, slope.at[pack], eu.at[pack])
        send(7, pack)
        g1 = g2 + unit_backward(gm * scale[...], unit1, inverse1)
        e1[pack] = g1.astype(BF)
        send(5, pack)
        go[pack] = nt(e1[pack], w_out[...]).astype(BF)
        yield
        yield from attend_backward_steps(
            qkv.at[pack], p.at[pack], go.at[pack], gqkv.at[pack], gp.at[pack], gs.at[pack]
        )
        send(3, pack)
        gn = nt(gqkv[pack], w_in[...])
        block_of(g1 + unit_backward(gn * gain[...], unit0, inverse0), g0.at[:, pl.ds(pack, 1)])

    together([run(pack) for pack in range(packs)])
    copies.send(g0, outs[0])
    copies.send(out, outs[1])
    copies.finish()


def alone_both(labels, frames, grad, *rest):
    space, (gain, w_in, w_out, scale, w_up, w_down) = rest[:6], rest[6:12]
    input_grad, out = rest[12:14]
    sz0, so, se1, sgqkv, sz1, seu, sh, se2 = [ref.at[0] for ref in rest[14:22]]
    z0, o, e1, gv, z1, eu, h, e2 = [ref.at[0] for ref in rest[22:30]]
    inv0, inv1, qkv, p, sslope, slope, go, *work = rest[30:]
    state = sz0, inv0, qkv, p, so, sz1, inv1, sh, sslope
    x = space_rows(frames[0, 0].astype(F32), space, state, work)
    width = x.shape[1]
    unit0, inverse0 = unit(x)
    z0[...] = unit0.astype(BF)
    o[...] = nn((unit0 * gain[...]).astype(BF), w_in[:, 2 * width :]).astype(BF)
    r1 = x + nn(o[...], w_out[...])
    unit1, inverse1 = unit(r1)
    z1[...] = unit1.astype(BF)
    m = (unit1 * scale[...]).astype(BF)
    out[0, 0] = r1 + feed_up(m, w_up, w_down, h, slope, work[1])
    e2[...] = grad[0, 0]
    g2 = grad[0, 0].astype(F32)
    gm = feed_back(e2[...], w_up, w_down, slope, eu)
    g1 = g2 + unit_backward(gm * scale[...], unit1, inverse1)
    e1[...] = g1.astype(BF)
    gv[...] = nt(e1[...], w_out[...]).astype(BF)
    gn = nt(gv[...], w_in[:, 2 * width :])
    g2 = g1 + unit_backward(gn * gain[...], unit0, inverse0)
    gain, w_in, w_out, scale, w_up, w_down = space
    se2[...] = g2.astype(BF)
    gm = feed_back(se2[...], w_up, w_down, sslope, seu)
    g1 = g2 + unit_backward(gm * scale[...], sz1[...].astype(F32), inv1[:, :1])
    se1[...] = g1.astype(BF)
    go[...] = nt(se1[...], w_out[...]).astype(BF)
    attend_backward(qkv, p, go, sgqkv, work[2], work[3])
    gn = nt(sgqkv[...], w_in[...])
    input_grad[0, 0] = g1 + unit_backward(gn * gain[...], sz0[...].astype(F32), inv0[:, :1])


def space_back_in(labels, gqkv, w_in, gain, z0, inv0, g1, moved, input_grad, result):
    gn = nt(gqkv[0], w_in[...])
    grad = unit_backward(gn * gain[...], z0[0].astype(F32), inv0[0, :, :1])
    input_grad[0, 0] = g1[0] + grad
    result[0, 0] = rows_of(moved[...])


class Copies:
    def __init__(self, semaphores):
        self.semaphores, self.count, self.sent = semaphores, 0, []

    def fetch(self, source, target):
        copy = pltpu.make_async_copy(source, target, self.semaphores.at[self.count])
        self.count += 1
        copy.start()
        return copy

    def send(self, source, target):
        self.sent.append(self.fetch(source, target))

    def finish(self):
        for copy in self.sent:
            copy.wait()


def wait(*copies):
    for copy in copies:
        copy.wait()


def space_kernel(hierarchical, ids, scale, inv1, *rest):
    (g2_in, slope_in, z1_in, w_out_in, w_up_in, w_down_in, qkv_in, p_in), rest = rest[:8], rest[8:]
    shared, one, rest = rest[:3], rest[3:11], rest[11:]
    (g1_out, gqkv_out), outs, scratch = rest[:2], rest[2 : 6 if hierarchical else 5], rest[6 if hierarchical else 5 :]
    g2, slope, w_out, w_up, w_down, qkv, p, go, g1, gp, gs = scratch[:11]
    z1, eu, h, e2, z0, gqkv, o, e1 = whole = scratch[11:19]
    copies = Copies(scratch[-1])
    packs, tokens, _ = g1.shape
    have = packs * tokens
    got_g2 = copies.fetch(g2_in, g2)
    got_down = copies.fetch(w_down_in, w_down)
    got_slope = [copies.fetch(slope_in.at[pack], slope.at[pack]) for pack in range(packs)]
    got_up = copies.fetch(w_up_in, w_up)
    got_z1 = [
        copies.fetch(z1_in.at[pack], z1.at[pl.ds(pack * tokens, tokens)]) for pack in range(packs)
    ]
    got_out = copies.fetch(w_out_in, w_out)
    got_attend = [
        (copies.fetch(qkv_in.at[pack], qkv.at[pack]), copies.fetch(p_in.at[pack], p.at[pack]))
        for pack in range(packs)
    ]
    got_rest = []
    if hierarchical:
        for source, target in zip(shared, (h, z0, o)):
            for pack in range(packs):
                rows = pl.ds(pack * tokens, tokens)
                got_rest.append(copies.fetch(source.at[pack], target.at[rows]))
        for source, target in zip(one, whole):
            got_rest.append(copies.fetch(source.at[0], target.at[pl.ds(have, tokens)]))
    wait(got_g2)

    def run(pack):
        rows = slice(pack * tokens, (pack + 1) * tokens)
        e2[rows] = rows_of(g2[:, pack : pack + 1]).astype(BF)
        if pack == 0:
            wait(got_down)
        wait(got_slope[pack])
        gm = yield from feed_back_steps(e2[rows], w_up, w_down, slope.at[pack], eu.at[rows], got_up if pack == 0 else None)
        if pack == 0:
            wait(*got_z1, got_out)
        grad = unit_backward(gm * scale[...], z1[rows].astype(F32), inv1[pack, :, :1])
        total = rows_of(g2[:, pack : pack + 1]) + grad
        g1[pack] = total
        e1[rows] = total.astype(BF)
        go[pack] = nt(e1[rows], w_out[...]).astype(BF)
        copies.send(g1.at[pack], g1_out.at[pack])
        yield
        wait(*got_attend[pack])
        rows = pl.ds(pack * tokens, tokens)
        yield from attend_backward_steps(
            qkv.at[pack], p.at[pack], go.at[pack], gqkv.at[rows], gp.at[pack], gs.at[pack]
        )
        copies.send(gqkv.at[rows], gqkv_out.at[pack])

    together([run(pack) for pack in range(packs)])
    if hierarchical:
        wait(*got_rest)
        one = Halves(copies, ids, scratch[19:21], outs[:2], x_high=True)
        two = Halves(copies, ids, scratch[21:23], outs[2:])
        up_tiles(one, z1, eu, 0)
        down_tiles(two, e2, h, 0)
        attend_tiles([one, one, two, two], z0, o, gqkv, e1, [64, 80, 64, 80], gqkv.shape[0])
    else:
        for source, target in zip((eu, e2, e1), outs):
            copies.send(source, target)
    copies.finish()


def to_send(labels, grad, out):
    for place in range(out.shape[1]):
        rows = grad[pack_at(labels, place), 0].astype(F32)
        out[:, place] = rows.reshape(out.shape[0], out.shape[2], out.shape[3]).astype(BF)


def pack_at(labels, place):
    packs, slots = labels.shape
    alone = packs - 1
    for pack in range(packs - 2, -1, -1):
        alone = jnp.where(labels[pack, slots - 1] == slots - 1, pack, alone)
    return jnp.where(place == packs - 1, alone, place + (place >= alone).astype(jnp.int32))


def without(kernel, first, count):
    def call(*refs):
        return kernel(*refs[:first], *refs[first + count :])

    return call


class Packs:
    def __init__(self, labels, first, count):
        self.labels, self.first, self.count = labels, first, count

    def call(self, kernel, args, outs, scratch=(), flops=0, after=()):
        first, last = self.first, self.labels.shape[0] - 2
        scalars = (self.labels,)

        def spec(kind, shape):
            rank = len(shape)
            if kind == "whole":
                return pl.BlockSpec(shape, lambda i, *s: (0,) * rank)
            if kind == "pack":
                return pl.BlockSpec(
                    (1,) + tuple(shape[1:]), lambda i, s: (pack_at(s, first + i),) + (0,) * (rank - 1)
                )
            if kind == "place":
                return pl.BlockSpec(
                    (1,) + tuple(shape[1:]), lambda i, *s: (first + i,) + (0,) * (rank - 1)
                )
            if kind == "step":
                return pl.BlockSpec(
                    (1,) + tuple(shape[1:]), lambda i, *s: (i,) + (0,) * (rank - 1)
                )
            if kind == "moved":
                return pl.BlockSpec(
                    (shape[0], 1, shape[2], shape[3]),
                    lambda i, *s: (0, jnp.minimum(i, last), 0, 0),
                )
            return pl.BlockSpec(memory_space=pl.ANY)

        in_specs = [spec(kind, array.shape) for kind, array in args]
        operands = [array for _, array in args]
        aliases = {}
        for index, (kind, shape, dtype, into) in enumerate(outs):
            if into is not None:
                aliases[len(scalars) + len(operands)] = index
                operands.append(into)
                in_specs.append(pl.BlockSpec(memory_space=pl.ANY))
        for array in after:
            operands.append(array)
            in_specs.append(pl.BlockSpec(memory_space=pl.ANY))
        moved = sum(a.size * a.dtype.itemsize for a in operands)
        unread = len(operands) - len(args)
        return pl.pallas_call(
            without(kernel, len(scalars) + len(args), unread),
            out_shape=[jax.ShapeDtypeStruct(shape, dtype) for _, shape, dtype, _ in outs],
            grid_spec=pltpu.PrefetchScalarGridSpec(
                num_scalar_prefetch=len(scalars),
                grid=(self.count,),
                in_specs=in_specs,
                out_specs=[spec(kind, shape) for kind, shape, _, _ in outs],
                scratch_shapes=list(scratch),
            ),
            input_output_aliases=aliases,
            compiler_params=pltpu.CompilerParams(
                vmem_limit_bytes=VMEM, dimension_semantics=("arbitrary",)
            ),
            cost_estimate=pl.CostEstimate(
                flops=int(flops * self.count * COST), bytes_accessed=int(moved * COST), transcendentals=0
            ),
        )(*scalars, *operands)


class Halves:
    def __init__(self, copies, ids, held, outs, x_high=False):
        self.copies, self.held, self.outs = copies, held, outs
        self.first, self.z, self.s, self.x_high = ids[0] == 0, ids[1], ids[2], x_high

    def part(self, s):
        if s is None:
            return slice(None)
        part = s ^ self.s
        return (part & 1) * 2 + (part >> 1) if self.x_high else part

    def put(self, s, z, at, even, odd):
        rows = slice(at, at + even.shape[0])
        self.held[0][self.part(s), z ^ self.z, rows] = jnp.where(self.first, even, odd)
        self.held[1][self.part(s), z ^ self.z, rows] = jnp.where(self.first, odd, even)

    def send(self, s, z, at, rows):
        index = self.part(s), slice(None) if z is None else z ^ self.z, pl.ds(at, rows)
        for ref, out in zip(self.held, self.outs):
            self.copies.send(ref.at[index], out.at[index])


def up_tiles(place, z1, eu, at):
    for step in range(4):
        tile = tn(z1[...], eu[:, step * CHUNK : (step + 1) * CHUNK]).astype(BF)
        for z in range(4):
            row = 128 * z
            place.put(step, z, at, tile[row : row + 64], tile[row + 64 : row + 128])
        place.send(step, None, at, 64)


def down_tiles(place, e2, h, at):
    for step in range(4):
        tile = tn(e2[...], h[:, step * CHUNK : (step + 1) * CHUNK]).astype(BF)
        for s in range(4):
            upper, lower = tile[128 * s : 128 * s + 64], tile[128 * s + 64 : 128 * s + 128]
            even = jnp.concatenate([upper[:, :256], lower[:, :256]], axis=1)
            odd = jnp.concatenate([upper[:, 256:], lower[:, 256:]], axis=1)
            place.put(s, step, at, even, odd)
        place.send(None, step, at, 64)


def attend_tiles(places, z0, o, gqkv, e1, ats, depth):
    for step, (place, at) in enumerate(zip(places, ats)):
        if step == 3:
            tile = tn(o[...], e1[...])
        else:
            rows = gqkv.shape[0] if step == 2 else depth
            tile = tn(z0[:rows], gqkv[:rows, step * CHUNK : (step + 1) * CHUNK])
        tile = tile.astype(BF)
        for z in range(4):
            for s in range(4):
                row = 128 * z + 16 * s
                place.put(s, z, at, tile[row : row + 16], tile[row + 64 : row + 80])
        if step % 2:
            place.send(None, None, at - 16, 32)


def time_weights_kernel(ids, *rest):
    names = 8
    shared, single, outs, scratch = rest[:names], rest[names : 2 * names], rest[16:20], rest[20:]
    z1, eu, e2, h, z0, gqkv, o, e1 = scratch[:names]
    copies = Copies(scratch[-1])
    one = Halves(copies, ids, scratch[8:10], outs[:2], x_high=True)
    two = Halves(copies, ids, scratch[10:12], outs[2:])
    packs, tokens, _ = shared[0].shape
    have = packs * tokens
    got = []
    for source, last, target in zip(shared, single, scratch):
        wide_target = target.at[pl.ds(have, tokens)]
        if last.shape[2] < target.shape[1]:
            wide_target = target.at[pl.ds(have, tokens), pl.ds(target.shape[1] - last.shape[2], last.shape[2])]
        got.append(
            [copies.fetch(source.at[pack], target.at[pl.ds(pack * tokens, tokens)]) for pack in range(packs)]
            + [copies.fetch(last.at[0], wide_target)]
        )
    wait(*got[0], *got[1], *got[2], *got[3])
    up_tiles(one, z1, eu, 0)
    down_tiles(two, e2, h, 0)
    wait(*got[4], *got[5], *got[6], *got[7])
    attend_tiles([one, one, two, two], z0, o, gqkv, e1, [64, 80, 64, 80], have)
    copies.finish()


def manual_call(kernel, ids, args, outs, scratch, semaphores, small=0, after=(), flops=0):
    anywhere = pl.BlockSpec(memory_space=pl.ANY)
    return pl.pallas_call(
        without(kernel, 1 + len(args), len(after)),
        out_shape=[jax.ShapeDtypeStruct(shape, dtype) for shape, dtype in outs],
        in_specs=[pl.BlockSpec(memory_space=pltpu.SMEM)]
        + [pl.BlockSpec(memory_space=pltpu.VMEM)] * small
        + [anywhere] * (len(args) - small + len(after)),
        out_specs=[anywhere] * len(outs),
        scratch_shapes=[pltpu.VMEM(shape, dtype) for shape, dtype in scratch]
        + [pltpu.SemaphoreType.DMA((semaphores,))],
        compiler_params=pltpu.CompilerParams(vmem_limit_bytes=VMEM),
        cost_estimate=pl.CostEstimate(
            flops=int(flops * COST), bytes_accessed=0, transcendentals=0
        ),
    )(ids, *args, *after)


def swap(array, axis, size, mask):
    return lax.ppermute(array, axis, [(i, i ^ mask) for i in range(size)])


def add(*terms):
    total = terms[0].astype(F32)
    for term in terms[1:]:
        total = total + term.astype(F32)
    return total.astype(BF)


def far_parts(mine, got, note):
    return [add(a[2:], b[2:], note) for a, b in zip(mine, got)]


def near_parts(mine, got, far):
    halves = [swap(far[0], "stream", 4, 1), swap(far[1], "stream", 4, 2)]
    return halves, [add(a[1], b[1], half[1]) for a, b, half in zip(mine, got, halves)]


def stream_rows(mine, got, halves, near):
    last = [swap(near[0], "stream", 4, 2), swap(near[1], "stream", 4, 1)]
    terms = list(zip(mine, got, halves, last))
    return [
        jnp.concatenate([add(a[0][d], b[0][d], half[0][d], end[d]) for a, b, half, end in terms])
        for d in range(4)
    ]


def z_sum(rows):
    return add(rows[0], *[swap(rows[d], "tm", 8, 2 * d) for d in range(1, 4)])


def gather_parts(final):
    return [final] + [swap(final, "stream", 4, d) for d in range(1, 4)]


def marker(array):
    def kernel(source, out):
        out[...] = jnp.zeros_like(out)

    return pl.pallas_call(
        kernel,
        out_shape=jax.ShapeDtypeStruct((1, CHUNK), F32),
        in_specs=[pl.BlockSpec(memory_space=pl.ANY)],
        out_specs=pl.BlockSpec(memory_space=pltpu.VMEM),
        cost_estimate=pl.CostEstimate(flops=10**12, bytes_accessed=10**8, transcendentals=0),
    )(array)


def stream_total(parts, own):
    return add(*own, *[swap(part, "stream", 4, d + 1) for d, part in enumerate(parts)])


def stream_total(parts, own):
    return add(*own, *[swap(part, "stream", 4, d + 1) for d, part in enumerate(parts)])


def stream_sum(parts, own):
    got = [swap(part, "stream", 4, d + 1) for d, part in enumerate(parts)]
    return [add(*[term[d] for term in (*own, *got)]) for d in range(4)]


def halved_sum(mine, got, far, first, second):
    half = swap(far, "stream", 4, first)
    near = swap(add(mine[1], got[1], half[1]), "stream", 4, second)
    return [(mine[0][d], got[0][d], half[0][d], near[d]) for d in range(4)]


def z_sum(rows):
    return add(rows[0], *[swap(rows[d], "tm", 8, 2 * d) for d in range(1, 4)])


def gather_parts(final):
    return [final] + [swap(final, "stream", 4, d) for d in range(1, 4)]


def marker(array):
    def kernel(source, out):
        out[...] = jnp.zeros_like(out)

    return pl.pallas_call(
        kernel,
        out_shape=jax.ShapeDtypeStruct((1, CHUNK), F32),
        in_specs=[pl.BlockSpec(memory_space=pl.ANY)],
        out_specs=pl.BlockSpec(memory_space=pltpu.VMEM),
        cost_estimate=pl.CostEstimate(flops=10**12, bytes_accessed=10**8, transcendentals=0),
    )(array)


def add_call(mine, got, after):
    def kernel(a, b, out):
        out[...] = (a[...].astype(F32) + b[...].astype(F32)).astype(BF)

    block = pl.BlockSpec((1,) + mine.shape[1:], lambda i: (i,) + (0,) * (mine.ndim - 1))
    return pl.pallas_call(
        without(kernel, 2, len(after)),
        out_shape=jax.ShapeDtypeStruct(mine.shape, BF),
        grid=(mine.shape[0],),
        in_specs=[block, block] + [pl.BlockSpec(memory_space=pl.ANY)] * len(after),
        out_specs=block,
        compiler_params=pltpu.CompilerParams(vmem_limit_bytes=VMEM),
    )(mine, got, *after)


def scatter_sum(total):
    share = lax.psum_scatter(total, "stream", scatter_dimension=0)
    groups = [[0, 2, 4, 6], [1, 3, 5, 7]]
    return lax.psum_scatter(share, "tm", scatter_dimension=0, axis_index_groups=groups)


def as_row(col):
    size = col.shape[0]
    eye = lax.broadcasted_iota(jnp.int32, (size, size), 0) == lax.broadcasted_iota(
        jnp.int32, (size, size), 1
    )
    return jnp.sum(jnp.where(eye, col, 0.0), axis=0, keepdims=True)


def own_rows(ids, vector):
    shape = 64, vector.shape[1]
    row = lax.broadcasted_iota(jnp.int32, shape, 0) + 64 * (2 * ids[1] + ids[0])
    lane = lax.broadcasted_iota(jnp.int32, shape, 1)
    return jnp.sum(jnp.where(row == lane, vector[...], 0.0), axis=1, keepdims=True)


def finish_kernel(ids, p0, p1, p2, p3, w_up, scale, w_in, gain, *outs):
    scale_grad, up_grad, down_grad, gain_grad, in_grad, out_grad = outs
    up_at, down_at, *in_at, out_at = ROWS
    for d, piece in enumerate((p0, p1, p2, p3)):
        s = ids[2] ^ d
        up_grad[:, pl.ds(pl.multiple_of(512 * s, 512), 512)] = piece[up_at : up_at + 64].astype(F32)
        lower = piece[down_at : down_at + 64].astype(F32)
        whole = jnp.concatenate([lower[:, :256], lower[:, 256:]], axis=0)
        down_grad[:, pl.ds(pl.multiple_of(128 * s, 128), 128)] = whole.T
        rows = pl.ds(pl.multiple_of(16 * s, 16), 16)
        for third, at in enumerate(in_at):
            in_grad[rows, 512 * third : 512 * third + 512] = piece[at : at + 16].astype(F32)
        out_grad[rows, :] = piece[out_at : out_at + 16].astype(F32)
    for grad, weight, factor, vector_grad in (
        (up_grad, w_up, scale, scale_grad),
        (in_grad, w_in, gain, gain_grad),
    ):
        total = grad[...]
        vector_grad[...] = as_row(jnp.sum(total * weight[...].astype(F32), axis=1, keepdims=True))
        grad[...] = total * own_rows(ids, factor)


def finish_call(kernel, ids, pieces, pairs, outs):
    whole = pl.BlockSpec(pieces[0].shape, lambda i, *s: (0, 0))
    specs, operands = [], []
    for weight, vector in pairs:
        height = weight.shape[0] // 8
        specs += [
            pl.BlockSpec((height, weight.shape[1]), lambda i, s: (2 * s[1] + s[0], 0)),
            pl.BlockSpec((1, vector.size), lambda i, *s: (0, 0)),
        ]
        operands += [weight, vector.reshape(1, -1)]
    results = pl.pallas_call(
        kernel,
        out_shape=[jax.ShapeDtypeStruct(shape, F32) for shape in outs],
        grid_spec=pltpu.PrefetchScalarGridSpec(
            num_scalar_prefetch=1,
            grid=(1,),
            in_specs=[whole] * 4 + specs,
            out_specs=[pl.BlockSpec(shape, lambda i, *s: (0, 0)) for shape in outs],
        ),
        compiler_params=pltpu.CompilerParams(vmem_limit_bytes=SMALL_VMEM),
    )(ids, *pieces, *operands)
    return [a.reshape(-1) if a.shape[0] == 1 else a for a in results]


def plain_grads(z, grads, left, right, weight, vector):
    product = tn(z, grads)
    vector_grad = jnp.sum(product * weight.astype(F32), axis=1)
    sums = []
    for term in (vector_grad, product * vector[:, None], tn(left, right)):
        share = lax.psum_scatter(term.astype(BF), "tm", scatter_dimension=0, tiled=True)
        sums.append(lax.psum(share, "stream").astype(F32))
    return sums


def everyone_once(labels, grad, moved):
    _, shape, dtype, _ = moved
    return pl.pallas_call(
        to_send,
        out_shape=[jax.ShapeDtypeStruct(shape, dtype)],
        grid_spec=pltpu.PrefetchScalarGridSpec(
            num_scalar_prefetch=1,
            grid=(1,),
            in_specs=[pl.BlockSpec(grad.shape, lambda i, s: (0, 0, 0, 0))],
            out_specs=[pl.BlockSpec(shape, lambda i, s: (0, 0, 0, 0))],
        ),
        compiler_params=pltpu.CompilerParams(vmem_limit_bytes=VMEM),
    )(labels, grad)


def per_device(
    ranks,
    streams,
    frames,
    space_gain,
    space_input,
    space_output,
    space_scale,
    space_up,
    space_down,
    time_gain,
    time_input,
    time_output,
    time_scale,
    time_up,
    time_down,
    clip_labels,
    output_grad,
):
    packs, _, tokens, width = frames.shape
    slots = clip_labels.shape[1]
    patches = tokens // ranks
    hidden = space_up.shape[1]
    some = packs - 1
    hierarchical = (ranks, streams) == (8, 4)
    tm = lax.axis_index("tm")
    ids = jnp.stack([tm % 2, tm // 2, lax.axis_index("stream")]).astype(jnp.int32)
    shared = Packs(clip_labels, 0, some)
    single = Packs(clip_labels, some, 1)

    def row(vector):
        return vector.reshape(1, -1)

    def exchange(array):
        return lax.all_to_all(array, "tm", split_axis=0, concat_axis=0, tiled=True)

    def steps(count, *tails):
        return [("step", (count,) + tail, BF, None) for tail in tails]

    moved = ("moved", (slots, some, patches, width), BF, None)
    whole = ("pack", frames.shape, F32, None)
    flops = 2 * tokens * width * (4 * width + 2 * hidden)

    (sent,) = everyone_once(clip_labels, output_grad, moved)
    grad_moved = exchange(sent)

    space_args = [
        ("whole", row(space_gain)),
        ("whole", space_input),
        ("whole", space_output),
        ("whole", row(space_scale)),
        ("whole", space_up),
        ("whole", space_down),
    ]
    time_args = [
        ("whole", row(time_gain)),
        ("whole", time_input),
        ("whole", time_output),
        ("whole", row(time_scale)),
        ("whole", time_up),
        ("whole", time_down),
    ]
    rows_w, rows_3, rows_h = (tokens, width), (tokens, 3 * width), (tokens, hidden)
    spread = ("step", (some, tokens, LANES), F32, None)
    x2, sz0, sinv0, sqkv, sp, so, sz1, sinv1, sh, sslope = shared.call(
        space_forward,
        [("pack", frames)] + space_args,
        [moved]
        + steps(some, rows_w)
        + [spread]
        + steps(some, rows_3, (HEADS, tokens, tokens), rows_w, rows_w)
        + [spread]
        + steps(some, rows_h, rows_h),
        scratch=work_shapes(tokens),
        flops=flops,
        after=(sent,),
    )
    x2, grad_moved = lax.optimization_barrier((x2, grad_moved))
    x2_moved = exchange(x2)

    block_tails = [rows_w, rows_w, rows_w, rows_3, rows_w, rows_h, rows_h, rows_w]
    time_tails = [rows_w, rows_w, rows_w, rows_w, rows_w, rows_h, rows_h, rows_w]
    input_grad, result, *alone = single.call(
        alone_both,
        [("pack", frames), ("pack", output_grad)] + space_args + time_args,
        [whole, whole] + steps(1, *block_tails) + steps(1, *time_tails),
        scratch=[
            pltpu.VMEM((tokens, LANES), F32),
            pltpu.VMEM((tokens, LANES), F32),
            pltpu.VMEM(rows_3, BF),
            pltpu.VMEM((HEADS, tokens, tokens), BF),
            pltpu.VMEM(rows_h, BF),
            pltpu.VMEM(rows_h, BF),
            pltpu.VMEM(rows_w, BF),
        ]
        + work_shapes(tokens),
        flops=6 * flops,
        after=(x2,),
    )
    sz0_one, so_one, se1_one, sgqkv_one, sz1_one, seu_one, sh_one, se2_one = alone[:8]
    tz0_one, to_one, te1_one, tgv_one, tz1_one, teu_one, th_one, te2_one = alone[8:]

    shared_w, shared_3, shared_h = [(some,) + tail for tail in (rows_w, rows_3, rows_h)]
    time_outs = [(x2.shape, BF)] * 2 + [
        (shape, BF)
        for shape in (shared_w, shared_3, shared_w, shared_w, shared_w, shared_h, shared_h, shared_w)
    ]
    square = (some, HEADS, tokens, tokens)
    g0, out, tz0, tgqkv, to, te1, tz1, teu, th, te2 = manual_call(
        time_kernel,
        clip_labels,
        [row(time_gain), row(time_scale), x2_moved, grad_moved]
        + [time_input, time_output, time_up, time_down],
        time_outs,
        [(x2.shape, BF)] * 2
        + [(w.shape, BF) for w in (time_input, time_output, time_up, time_down)]
        + time_outs
        + [
            (shared_3, BF),
            (square, BF),
            (shared_h, BF),
            ((some, tokens, tokens), F32),
            (shared_w, BF),
            ((some, 4, tokens, tokens), F32),
            ((some, 2, tokens, CHUNK), BF),
            ((some, 4, tokens, tokens), BF),
            (square, BF),
        ],
        6 + 8 * some + 2,
        small=2,
        after=(sz0_one,),
        flops=3 * some * flops,
    )
    g0_moved = exchange(g0)
    out, g0_moved = lax.optimization_barrier((out, g0_moved))
    out_moved = exchange(out)

    held_back = ()
    everything = packs * tokens
    feed_shapes = [(1, width // 8), (width // 8, hidden), (hidden // 8, width)]
    attend_shapes = [(1, width // 8), (width // 8, 3 * width), (width // 8, width)]
    time_shared = [tz1, teu, te2, th, tz0, tgqkv, to, te1]
    time_one = [tz1_one, teu_one, te2_one, th_one, tz0_one, tgv_one, to_one, te1_one]
    if hierarchical:
        parts_shapes = [((4, 4, 96, CHUNK), BF)] * 4
        time_terms = manual_call(
            time_weights_kernel,
            ids,
            time_shared + time_one,
            parts_shapes,
            [((everything, a.shape[2]), BF) for a in time_shared] + parts_shapes,
            8 * packs + 20,
            flops=packs * flops,
        )
        time_got = [swap(other, "tm", 8, 1) for other in time_terms[1::2]]
        time_far = far_parts(time_terms[::2], time_got, marker(g0_moved))
        held_back = time_far
    else:
        grad_one = jnp.pad(tgv_one, ((0, 0), (0, 0), (2 * width, 0)))
        joined = [joint(a, b) for a, b in zip(time_shared, time_one[:5] + [grad_one] + time_one[6:])]
        time_grads = plain_grads(joined[0], joined[1], joined[3], joined[2], time_up, time_scale)
        time_grads += plain_grads(joined[4], joined[5], joined[6], joined[7], time_input, time_gain)

    space_one = [sz1_one, seu_one, sh_one, se2_one, sz0_one, sgqkv_one, so_one, se1_one]
    whole_shapes = [((everything, a.shape[2]), BF) for a in space_one]
    parts_shapes = [((4, 4, 96, CHUNK), BF)] * 4
    sg1, sgqkv, *weights = manual_call(
        functools.partial(space_kernel, hierarchical),
        ids,
        [row(space_scale), sinv1, g0_moved, sslope, sz1, space_output, space_up, space_down]
        + [sqkv, sp, sh, sz0, so]
        + space_one,
        [(shared_w, F32), (shared_3, BF)]
        + (parts_shapes if hierarchical else [whole_shapes[i] for i in (1, 3, 7)]),
        [
            (g0_moved.shape, BF),
            (sslope.shape, BF),
            (space_output.shape, BF),
            (space_up.shape, BF),
            (space_down.shape, BF),
            (sqkv.shape, BF),
            (sp.shape, BF),
            (shared_w, BF),
            (shared_w, F32),
            ((some, 4, tokens, tokens), BF),
            (square, BF),
        ]
        + whole_shapes
        + (parts_shapes if hierarchical else []),
        80,
        small=2,
        after=held_back,
        flops=2 * packs * flops,
    )
    held_back = ()
    if hierarchical:
        time_got, sgqkv = lax.optimization_barrier((time_got, sgqkv))
        time_mine = time_terms[::2]
        time_halves, time_near = near_parts(time_mine, time_got, time_far)
        mine = weights[::2]
        got = [swap(other, "tm", 8, 1) for other in weights[1::2]]
        far = far_parts(mine, got, marker(time_near[1]))
        far, time_halves = lax.optimization_barrier((far, time_halves))
        held_back = far
    input_grad, result = shared.call(
        space_back_in,
        [
            ("step", sgqkv),
            ("whole", space_input),
            ("whole", row(space_gain)),
            ("step", sz0),
            ("step", sinv0),
            ("step", sg1),
            ("moved", out_moved),
        ],
        [("pack", frames.shape, F32, input_grad), ("pack", frames.shape, F32, result)],
        flops=flops // 4,
        after=held_back,
    )
    if hierarchical:
        time_rows = stream_rows(time_mine, time_got, time_halves, time_near)
        time_final = z_sum(time_rows)
        got, time_final, input_grad = lax.optimization_barrier((got, time_final, input_grad))
        final = z_sum(stream_rows(mine, got, *near_parts(mine, got, far)))
        grads = finish_call(
            finish_kernel,
            ids,
            gather_parts(final),
            [(space_up, space_scale), (space_input, space_gain)],
            feed_shapes + attend_shapes,
        )
        feed_grads, attend_grads = grads[:3], grads[3:]
        time_grads = finish_call(
            finish_kernel,
            ids,
            gather_parts(time_final),
            [(time_up, time_scale), (time_input, time_gain)],
            feed_shapes + attend_shapes,
        )
    else:
        have = some * tokens
        seu, se2, se1 = [a[:have].reshape(some, tokens, -1) for a in weights]
        feed_grads = plain_grads(
            joint(sz1, sz1_one),
            joint(seu, seu_one),
            joint(sh, sh_one),
            joint(se2, se2_one),
            space_up,
            space_scale,
        )
        attend_grads = plain_grads(
            joint(sz0, sz0_one),
            joint(sgqkv, sgqkv_one),
            joint(so, so_one),
            joint(se1, se1_one),
            space_input,
            space_gain,
        )
    grads = attend_grads + feed_grads + time_grads[3:] + time_grads[:3]
    return (result, input_grad, *grads)


def joint(shared, one):
    return jnp.concatenate([shared, one]).reshape(-1, shared.shape[-1])


def solution(mesh):
    tokens = P("stream", "tm", None, None)
    vector, matrix = P("tm"), P("tm", None)
    return jax.shard_map(
        functools.partial(per_device, mesh.shape["tm"], mesh.shape["stream"]),
        mesh=mesh,
        in_specs=(tokens,) + (P(),) * 12 + (P("stream", None), tokens),
        out_specs=(tokens, tokens) + (vector, matrix, matrix, vector, matrix, matrix) * 2,
        check_vma=False,
    )
```

```python
import functools

import jax
import jax.numpy as jnp
from jax import lax
from jax.experimental import pallas as pl
from jax.experimental.pallas import tpu as pltpu
from jax.sharding import PartitionSpec as P

HEADS = 8
EPS = 1e-05
GELU_A = 0.7978845608028654
GELU_B = 0.044715
BF = jnp.bfloat16
F32 = jnp.float32
CHUNK = 512
LANES = 128
COST = 1
ROWS = (0, 96, 64, 80, 160, 176)
VMEM = 60 * 1024 * 1024
SMALL_VMEM = 24 * 1024 * 1024


def nn(a, b):
    return jnp.dot(a, b, preferred_element_type=F32)


def nt(a, b):
    return lax.dot_general(a, b, (((1,), (1,)), ((), ())), preferred_element_type=F32)


def tn(a, b):
    return lax.dot_general(a, b, (((0,), (0,)), ((), ())), preferred_element_type=F32)


def unit(values):
    average = jnp.mean(values, axis=-1, keepdims=True)
    centered = values - average
    inverse = lax.rsqrt(jnp.mean(centered * centered, axis=-1, keepdims=True) + EPS)
    return centered * inverse, inverse


def unit_backward(grad, unit_rows, inverse):
    first = jnp.mean(grad, axis=-1, keepdims=True)
    second = jnp.mean(grad * unit_rows, axis=-1, keepdims=True)
    return inverse * (grad - first - unit_rows * second)


def gelu_parts(u):
    square = u * u
    tangent = jnp.tanh(u * (BF(GELU_A) + BF(GELU_A * GELU_B) * square))
    half = BF(0.5) * u
    value = half + half * tangent
    slope = (BF(0.5) + BF(0.5) * tangent) + half * (BF(1.0) - tangent * tangent) * (
        BF(GELU_A) + BF(3.0 * GELU_A * GELU_B) * square
    )
    return value, slope


def head_masks(width):
    lane = lax.broadcasted_iota(jnp.int32, (1, 2 * width), 1)
    low = lane < width
    return low, (low.astype(F32).astype(BF), (1.0 - low.astype(F32)).astype(BF))


def attend_steps(qkv_ref, p_ref, o_ref, bias_ref, s_ref):
    width = qkv_ref.shape[1] // 3
    size = width // HEADS
    _, masks = head_masks(size)

    def lanes(part, head):
        at = part * width + (head // 2) * 2 * size
        return qkv_ref[:, at : at + 2 * size]

    def score(head):
        s_ref[head % 4] = nt(lanes(1, head) * masks[head % 2], lanes(0, head) * BF(size**-0.5))

    def soften(head):
        scores = s_ref[head % 4]
        if bias_ref is not None:
            scores = scores + bias_ref[...]
        e = jnp.exp(scores - jnp.max(scores, axis=0, keepdims=True))
        p_ref[head] = (e * (1.0 / jnp.sum(e, axis=0, keepdims=True))).astype(BF)

    for head in range(0, HEADS, 2):
        if head == 0:
            score(0)
            score(1)
        if head + 2 < HEADS:
            score(head + 2)
            score(head + 3)
        soften(head)
        soften(head + 1)
        yield
    for head in range(0, HEADS, 2):
        v = lanes(2, head).T
        both = jnp.concatenate([nn(v[:size], p_ref[head]), nn(v[size:], p_ref[head + 1])], axis=0)
        o_ref[:, head * size : (head + 2) * size] = both.T.astype(BF)
        yield


def attend_backward_steps(qkv_ref, p_ref, go_ref, out_ref, gp_ref, gs_ref):
    width = qkv_ref.shape[1] // 3
    size = width // HEADS
    _, masks = head_masks(size)

    def lanes(part, head):
        at = part * width + (head // 2) * 2 * size
        return qkv_ref[:, at : at + 2 * size]

    def gos(head):
        return go_ref[:, (head // 2) * 2 * size : (head // 2 + 1) * 2 * size]

    def put(part, head, value):
        at = part * width + head * size
        out_ref[:, at : at + 2 * size] = value.astype(BF)

    def start(head):
        for h in (head, head + 1):
            gp_ref[h % 4] = nt(lanes(2, h) * masks[h % 2], gos(h)).astype(BF)
        g = gos(head)
        put(2, head, nn(p_ref[head], g * masks[0]) + nn(p_ref[head + 1], g * masks[1]))

    def middle(head):
        p = p_ref[head]
        weighted = p * gp_ref[head % 4]
        total = jnp.sum(weighted.astype(F32), axis=0, keepdims=True).astype(BF)
        gs_ref[head] = weighted - p * total

    def finish(head):
        q = lanes(0, head) * BF(size**-0.5)
        k = (lanes(1, head) * BF(size**-0.5)).T
        put(1, head, nn(gs_ref[head], q * masks[0]) + nn(gs_ref[head + 1], q * masks[1]))
        both = jnp.concatenate([nn(k[:size], gs_ref[head]), nn(k[size:], gs_ref[head + 1])], axis=0)
        put(0, head, both.T)

    start(0)
    yield
    for head in range(0, HEADS, 2):
        middle(head)
        middle(head + 1)
        if head + 2 < HEADS:
            start(head + 2)
        if head > 0:
            finish(head - 2)
        yield
    finish(HEADS - 2)


def feed_up_steps(m, up_ref, down_ref, h_ref, slope_ref, u_ref):
    steps = up_ref.shape[1] // CHUNK

    def before(step):
        u_ref[step % 2] = nn(m, up_ref[:, step * CHUNK : (step + 1) * CHUNK]).astype(BF)

    before(0)
    for step in range(steps):
        if step + 1 < steps:
            before(step + 1)
        at = step * CHUNK
        h_ref[:, at : at + CHUNK], slope_ref[:, at : at + CHUNK] = gelu_parts(u_ref[step % 2])
        yield
    return nn(h_ref[...], down_ref[...])


def feed_back_steps(e2, up_ref, down_ref, slope_ref, eu_ref, up_copy=None):
    for at in range(0, up_ref.shape[1], CHUNK):
        gh = nt(e2, down_ref[at : at + CHUNK, :]).astype(BF)
        eu_ref[:, at : at + CHUNK] = gh * slope_ref[:, at : at + CHUNK]
        yield
    if up_copy is not None:
        wait(up_copy)
    return nt(eu_ref[...], up_ref[...])


def whole(steps):
    while True:
        try:
            next(steps)
        except StopIteration as end:
            return end.value


def together(runs):
    while runs:
        runs = [run for run in runs if next(run, "end") != "end"]


def attend(*args):
    whole(attend_steps(*args))


def attend_backward(*args):
    whole(attend_backward_steps(*args))


def feed_up(*args):
    return whole(feed_up_steps(*args))


def feed_back(*args):
    return whole(feed_back_steps(*args))


def rows_of(block):
    slots, _, patches, width = block.shape
    return block[:, 0].astype(F32).reshape(slots * patches, width)


def block_of(rows, ref):
    slots, _, patches, width = ref.shape
    ref[:, 0] = rows.reshape(slots, patches, width).astype(ref.dtype)


def work_shapes(tokens):
    return [
        pltpu.VMEM((4, tokens, tokens), F32),
        pltpu.VMEM((2, tokens, CHUNK), BF),
        pltpu.VMEM((4, tokens, tokens), BF),
        pltpu.VMEM((HEADS, tokens, tokens), BF),
    ]


def wide(column):
    return jnp.broadcast_to(column, (column.shape[0], LANES))


def space_rows(x, weights, state, work):
    gain, w_in, w_out, scale, w_up, w_down = weights
    z0, inv0, qkv, p, o, z1, inv1, h, slope = state
    unit0, inverse0 = unit(x)
    z0[...] = unit0.astype(BF)
    inv0[...] = wide(inverse0)
    qkv[...] = nn((unit0 * gain[...]).astype(BF), w_in[...]).astype(BF)
    attend(qkv, p, o, None, work[0])
    r1 = x + nn(o[...], w_out[...])
    unit1, inverse1 = unit(r1)
    z1[...] = unit1.astype(BF)
    inv1[...] = wide(inverse1)
    m = (unit1 * scale[...]).astype(BF)
    return r1 + feed_up(m, w_up, w_down, h, slope, work[1])


def space_forward(labels, frames, *rest):
    weights, x2, state, work = rest[:6], rest[6], rest[7:16], rest[16:]
    rows = space_rows(frames[0, 0].astype(F32), weights, [ref.at[0] for ref in state], work)
    block_of(rows, x2)


def build_bias(labels, pack, slots, patches, bias):
    tokens = slots * patches
    row = lax.broadcasted_iota(jnp.int32, (1, tokens), 1)
    column = lax.broadcasted_iota(jnp.int32, (tokens, 1), 0)

    def label_of(position):
        slot = position // patches
        value = jnp.zeros_like(position)
        for f in range(slots):
            value = jnp.where(slot == f, labels[pack, f], value)
        return value

    same_patch = (row % patches) == (column % patches)
    allowed = same_patch & (column <= row) & (label_of(column) == label_of(row))
    bias[...] = jnp.where(allowed, 0.0, -1e30)


def send_moved(copies, ids, held, outs):
    if len(outs) == 1:
        copies.send(held, outs[0])
        return
    for d in range(4):
        at = 2 * (ids[1] ^ d)
        copies.send(held.at[at + ids[0]], outs[0].at[d])
        copies.send(held.at[at + 1 - ids[0]], outs[1].at[d])


def fetch_moved(copies, ids, pieces, held):
    if len(pieces) == 1:
        return [copies.fetch(pieces[0], held)]
    near, far, *others = pieces
    at = 2 * ids[1]
    got = [copies.fetch(near.at[0], held.at[at + ids[0]])]
    got.append(copies.fetch(far.at[0], held.at[at + 1 - ids[0]]))
    for d, piece in enumerate(others, 1):
        at = 2 * (ids[1] ^ d)
        got.append(copies.fetch(piece.at[0], held.at[at + ids[0]]))
        got.append(copies.fetch(piece.at[1], held.at[at + 1 - ids[0]]))
    return got


def exchange_pieces(arrays):
    if len(arrays) == 1:
        return [lax.all_to_all(arrays[0], "tm", split_axis=0, concat_axis=0, tiled=True)]
    near, far = arrays[0], swap(arrays[1], "tm", 8, 1)
    return [near, far] + [swap(jnp.stack([near[d], far[d]]), "tm", 8, 2 * d) for d in range(1, 4)]


def time_kernel(moved, labels, ids, gain, scale, x2_in, grad_in, w_in_in, w_out_in, w_up_in, w_down_in, *rest):
    g0_outs, outs, rest = rest[:moved], (None,) + rest[moved : moved + 9], rest[moved + 9 :]
    x2, grad, w_in, w_out, w_up, w_down = rest[:6]
    held = rest[6:16]
    g0, out, z0, gqkv, o, e1, z1, eu, h, e2 = held
    qkv, p, slope, bias, go, scores, u, gp, gs = rest[16:25]
    copies = Copies(rest[-1])
    slots, packs, patches, _ = x2.shape
    got_x2, got_in = copies.fetch(x2_in, x2), copies.fetch(w_in_in, w_in)
    got_out, got_up = copies.fetch(w_out_in, w_out), copies.fetch(w_up_in, w_up)
    got_down, got_grad = copies.fetch(w_down_in, w_down), copies.fetch(grad_in, grad)

    def send(index, pack):
        copies.send(held[index].at[pack], outs[index].at[pack])

    def run(pack):
        if pack == 0:
            wait(got_x2)
        build_bias(labels, pack_at(labels, pack), slots, patches, bias.at[pack])
        x = rows_of(x2[:, pack : pack + 1])
        unit0, inverse0 = unit(x)
        z0[pack] = unit0.astype(BF)
        send(2, pack)
        if pack == 0:
            wait(got_in)
        qkv[pack] = nn((unit0 * gain[...]).astype(BF), w_in[...]).astype(BF)
        yield
        yield from attend_steps(qkv.at[pack], p.at[pack], o.at[pack], bias.at[pack], scores.at[pack])
        send(4, pack)
        if pack == 0:
            wait(got_out)
        r1 = x + nn(o[pack], w_out[...])
        unit1, inverse1 = unit(r1)
        z1[pack] = unit1.astype(BF)
        send(6, pack)
        m = (unit1 * scale[...]).astype(BF)
        yield
        if pack == 0:
            wait(got_up, got_down)
        total = yield from feed_up_steps(m, w_up, w_down, h.at[pack], slope.at[pack], u.at[pack])
        send(8, pack)
        block_of(r1 + total, out.at[:, pl.ds(pack, 1)])
        if pack == 0:
            wait(got_grad)
        g2 = rows_of(grad[:, pack : pack + 1])
        e2[pack] = g2.astype(BF)
        send(9, pack)
        yield
        gm = yield from feed_back_steps(e2[pack], w_up, w_down, slope.at[pack], eu.at[pack])
        send(7, pack)
        g1 = g2 + unit_backward(gm * scale[...], unit1, inverse1)
        e1[pack] = g1.astype(BF)
        send(5, pack)
        go[pack] = nt(e1[pack], w_out[...]).astype(BF)
        yield
        yield from attend_backward_steps(
            qkv.at[pack], p.at[pack], go.at[pack], gqkv.at[pack], gp.at[pack], gs.at[pack]
        )
        send(3, pack)
        gn = nt(gqkv[pack], w_in[...])
        block_of(g1 + unit_backward(gn * gain[...], unit0, inverse0), g0.at[:, pl.ds(pack, 1)])

    together([run(pack) for pack in range(packs)])
    send_moved(copies, ids, g0, g0_outs)
    copies.send(out, outs[1])
    copies.finish()


def alone_both(labels, frames, grad, *rest):
    space, (gain, w_in, w_out, scale, w_up, w_down) = rest[:6], rest[6:12]
    input_grad, out = rest[12:14]
    sz0, so, se1, sgqkv, sz1, seu, sh, se2 = [ref.at[0] for ref in rest[14:22]]
    z0, o, e1, gv, z1, eu, h, e2 = [ref.at[0] for ref in rest[22:30]]
    inv0, inv1, qkv, p, sslope, slope, go, *work = rest[30:]
    state = sz0, inv0, qkv, p, so, sz1, inv1, sh, sslope
    x = space_rows(frames[0, 0].astype(F32), space, state, work)
    width = x.shape[1]
    unit0, inverse0 = unit(x)
    z0[...] = unit0.astype(BF)
    o[...] = nn((unit0 * gain[...]).astype(BF), w_in[:, 2 * width :]).astype(BF)
    r1 = x + nn(o[...], w_out[...])
    unit1, inverse1 = unit(r1)
    z1[...] = unit1.astype(BF)
    m = (unit1 * scale[...]).astype(BF)
    out[0, 0] = r1 + feed_up(m, w_up, w_down, h, slope, work[1])
    e2[...] = grad[0, 0]
    g2 = grad[0, 0].astype(F32)
    gm = feed_back(e2[...], w_up, w_down, slope, eu)
    g1 = g2 + unit_backward(gm * scale[...], unit1, inverse1)
    e1[...] = g1.astype(BF)
    gv[...] = nt(e1[...], w_out[...]).astype(BF)
    gn = nt(gv[...], w_in[:, 2 * width :])
    g2 = g1 + unit_backward(gn * gain[...], unit0, inverse0)
    gain, w_in, w_out, scale, w_up, w_down = space
    se2[...] = g2.astype(BF)
    gm = feed_back(se2[...], w_up, w_down, sslope, seu)
    g1 = g2 + unit_backward(gm * scale[...], sz1[...].astype(F32), inv1[:, :1])
    se1[...] = g1.astype(BF)
    go[...] = nt(se1[...], w_out[...]).astype(BF)
    attend_backward(qkv, p, go, sgqkv, work[2], work[3])
    gn = nt(sgqkv[...], w_in[...])
    input_grad[0, 0] = g1 + unit_backward(gn * gain[...], sz0[...].astype(F32), inv0[:, :1])


def space_back_in(labels, gqkv, w_in, gain, z0, inv0, g1, moved, input_grad, result):
    gn = nt(gqkv[0], w_in[...])
    grad = unit_backward(gn * gain[...], z0[0].astype(F32), inv0[0, :, :1])
    input_grad[0, 0] = g1[0] + grad
    result[0, 0] = rows_of(moved[...])


class Copies:
    def __init__(self, semaphores):
        self.semaphores, self.count, self.sent = semaphores, 0, []

    def fetch(self, source, target):
        copy = pltpu.make_async_copy(source, target, self.semaphores.at[self.count])
        self.count += 1
        copy.start()
        return copy

    def send(self, source, target):
        self.sent.append(self.fetch(source, target))

    def finish(self):
        for copy in self.sent:
            copy.wait()


def wait(*copies):
    for copy in copies:
        copy.wait()


def space_kernel(hierarchical, pieces, ids, scale, inv1, *rest):
    g2_in, rest = rest[:pieces], rest[pieces:]
    (slope_in, z1_in, w_out_in, w_up_in, w_down_in, qkv_in, p_in), rest = rest[:7], rest[7:]
    shared, one, rest = rest[:3], rest[3:11], rest[11:]
    (g1_out, gqkv_out), outs, scratch = rest[:2], rest[2 : 6 if hierarchical else 5], rest[6 if hierarchical else 5 :]
    g2, slope, w_out, w_up, w_down, qkv, p, go, g1, gp, gs = scratch[:11]
    z1, eu, h, e2, z0, gqkv, o, e1 = whole = scratch[11:19]
    copies = Copies(scratch[-1])
    packs, tokens, _ = g1.shape
    have = packs * tokens
    got_g2 = fetch_moved(copies, ids, g2_in, g2)
    got_down = copies.fetch(w_down_in, w_down)
    got_slope = [copies.fetch(slope_in.at[pack], slope.at[pack]) for pack in range(packs)]
    got_up = copies.fetch(w_up_in, w_up)
    got_z1 = [
        copies.fetch(z1_in.at[pack], z1.at[pl.ds(pack * tokens, tokens)]) for pack in range(packs)
    ]
    got_out = copies.fetch(w_out_in, w_out)
    got_attend = [
        (copies.fetch(qkv_in.at[pack], qkv.at[pack]), copies.fetch(p_in.at[pack], p.at[pack]))
        for pack in range(packs)
    ]
    got_rest = []
    if hierarchical:
        for source, target in zip(shared, (h, z0, o)):
            for pack in range(packs):
                rows = pl.ds(pack * tokens, tokens)
                got_rest.append(copies.fetch(source.at[pack], target.at[rows]))
        for source, target in zip(one, whole):
            got_rest.append(copies.fetch(source.at[0], target.at[pl.ds(have, tokens)]))
    wait(*got_g2)

    def run(pack):
        rows = slice(pack * tokens, (pack + 1) * tokens)
        e2[rows] = rows_of(g2[:, pack : pack + 1]).astype(BF)
        if pack == 0:
            wait(got_down)
        wait(got_slope[pack])
        gm = yield from feed_back_steps(e2[rows], w_up, w_down, slope.at[pack], eu.at[rows], got_up if pack == 0 else None)
        if pack == 0:
            wait(*got_z1, got_out)
        grad = unit_backward(gm * scale[...], z1[rows].astype(F32), inv1[pack, :, :1])
        total = rows_of(g2[:, pack : pack + 1]) + grad
        g1[pack] = total
        e1[rows] = total.astype(BF)
        go[pack] = nt(e1[rows], w_out[...]).astype(BF)
        copies.send(g1.at[pack], g1_out.at[pack])
        yield
        wait(*got_attend[pack])
        rows = pl.ds(pack * tokens, tokens)
        yield from attend_backward_steps(
            qkv.at[pack], p.at[pack], go.at[pack], gqkv.at[rows], gp.at[pack], gs.at[pack]
        )
        copies.send(gqkv.at[rows], gqkv_out.at[pack])

    together([run(pack) for pack in range(packs)])
    if hierarchical:
        wait(*got_rest)
        one = Halves(copies, ids, scratch[19:21], outs[:2], x_high=True)
        two = Halves(copies, ids, scratch[21:23], outs[2:])
        up_tiles(one, z1, eu, 0)
        down_tiles(two, e2, h, 0)
        attend_tiles([one, one, two, two], z0, o, gqkv, e1, [64, 80, 64, 80], gqkv.shape[0])
    else:
        for source, target in zip((eu, e2, e1), outs):
            copies.send(source, target)
    copies.finish()


def to_send(labels, grad, out):
    for place in range(out.shape[1]):
        rows = grad[pack_at(labels, place), 0].astype(F32)
        out[:, place] = rows.reshape(out.shape[0], out.shape[2], out.shape[3]).astype(BF)


def pack_at(labels, place):
    packs, slots = labels.shape
    alone = packs - 1
    for pack in range(packs - 2, -1, -1):
        alone = jnp.where(labels[pack, slots - 1] == slots - 1, pack, alone)
    return jnp.where(place == packs - 1, alone, place + (place >= alone).astype(jnp.int32))


def without(kernel, first, count):
    def call(*refs):
        return kernel(*refs[:first], *refs[first + count :])

    return call


class Packs:
    def __init__(self, labels, first, count):
        self.labels, self.first, self.count = labels, first, count

    def call(self, kernel, args, outs, scratch=(), flops=0, after=()):
        first, last = self.first, self.labels.shape[0] - 2
        scalars = (self.labels,)

        def spec(kind, shape):
            rank = len(shape)
            if kind == "whole":
                return pl.BlockSpec(shape, lambda i, *s: (0,) * rank)
            if kind == "pack":
                return pl.BlockSpec(
                    (1,) + tuple(shape[1:]), lambda i, s: (pack_at(s, first + i),) + (0,) * (rank - 1)
                )
            if kind == "place":
                return pl.BlockSpec(
                    (1,) + tuple(shape[1:]), lambda i, *s: (first + i,) + (0,) * (rank - 1)
                )
            if kind == "step":
                return pl.BlockSpec(
                    (1,) + tuple(shape[1:]), lambda i, *s: (i,) + (0,) * (rank - 1)
                )
            if kind == "moved":
                return pl.BlockSpec(
                    (shape[0], 1, shape[2], shape[3]),
                    lambda i, *s: (0, jnp.minimum(i, last), 0, 0),
                )
            return pl.BlockSpec(memory_space=pl.ANY)

        in_specs = [spec(kind, array.shape) for kind, array in args]
        operands = [array for _, array in args]
        aliases = {}
        for index, (kind, shape, dtype, into) in enumerate(outs):
            if into is not None:
                aliases[len(scalars) + len(operands)] = index
                operands.append(into)
                in_specs.append(pl.BlockSpec(memory_space=pl.ANY))
        for array in after:
            operands.append(array)
            in_specs.append(pl.BlockSpec(memory_space=pl.ANY))
        moved = sum(a.size * a.dtype.itemsize for a in operands)
        unread = len(operands) - len(args)
        return pl.pallas_call(
            without(kernel, len(scalars) + len(args), unread),
            out_shape=[jax.ShapeDtypeStruct(shape, dtype) for _, shape, dtype, _ in outs],
            grid_spec=pltpu.PrefetchScalarGridSpec(
                num_scalar_prefetch=len(scalars),
                grid=(self.count,),
                in_specs=in_specs,
                out_specs=[spec(kind, shape) for kind, shape, _, _ in outs],
                scratch_shapes=list(scratch),
            ),
            input_output_aliases=aliases,
            compiler_params=pltpu.CompilerParams(
                vmem_limit_bytes=VMEM, dimension_semantics=("arbitrary",)
            ),
            cost_estimate=pl.CostEstimate(
                flops=int(flops * self.count * COST), bytes_accessed=int(moved * COST), transcendentals=0
            ),
        )(*scalars, *operands)


class Halves:
    def __init__(self, copies, ids, held, outs, x_high=False):
        self.copies, self.held, self.outs = copies, held, outs
        self.first, self.z, self.s, self.x_high = ids[0] == 0, ids[1], ids[2], x_high

    def part(self, s):
        if s is None:
            return slice(None)
        part = s ^ self.s
        return (part & 1) * 2 + (part >> 1) if self.x_high else part

    def put(self, s, z, at, even, odd):
        rows = slice(at, at + even.shape[0])
        self.held[0][self.part(s), z ^ self.z, rows] = jnp.where(self.first, even, odd)
        self.held[1][self.part(s), z ^ self.z, rows] = jnp.where(self.first, odd, even)

    def send(self, s, z, at, rows):
        index = self.part(s), slice(None) if z is None else z ^ self.z, pl.ds(at, rows)
        for ref, out in zip(self.held, self.outs):
            self.copies.send(ref.at[index], out.at[index])


def up_tiles(place, z1, eu, at):
    for step in range(4):
        tile = tn(z1[...], eu[:, step * CHUNK : (step + 1) * CHUNK]).astype(BF)
        for z in range(4):
            row = 128 * z
            place.put(step, z, at, tile[row : row + 64], tile[row + 64 : row + 128])
        place.send(step, None, at, 64)


def down_tiles(place, e2, h, at):
    for step in range(4):
        tile = tn(e2[...], h[:, step * CHUNK : (step + 1) * CHUNK]).astype(BF)
        for s in range(4):
            upper, lower = tile[128 * s : 128 * s + 64], tile[128 * s + 64 : 128 * s + 128]
            even = jnp.concatenate([upper[:, :256], lower[:, :256]], axis=1)
            odd = jnp.concatenate([upper[:, 256:], lower[:, 256:]], axis=1)
            place.put(s, step, at, even, odd)
        place.send(None, step, at, 64)


def attend_tiles(places, z0, o, gqkv, e1, ats, depth):
    for step, (place, at) in enumerate(zip(places, ats)):
        if step == 3:
            tile = tn(o[...], e1[...])
        else:
            rows = gqkv.shape[0] if step == 2 else depth
            tile = tn(z0[:rows], gqkv[:rows, step * CHUNK : (step + 1) * CHUNK])
        tile = tile.astype(BF)
        for z in range(4):
            for s in range(4):
                row = 128 * z + 16 * s
                place.put(s, z, at, tile[row : row + 16], tile[row + 64 : row + 80])
        if step % 2:
            place.send(None, None, at - 16, 32)


def time_weights_kernel(ids, *rest):
    names = 8
    shared, single, outs, scratch = rest[:names], rest[names : 2 * names], rest[16:20], rest[20:]
    z1, eu, e2, h, z0, gqkv, o, e1 = scratch[:names]
    copies = Copies(scratch[-1])
    one = Halves(copies, ids, scratch[8:10], outs[:2], x_high=True)
    two = Halves(copies, ids, scratch[10:12], outs[2:])
    packs, tokens, _ = shared[0].shape
    have = packs * tokens
    got = []
    for source, last, target in zip(shared, single, scratch):
        wide_target = target.at[pl.ds(have, tokens)]
        if last.shape[2] < target.shape[1]:
            wide_target = target.at[pl.ds(have, tokens), pl.ds(target.shape[1] - last.shape[2], last.shape[2])]
        got.append(
            [copies.fetch(source.at[pack], target.at[pl.ds(pack * tokens, tokens)]) for pack in range(packs)]
            + [copies.fetch(last.at[0], wide_target)]
        )
    wait(*got[0], *got[1], *got[2], *got[3])
    up_tiles(one, z1, eu, 0)
    down_tiles(two, e2, h, 0)
    wait(*got[4], *got[5], *got[6], *got[7])
    attend_tiles([one, one, two, two], z0, o, gqkv, e1, [64, 80, 64, 80], have)
    copies.finish()


def manual_call(kernel, ids, args, outs, scratch, semaphores, small=0, after=(), flops=0):
    anywhere = pl.BlockSpec(memory_space=pl.ANY)
    scalars = ids if isinstance(ids, tuple) else (ids,)
    return pl.pallas_call(
        without(kernel, len(scalars) + len(args), len(after)),
        out_shape=[jax.ShapeDtypeStruct(shape, dtype) for shape, dtype in outs],
        in_specs=[pl.BlockSpec(memory_space=pltpu.SMEM)] * len(scalars)
        + [pl.BlockSpec(memory_space=pltpu.VMEM)] * small
        + [anywhere] * (len(args) - small + len(after)),
        out_specs=[anywhere] * len(outs),
        scratch_shapes=[pltpu.VMEM(shape, dtype) for shape, dtype in scratch]
        + [pltpu.SemaphoreType.DMA((semaphores,))],
        compiler_params=pltpu.CompilerParams(vmem_limit_bytes=VMEM),
        cost_estimate=pl.CostEstimate(
            flops=int(flops * COST), bytes_accessed=0, transcendentals=0
        ),
    )(*scalars, *args, *after)


def swap(array, axis, size, mask):
    return lax.ppermute(array, axis, [(i, i ^ mask) for i in range(size)])


def add(*terms):
    total = terms[0].astype(F32)
    for term in terms[1:]:
        total = total + term.astype(F32)
    return total.astype(BF)


def far_parts(mine, got, note):
    return [add(a[2:], b[2:], note) for a, b in zip(mine, got)]


def near_parts(mine, got, far):
    halves = [swap(far[0], "stream", 4, 1), swap(far[1], "stream", 4, 2)]
    return halves, [add(a[1], b[1], half[1]) for a, b, half in zip(mine, got, halves)]


def stream_rows(mine, got, halves, near, *note):
    last = [swap(near[0], "stream", 4, 2), swap(near[1], "stream", 4, 1)]
    terms = list(zip(mine, got, halves, last))
    return [
        jnp.concatenate([add(a[0][d], b[0][d], half[0][d], end[d], *note) for a, b, half, end in terms])
        for d in range(4)
    ]


def z_got(rows):
    return [swap(rows[d], "tm", 8, 2 * d) for d in range(1, 4)]


def z_sum(rows):
    return add(rows[0], *[swap(rows[d], "tm", 8, 2 * d) for d in range(1, 4)])


def gather_parts(final):
    return [final] + [swap(final, "stream", 4, d) for d in range(1, 4)]


def marker(*arrays):
    def kernel(*refs):
        refs[-1][...] = jnp.zeros_like(refs[-1])

    return pl.pallas_call(
        kernel,
        out_shape=jax.ShapeDtypeStruct((1, CHUNK), F32),
        in_specs=[pl.BlockSpec(memory_space=pl.ANY)] * len(arrays),
        out_specs=pl.BlockSpec(memory_space=pltpu.VMEM),
        cost_estimate=pl.CostEstimate(flops=10**12, bytes_accessed=10**8, transcendentals=0),
    )(*arrays)


def as_row(col):
    size = col.shape[0]
    eye = lax.broadcasted_iota(jnp.int32, (size, size), 0) == lax.broadcasted_iota(
        jnp.int32, (size, size), 1
    )
    return jnp.sum(jnp.where(eye, col, 0.0), axis=0, keepdims=True)


def own_rows(ids, vector):
    shape = 64, vector.shape[1]
    row = lax.broadcasted_iota(jnp.int32, shape, 0) + 64 * (2 * ids[1] + ids[0])
    lane = lax.broadcasted_iota(jnp.int32, shape, 1)
    return jnp.sum(jnp.where(row == lane, vector[...], 0.0), axis=1, keepdims=True)


def finish_kernel(ids, p0, p1, p2, p3, w_up, scale, w_in, gain, *outs):
    scale_grad, up_grad, down_grad, gain_grad, in_grad, out_grad = outs
    up_at, down_at, *in_at, out_at = ROWS
    for d, piece in enumerate((p0, p1, p2, p3)):
        s = ids[2] ^ d
        up_grad[:, pl.ds(pl.multiple_of(512 * s, 512), 512)] = piece[up_at : up_at + 64].astype(F32)
        lower = piece[down_at : down_at + 64].astype(F32)
        whole = jnp.concatenate([lower[:, :256], lower[:, 256:]], axis=0)
        down_grad[:, pl.ds(pl.multiple_of(128 * s, 128), 128)] = whole.T
        rows = pl.ds(pl.multiple_of(16 * s, 16), 16)
        for third, at in enumerate(in_at):
            in_grad[rows, 512 * third : 512 * third + 512] = piece[at : at + 16].astype(F32)
        out_grad[rows, :] = piece[out_at : out_at + 16].astype(F32)
    for grad, weight, factor, vector_grad in (
        (up_grad, w_up, scale, scale_grad),
        (in_grad, w_in, gain, gain_grad),
    ):
        total = grad[...]
        vector_grad[...] = as_row(jnp.sum(total * weight[...].astype(F32), axis=1, keepdims=True))
        grad[...] = total * own_rows(ids, factor)


def finish_call(kernel, ids, pieces, pairs, outs):
    whole = pl.BlockSpec(pieces[0].shape, lambda i, *s: (0, 0))
    specs, operands = [], []
    for weight, vector in pairs:
        height = weight.shape[0] // 8
        specs += [
            pl.BlockSpec((height, weight.shape[1]), lambda i, s: (2 * s[1] + s[0], 0)),
            pl.BlockSpec((1, vector.size), lambda i, *s: (0, 0)),
        ]
        operands += [weight, vector.reshape(1, -1)]
    results = pl.pallas_call(
        kernel,
        out_shape=[jax.ShapeDtypeStruct(shape, F32) for shape in outs],
        grid_spec=pltpu.PrefetchScalarGridSpec(
            num_scalar_prefetch=1,
            grid=(1,),
            in_specs=[whole] * 4 + specs,
            out_specs=[pl.BlockSpec(shape, lambda i, *s: (0, 0)) for shape in outs],
        ),
        compiler_params=pltpu.CompilerParams(vmem_limit_bytes=SMALL_VMEM),
    )(ids, *pieces, *operands)
    return [a.reshape(-1) if a.shape[0] == 1 else a for a in results]


def plain_grads(z, grads, left, right, weight, vector):
    product = tn(z, grads)
    vector_grad = jnp.sum(product * weight.astype(F32), axis=1)
    sums = []
    for term in (vector_grad, product * vector[:, None], tn(left, right)):
        share = lax.psum_scatter(term.astype(BF), "tm", scatter_dimension=0, tiled=True)
        sums.append(lax.psum(share, "stream").astype(F32))
    return sums


def everyone_once(labels, grad, moved):
    _, shape, dtype, _ = moved
    return pl.pallas_call(
        to_send,
        out_shape=[jax.ShapeDtypeStruct(shape, dtype)],
        grid_spec=pltpu.PrefetchScalarGridSpec(
            num_scalar_prefetch=1,
            grid=(1,),
            in_specs=[pl.BlockSpec(grad.shape, lambda i, s: (0, 0, 0, 0))],
            out_specs=[pl.BlockSpec(shape, lambda i, s: (0, 0, 0, 0))],
        ),
        compiler_params=pltpu.CompilerParams(vmem_limit_bytes=VMEM),
    )(labels, grad)


def per_device(
    ranks,
    streams,
    frames,
    space_gain,
    space_input,
    space_output,
    space_scale,
    space_up,
    space_down,
    time_gain,
    time_input,
    time_output,
    time_scale,
    time_up,
    time_down,
    clip_labels,
    output_grad,
):
    packs, _, tokens, width = frames.shape
    slots = clip_labels.shape[1]
    patches = tokens // ranks
    hidden = space_up.shape[1]
    some = packs - 1
    hierarchical = (ranks, streams) == (8, 4)
    tm = lax.axis_index("tm")
    ids = jnp.stack([tm % 2, tm // 2, lax.axis_index("stream")]).astype(jnp.int32)
    shared = Packs(clip_labels, 0, some)
    single = Packs(clip_labels, some, 1)

    def row(vector):
        return vector.reshape(1, -1)

    def exchange(array):
        return lax.all_to_all(array, "tm", split_axis=0, concat_axis=0, tiled=True)

    def steps(count, *tails):
        return [("step", (count,) + tail, BF, None) for tail in tails]

    moved = ("moved", (slots, some, patches, width), BF, None)
    whole = ("pack", frames.shape, F32, None)
    flops = 2 * tokens * width * (4 * width + 2 * hidden)

    (sent,) = everyone_once(clip_labels, output_grad, moved)
    grad_moved = exchange(sent)

    space_args = [
        ("whole", row(space_gain)),
        ("whole", space_input),
        ("whole", space_output),
        ("whole", row(space_scale)),
        ("whole", space_up),
        ("whole", space_down),
    ]
    time_args = [
        ("whole", row(time_gain)),
        ("whole", time_input),
        ("whole", time_output),
        ("whole", row(time_scale)),
        ("whole", time_up),
        ("whole", time_down),
    ]
    rows_w, rows_3, rows_h = (tokens, width), (tokens, 3 * width), (tokens, hidden)
    spread = ("step", (some, tokens, LANES), F32, None)
    x2, sz0, sinv0, sqkv, sp, so, sz1, sinv1, sh, sslope = shared.call(
        space_forward,
        [("pack", frames)] + space_args,
        [moved]
        + steps(some, rows_w)
        + [spread]
        + steps(some, rows_3, (HEADS, tokens, tokens), rows_w, rows_w)
        + [spread]
        + steps(some, rows_h, rows_h),
        scratch=work_shapes(tokens),
        flops=flops,
        after=(sent,),
    )
    x2, grad_moved = lax.optimization_barrier((x2, grad_moved))
    x2_moved = exchange(x2)

    block_tails = [rows_w, rows_w, rows_w, rows_3, rows_w, rows_h, rows_h, rows_w]
    time_tails = [rows_w, rows_w, rows_w, rows_w, rows_w, rows_h, rows_h, rows_w]
    input_grad, result, *alone = single.call(
        alone_both,
        [("pack", frames), ("pack", output_grad)] + space_args + time_args,
        [whole, whole] + steps(1, *block_tails) + steps(1, *time_tails),
        scratch=[
            pltpu.VMEM((tokens, LANES), F32),
            pltpu.VMEM((tokens, LANES), F32),
            pltpu.VMEM(rows_3, BF),
            pltpu.VMEM((HEADS, tokens, tokens), BF),
            pltpu.VMEM(rows_h, BF),
            pltpu.VMEM(rows_h, BF),
            pltpu.VMEM(rows_w, BF),
        ]
        + work_shapes(tokens),
        flops=6 * flops,
        after=(x2,),
    )
    sz0_one, so_one, se1_one, sgqkv_one, sz1_one, seu_one, sh_one, se2_one = alone[:8]
    tz0_one, to_one, te1_one, tgv_one, tz1_one, teu_one, th_one, te2_one = alone[8:]

    shared_w, shared_3, shared_h = [(some,) + tail for tail in (rows_w, rows_3, rows_h)]
    time_outs = [(x2.shape, BF)] * 2 + [
        (shape, BF)
        for shape in (shared_w, shared_3, shared_w, shared_w, shared_w, shared_h, shared_h, shared_w)
    ]
    square = (some, HEADS, tokens, tokens)
    halves = (slots // 2,) + x2.shape[1:]
    g0_outs = [(halves, BF)] * 2 if hierarchical else [(x2.shape, BF)]
    *g0, out, tz0, tgqkv, to, te1, tz1, teu, th, te2 = manual_call(
        functools.partial(time_kernel, len(g0_outs)),
        (clip_labels, ids),
        [row(time_gain), row(time_scale), x2_moved, grad_moved]
        + [time_input, time_output, time_up, time_down],
        g0_outs + time_outs[1:],
        [(x2.shape, BF)] * 2
        + [(w.shape, BF) for w in (time_input, time_output, time_up, time_down)]
        + time_outs
        + [
            (shared_3, BF),
            (square, BF),
            (shared_h, BF),
            ((some, tokens, tokens), F32),
            (shared_w, BF),
            ((some, 4, tokens, tokens), F32),
            ((some, 2, tokens, CHUNK), BF),
            ((some, 4, tokens, tokens), BF),
            (square, BF),
        ],
        6 + 8 * some + 9,
        small=2,
        after=(sz0_one,),
        flops=3 * some * flops,
    )
    g0_moved = exchange_pieces(g0)
    out, g0_moved = lax.optimization_barrier((out, g0_moved))
    out_moved = exchange(out)

    held_back = ()
    everything = packs * tokens
    feed_shapes = [(1, width // 8), (width // 8, hidden), (hidden // 8, width)]
    attend_shapes = [(1, width // 8), (width // 8, 3 * width), (width // 8, width)]
    time_shared = [tz1, teu, te2, th, tz0, tgqkv, to, te1]
    time_one = [tz1_one, teu_one, te2_one, th_one, tz0_one, tgv_one, to_one, te1_one]
    if hierarchical:
        parts_shapes = [((4, 4, 96, CHUNK), BF)] * 4
        time_terms = manual_call(
            time_weights_kernel,
            ids,
            time_shared + time_one,
            parts_shapes,
            [((everything, a.shape[2]), BF) for a in time_shared] + parts_shapes,
            8 * packs + 20,
            flops=packs * flops,
        )
        time_got = [swap(other, "tm", 8, 1) for other in time_terms[1::2]]
        time_far = far_parts(time_terms[::2], time_got, marker(*g0_moved[2:]))
        held_back = time_far
    else:
        grad_one = jnp.pad(tgv_one, ((0, 0), (0, 0), (2 * width, 0)))
        joined = [joint(a, b) for a, b in zip(time_shared, time_one[:5] + [grad_one] + time_one[6:])]
        time_grads = plain_grads(joined[0], joined[1], joined[3], joined[2], time_up, time_scale)
        time_grads += plain_grads(joined[4], joined[5], joined[6], joined[7], time_input, time_gain)

    space_one = [sz1_one, seu_one, sh_one, se2_one, sz0_one, sgqkv_one, so_one, se1_one]
    whole_shapes = [((everything, a.shape[2]), BF) for a in space_one]
    parts_shapes = [((4, 4, 96, CHUNK), BF)] * 4
    sg1, sgqkv, *weights = manual_call(
        functools.partial(space_kernel, hierarchical, len(g0_moved)),
        ids,
        [row(space_scale), sinv1, *g0_moved, sslope, sz1, space_output, space_up, space_down]
        + [sqkv, sp, sh, sz0, so]
        + space_one,
        [(shared_w, F32), (shared_3, BF)]
        + (parts_shapes if hierarchical else [whole_shapes[i] for i in (1, 3, 7)]),
        [
            (x2.shape, BF),
            (sslope.shape, BF),
            (space_output.shape, BF),
            (space_up.shape, BF),
            (space_down.shape, BF),
            (sqkv.shape, BF),
            (sp.shape, BF),
            (shared_w, BF),
            (shared_w, F32),
            ((some, 4, tokens, tokens), BF),
            (square, BF),
        ]
        + whole_shapes
        + (parts_shapes if hierarchical else []),
        96,
        small=2,
        after=held_back,
        flops=2 * packs * flops,
    )
    held_back = ()
    if hierarchical:
        time_got, sgqkv = lax.optimization_barrier((time_got, sgqkv))
        time_mine = time_terms[::2]
        time_halves, time_near = near_parts(time_mine, time_got, time_far)
        mine = weights[::2]
        got = [swap(other, "tm", 8, 1) for other in weights[1::2]]
        far = far_parts(mine, got, marker(time_near[1]))
        held_back = far
    input_grad, result = shared.call(
        space_back_in,
        [
            ("step", sgqkv),
            ("whole", space_input),
            ("whole", row(space_gain)),
            ("step", sz0),
            ("step", sinv0),
            ("step", sg1),
            ("moved", out_moved),
        ],
        [("pack", frames.shape, F32, input_grad), ("pack", frames.shape, F32, result)],
        flops=flops // 4,
        after=held_back,
    )
    if hierarchical:
        time_halves, input_grad = lax.optimization_barrier((time_halves, input_grad))
        time_rows = stream_rows(time_mine, time_got, time_halves, time_near)
        time_last = z_got(time_rows)
        time_final = add(time_rows[0], *time_last)
        final = z_sum(stream_rows(mine, got, *near_parts(mine, got, far), marker(*time_last)))
        grads = finish_call(
            finish_kernel,
            ids,
            gather_parts(final),
            [(space_up, space_scale), (space_input, space_gain)],
            feed_shapes + attend_shapes,
        )
        feed_grads, attend_grads = grads[:3], grads[3:]
        time_grads = finish_call(
            finish_kernel,
            ids,
            gather_parts(time_final),
            [(time_up, time_scale), (time_input, time_gain)],
            feed_shapes + attend_shapes,
        )
    else:
        have = some * tokens
        seu, se2, se1 = [a[:have].reshape(some, tokens, -1) for a in weights]
        feed_grads = plain_grads(
            joint(sz1, sz1_one),
            joint(seu, seu_one),
            joint(sh, sh_one),
            joint(se2, se2_one),
            space_up,
            space_scale,
        )
        attend_grads = plain_grads(
            joint(sz0, sz0_one),
            joint(sgqkv, sgqkv_one),
            joint(so, so_one),
            joint(se1, se1_one),
            space_input,
            space_gain,
        )
    grads = attend_grads + feed_grads + time_grads[3:] + time_grads[:3]
    return (result, input_grad, *grads)


def joint(shared, one):
    return jnp.concatenate([shared, one]).reshape(-1, shared.shape[-1])


def solution(mesh):
    tokens = P("stream", "tm", None, None)
    vector, matrix = P("tm"), P("tm", None)
    return jax.shard_map(
        functools.partial(per_device, mesh.shape["tm"], mesh.shape["stream"]),
        mesh=mesh,
        in_specs=(tokens,) + (P(),) * 12 + (P("stream", None), tokens),
        out_specs=(tokens, tokens) + (vector, matrix, matrix, vector, matrix, matrix) * 2,
        check_vma=False,
    )
```

```python
import functools

import jax
import jax.numpy as jnp
from jax import lax
from jax.experimental import pallas as pl
from jax.experimental.pallas import tpu as pltpu
from jax.sharding import PartitionSpec as P

HEADS = 8
EPS = 1e-05
GELU_A = 0.7978845608028654
GELU_B = 0.044715
BF = jnp.bfloat16
F32 = jnp.float32
CHUNK = 512
LANES = 128
COST = 1
ROWS = (0, 96, 64, 80, 160, 176)
VMEM = 60 * 1024 * 1024
SMALL_VMEM = 24 * 1024 * 1024


def nn(a, b):
    return jnp.dot(a, b, preferred_element_type=F32)


def nt(a, b):
    return lax.dot_general(a, b, (((1,), (1,)), ((), ())), preferred_element_type=F32)


def tn(a, b):
    return lax.dot_general(a, b, (((0,), (0,)), ((), ())), preferred_element_type=F32)


def unit(values):
    average = jnp.mean(values, axis=-1, keepdims=True)
    centered = values - average
    inverse = lax.rsqrt(jnp.mean(centered * centered, axis=-1, keepdims=True) + EPS)
    return centered * inverse, inverse


def unit_backward(grad, unit_rows, inverse):
    first = jnp.mean(grad, axis=-1, keepdims=True)
    second = jnp.mean(grad * unit_rows, axis=-1, keepdims=True)
    return inverse * (grad - first - unit_rows * second)


def gelu_parts(u):
    square = u * u
    tangent = jnp.tanh(u * (BF(GELU_A) + BF(GELU_A * GELU_B) * square))
    half = BF(0.5) * u
    value = half + half * tangent
    slope = (BF(0.5) + BF(0.5) * tangent) + half * (BF(1.0) - tangent * tangent) * (
        BF(GELU_A) + BF(3.0 * GELU_A * GELU_B) * square
    )
    return value, slope


def head_masks(width):
    lane = lax.broadcasted_iota(jnp.int32, (1, 2 * width), 1)
    low = lane < width
    return low, (low.astype(F32).astype(BF), (1.0 - low.astype(F32)).astype(BF))


def attend_steps(qkv_ref, p_ref, o_ref, bias_ref, s_ref):
    width = qkv_ref.shape[1] // 3
    size = width // HEADS
    _, masks = head_masks(size)

    def lanes(part, head):
        at = part * width + (head // 2) * 2 * size
        return qkv_ref[:, at : at + 2 * size]

    def score(head):
        s_ref[head % 4] = nt(lanes(1, head) * masks[head % 2], lanes(0, head) * BF(size**-0.5))

    def soften(head):
        scores = s_ref[head % 4]
        if bias_ref is not None:
            scores = scores + bias_ref[...]
        e = jnp.exp(scores - jnp.max(scores, axis=0, keepdims=True))
        p_ref[head] = (e * (1.0 / jnp.sum(e, axis=0, keepdims=True))).astype(BF)

    for head in range(0, HEADS, 2):
        if head == 0:
            score(0)
            score(1)
        if head + 2 < HEADS:
            score(head + 2)
            score(head + 3)
        soften(head)
        soften(head + 1)
        yield
    for head in range(0, HEADS, 2):
        v = lanes(2, head).T
        both = jnp.concatenate([nn(v[:size], p_ref[head]), nn(v[size:], p_ref[head + 1])], axis=0)
        o_ref[:, head * size : (head + 2) * size] = both.T.astype(BF)
        yield


def attend_backward_steps(qkv_ref, p_ref, go_ref, out_ref, gp_ref, gs_ref):
    width = qkv_ref.shape[1] // 3
    size = width // HEADS
    _, masks = head_masks(size)

    def lanes(part, head):
        at = part * width + (head // 2) * 2 * size
        return qkv_ref[:, at : at + 2 * size]

    def gos(head):
        return go_ref[:, (head // 2) * 2 * size : (head // 2 + 1) * 2 * size]

    def put(part, head, value):
        at = part * width + head * size
        out_ref[:, at : at + 2 * size] = value.astype(BF)

    def start(head):
        for h in (head, head + 1):
            gp_ref[h % 4] = nt(lanes(2, h) * masks[h % 2], gos(h)).astype(BF)
        g = gos(head)
        put(2, head, nn(p_ref[head], g * masks[0]) + nn(p_ref[head + 1], g * masks[1]))

    def middle(head):
        p = p_ref[head]
        weighted = p * gp_ref[head % 4]
        total = jnp.sum(weighted.astype(F32), axis=0, keepdims=True).astype(BF)
        gs_ref[head] = weighted - p * total

    def finish(head):
        q = lanes(0, head) * BF(size**-0.5)
        k = (lanes(1, head) * BF(size**-0.5)).T
        put(1, head, nn(gs_ref[head], q * masks[0]) + nn(gs_ref[head + 1], q * masks[1]))
        both = jnp.concatenate([nn(k[:size], gs_ref[head]), nn(k[size:], gs_ref[head + 1])], axis=0)
        put(0, head, both.T)

    start(0)
    yield
    for head in range(0, HEADS, 2):
        middle(head)
        middle(head + 1)
        if head + 2 < HEADS:
            start(head + 2)
        if head > 0:
            finish(head - 2)
        yield
    finish(HEADS - 2)


def feed_up_steps(m, up_ref, down_ref, h_ref, slope_ref, u_ref):
    steps = up_ref.shape[1] // CHUNK

    def before(step):
        u_ref[step % 2] = nn(m, up_ref[:, step * CHUNK : (step + 1) * CHUNK]).astype(BF)

    before(0)
    for step in range(steps):
        if step + 1 < steps:
            before(step + 1)
        at = step * CHUNK
        h_ref[:, at : at + CHUNK], slope_ref[:, at : at + CHUNK] = gelu_parts(u_ref[step % 2])
        yield
    return nn(h_ref[...], down_ref[...])


def feed_back_steps(e2, up_ref, down_ref, slope_ref, eu_ref, up_copy=None):
    for at in range(0, up_ref.shape[1], CHUNK):
        gh = nt(e2, down_ref[at : at + CHUNK, :]).astype(BF)
        eu_ref[:, at : at + CHUNK] = gh * slope_ref[:, at : at + CHUNK]
        yield
    if up_copy is not None:
        wait(up_copy)
    return nt(eu_ref[...], up_ref[...])


def whole(steps):
    while True:
        try:
            next(steps)
        except StopIteration as end:
            return end.value


def together(runs):
    while runs:
        runs = [run for run in runs if next(run, "end") != "end"]


def attend_backward(*args):
    whole(attend_backward_steps(*args))


def feed_up(*args):
    return whole(feed_up_steps(*args))


def feed_back(*args):
    return whole(feed_back_steps(*args))


def rows_of(block):
    slots, _, patches, width = block.shape
    return block[:, 0].astype(F32).reshape(slots * patches, width)


def block_of(rows, ref):
    slots, _, patches, width = ref.shape
    ref[:, 0] = rows.reshape(slots, patches, width).astype(ref.dtype)


def work_shapes(tokens):
    return [
        pltpu.VMEM((4, tokens, tokens), F32),
        pltpu.VMEM((2, tokens, CHUNK), BF),
        pltpu.VMEM((4, tokens, tokens), BF),
        pltpu.VMEM((HEADS, tokens, tokens), BF),
    ]


def wide(column):
    return jnp.broadcast_to(column, (column.shape[0], LANES))


def space_steps(x, weights, state, work, waits=((), (), ()), sent=lambda *indices: None):
    gain, w_in, w_out, scale, w_up, w_down = weights
    z0, inv0, qkv, p, o, z1, inv1, h, slope = state
    unit0, inverse0 = unit(x)
    z0[...] = unit0.astype(BF)
    inv0[...] = wide(inverse0)
    sent(0, 1)
    wait(*waits[0])
    qkv[...] = nn((unit0 * gain[...]).astype(BF), w_in[...]).astype(BF)
    sent(2)
    yield
    yield from attend_steps(qkv, p, o, None, work[0])
    sent(3, 4)
    wait(*waits[1])
    r1 = x + nn(o[...], w_out[...])
    unit1, inverse1 = unit(r1)
    z1[...] = unit1.astype(BF)
    inv1[...] = wide(inverse1)
    sent(5, 6)
    m = (unit1 * scale[...]).astype(BF)
    yield
    wait(*waits[2])
    total = yield from feed_up_steps(m, w_up, w_down, h, slope, work[1])
    sent(7, 8)
    return r1 + total


def space_rows(x, weights, state, work):
    return whole(space_steps(x, weights, state, work))


def space_forward(labels, gain, scale, frames_in, w_in_in, w_out_in, w_up_in, w_down_in, *rest):
    outs, (frames, w_in, w_out, w_up, w_down), rest = rest[:10], rest[10:15], rest[15:]
    (x2, *state), (scores, u, semaphores) = rest[:10], rest[10:]
    copies = Copies(semaphores)
    packs = frames.shape[0]
    got = [
        copies.fetch(frames_in.at[pack_at(labels, pack), 0], frames.at[pack])
        for pack in range(packs)
    ]
    waits = [
        [copies.fetch(w_in_in, w_in)],
        [copies.fetch(w_out_in, w_out)],
        [copies.fetch(w_up_in, w_up), copies.fetch(w_down_in, w_down)],
    ]
    weights = gain, w_in, w_out, scale, w_up, w_down

    def run(pack):
        def sent(*indices):
            for index in indices:
                copies.send(state[index].at[pack], outs[1 + index].at[pack])

        wait(got[pack])
        rows = yield from space_steps(
            frames[pack].astype(F32),
            weights,
            [ref.at[pack] for ref in state],
            (scores.at[pack], u.at[pack]),
            waits if pack == 0 else ((), (), ()),
            sent,
        )
        block_of(rows, x2.at[:, pl.ds(pack, 1)])

    together([run(pack) for pack in range(packs)])
    copies.send(x2, outs[0])
    copies.finish()


def build_bias(labels, pack, slots, patches, bias):
    tokens = slots * patches
    row = lax.broadcasted_iota(jnp.int32, (1, tokens), 1)
    column = lax.broadcasted_iota(jnp.int32, (tokens, 1), 0)

    def label_of(position):
        slot = position // patches
        value = jnp.zeros_like(position)
        for f in range(slots):
            value = jnp.where(slot == f, labels[pack, f], value)
        return value

    same_patch = (row % patches) == (column % patches)
    allowed = same_patch & (column <= row) & (label_of(column) == label_of(row))
    bias[...] = jnp.where(allowed, 0.0, -1e30)


def send_moved(copies, ids, held, outs):
    if len(outs) == 1:
        copies.send(held, outs[0])
        return
    for d in range(4):
        at = 2 * (ids[1] ^ d)
        copies.send(held.at[at + ids[0]], outs[0].at[d])
        copies.send(held.at[at + 1 - ids[0]], outs[1].at[d])


def fetch_moved(copies, ids, pieces, held):
    if len(pieces) == 1:
        return [copies.fetch(pieces[0], held)]
    near, far, *others = pieces
    at = 2 * ids[1]
    got = [copies.fetch(near.at[0], held.at[at + ids[0]])]
    got.append(copies.fetch(far.at[0], held.at[at + 1 - ids[0]]))
    for d, piece in enumerate(others, 1):
        at = 2 * (ids[1] ^ d)
        got.append(copies.fetch(piece.at[0], held.at[at + ids[0]]))
        got.append(copies.fetch(piece.at[1], held.at[at + 1 - ids[0]]))
    return got


def exchange_pieces(arrays):
    if len(arrays) == 1:
        return [lax.all_to_all(arrays[0], "tm", split_axis=0, concat_axis=0, tiled=True)]
    near, far = arrays[0], swap(arrays[1], "tm", 8, 1)
    return [near, far] + [swap(jnp.stack([near[d], far[d]]), "tm", 8, 2 * d) for d in range(1, 4)]


def time_kernel(pieces, moved, labels, ids, gain, scale, x2_in, *rest):
    grad_in, rest = rest[:pieces], rest[pieces:]
    (w_in_in, w_out_in, w_up_in, w_down_in), rest = rest[:4], rest[4:]
    g0_outs, outs, rest = rest[:moved], (None,) + rest[moved : moved + 9], rest[moved + 9 :]
    x2, grad, w_in, w_out, w_up, w_down = rest[:6]
    held = rest[6:16]
    g0, out, z0, gqkv, o, e1, z1, eu, h, e2 = held
    qkv, p, slope, bias, go, scores, u, gp, gs = rest[16:25]
    copies = Copies(rest[-1])
    slots, packs, patches, _ = x2.shape
    got_x2, got_in = copies.fetch(x2_in, x2), copies.fetch(w_in_in, w_in)
    got_out, got_up = copies.fetch(w_out_in, w_out), copies.fetch(w_up_in, w_up)
    got_down, got_grad = copies.fetch(w_down_in, w_down), fetch_moved(copies, ids, grad_in, grad)

    def send(index, pack):
        copies.send(held[index].at[pack], outs[index].at[pack])

    def run(pack):
        if pack == 0:
            wait(got_x2)
        build_bias(labels, pack_at(labels, pack), slots, patches, bias.at[pack])
        x = rows_of(x2[:, pack : pack + 1])
        unit0, inverse0 = unit(x)
        z0[pack] = unit0.astype(BF)
        send(2, pack)
        if pack == 0:
            wait(got_in)
        qkv[pack] = nn((unit0 * gain[...]).astype(BF), w_in[...]).astype(BF)
        yield
        yield from attend_steps(qkv.at[pack], p.at[pack], o.at[pack], bias.at[pack], scores.at[pack])
        send(4, pack)
        if pack == 0:
            wait(got_out)
        r1 = x + nn(o[pack], w_out[...])
        unit1, inverse1 = unit(r1)
        z1[pack] = unit1.astype(BF)
        send(6, pack)
        m = (unit1 * scale[...]).astype(BF)
        yield
        if pack == 0:
            wait(got_up, got_down)
        total = yield from feed_up_steps(m, w_up, w_down, h.at[pack], slope.at[pack], u.at[pack])
        send(8, pack)
        block_of(r1 + total, out.at[:, pl.ds(pack, 1)])
        if pack == 0:
            wait(*got_grad)
        g2 = rows_of(grad[:, pack : pack + 1])
        e2[pack] = g2.astype(BF)
        send(9, pack)
        yield
        gm = yield from feed_back_steps(e2[pack], w_up, w_down, slope.at[pack], eu.at[pack])
        send(7, pack)
        g1 = g2 + unit_backward(gm * scale[...], unit1, inverse1)
        e1[pack] = g1.astype(BF)
        send(5, pack)
        go[pack] = nt(e1[pack], w_out[...]).astype(BF)
        yield
        yield from attend_backward_steps(
            qkv.at[pack], p.at[pack], go.at[pack], gqkv.at[pack], gp.at[pack], gs.at[pack]
        )
        send(3, pack)
        gn = nt(gqkv[pack], w_in[...])
        block_of(g1 + unit_backward(gn * gain[...], unit0, inverse0), g0.at[:, pl.ds(pack, 1)])

    together([run(pack) for pack in range(packs)])
    send_moved(copies, ids, g0, g0_outs)
    copies.send(out, outs[1])
    copies.finish()


def alone_both(labels, frames, grad, *rest):
    space, (gain, w_in, w_out, scale, w_up, w_down) = rest[:6], rest[6:12]
    input_grad, out = rest[12:14]
    sz0, so, se1, sgqkv, sz1, seu, sh, se2 = [ref.at[0] for ref in rest[14:22]]
    z0, o, e1, gv, z1, eu, h, e2 = [ref.at[0] for ref in rest[22:30]]
    inv0, inv1, qkv, p, sslope, slope, go, *work = rest[30:]
    state = sz0, inv0, qkv, p, so, sz1, inv1, sh, sslope
    x = space_rows(frames[0, 0].astype(F32), space, state, work)
    width = x.shape[1]
    unit0, inverse0 = unit(x)
    z0[...] = unit0.astype(BF)
    o[...] = nn((unit0 * gain[...]).astype(BF), w_in[:, 2 * width :]).astype(BF)
    r1 = x + nn(o[...], w_out[...])
    unit1, inverse1 = unit(r1)
    z1[...] = unit1.astype(BF)
    m = (unit1 * scale[...]).astype(BF)
    out[0, 0] = r1 + feed_up(m, w_up, w_down, h, slope, work[1])
    e2[...] = grad[0, 0]
    g2 = grad[0, 0].astype(F32)
    gm = feed_back(e2[...], w_up, w_down, slope, eu)
    g1 = g2 + unit_backward(gm * scale[...], unit1, inverse1)
    e1[...] = g1.astype(BF)
    gv[...] = nt(e1[...], w_out[...]).astype(BF)
    gn = nt(gv[...], w_in[:, 2 * width :])
    g2 = g1 + unit_backward(gn * gain[...], unit0, inverse0)
    gain, w_in, w_out, scale, w_up, w_down = space
    se2[...] = g2.astype(BF)
    gm = feed_back(se2[...], w_up, w_down, sslope, seu)
    g1 = g2 + unit_backward(gm * scale[...], sz1[...].astype(F32), inv1[:, :1])
    se1[...] = g1.astype(BF)
    go[...] = nt(se1[...], w_out[...]).astype(BF)
    attend_backward(qkv, p, go, sgqkv, work[2], work[3])
    gn = nt(sgqkv[...], w_in[...])
    input_grad[0, 0] = g1 + unit_backward(gn * gain[...], sz0[...].astype(F32), inv0[:, :1])


def space_back_in(labels, gqkv, w_in, gain, z0, inv0, g1, moved, input_grad, result):
    gn = nt(gqkv[0], w_in[...])
    grad = unit_backward(gn * gain[...], z0[0].astype(F32), inv0[0, :, :1])
    input_grad[0, 0] = g1[0] + grad
    result[0, 0] = rows_of(moved[...])


class Copies:
    def __init__(self, semaphores):
        self.semaphores, self.count, self.sent = semaphores, 0, []

    def fetch(self, source, target):
        copy = pltpu.make_async_copy(source, target, self.semaphores.at[self.count])
        self.count += 1
        copy.start()
        return copy

    def send(self, source, target):
        self.sent.append(self.fetch(source, target))

    def finish(self):
        for copy in self.sent:
            copy.wait()


def wait(*copies):
    for copy in copies:
        copy.wait()


def space_kernel(hierarchical, pieces, ids, scale, inv1, *rest):
    g2_in, rest = rest[:pieces], rest[pieces:]
    (slope_in, z1_in, w_out_in, w_up_in, w_down_in, qkv_in, p_in), rest = rest[:7], rest[7:]
    shared, one, rest = rest[:3], rest[3:11], rest[11:]
    (g1_out, gqkv_out), outs, scratch = rest[:2], rest[2 : 6 if hierarchical else 5], rest[6 if hierarchical else 5 :]
    g2, slope, w_out, w_up, w_down, qkv, p, go, g1, gp, gs = scratch[:11]
    z1, eu, h, e2, z0, gqkv, o, e1 = whole = scratch[11:19]
    copies = Copies(scratch[-1])
    packs, tokens, _ = g1.shape
    have = packs * tokens
    got_g2 = fetch_moved(copies, ids, g2_in, g2)
    got_down = copies.fetch(w_down_in, w_down)
    got_slope = [copies.fetch(slope_in.at[pack], slope.at[pack]) for pack in range(packs)]
    got_up = copies.fetch(w_up_in, w_up)
    got_z1 = [
        copies.fetch(z1_in.at[pack], z1.at[pl.ds(pack * tokens, tokens)]) for pack in range(packs)
    ]
    got_out = copies.fetch(w_out_in, w_out)
    got_attend = [
        (copies.fetch(qkv_in.at[pack], qkv.at[pack]), copies.fetch(p_in.at[pack], p.at[pack]))
        for pack in range(packs)
    ]
    got_rest = []
    if hierarchical:
        for source, target in zip(shared, (h, z0, o)):
            for pack in range(packs):
                rows = pl.ds(pack * tokens, tokens)
                got_rest.append(copies.fetch(source.at[pack], target.at[rows]))
        for source, target in zip(one, whole):
            got_rest.append(copies.fetch(source.at[0], target.at[pl.ds(have, tokens)]))
    wait(*got_g2)

    def run(pack):
        rows = slice(pack * tokens, (pack + 1) * tokens)
        e2[rows] = rows_of(g2[:, pack : pack + 1]).astype(BF)
        if pack == 0:
            wait(got_down)
        wait(got_slope[pack])
        gm = yield from feed_back_steps(e2[rows], w_up, w_down, slope.at[pack], eu.at[rows], got_up if pack == 0 else None)
        if pack == 0:
            wait(*got_z1, got_out)
        grad = unit_backward(gm * scale[...], z1[rows].astype(F32), inv1[pack, :, :1])
        total = rows_of(g2[:, pack : pack + 1]) + grad
        g1[pack] = total
        e1[rows] = total.astype(BF)
        go[pack] = nt(e1[rows], w_out[...]).astype(BF)
        copies.send(g1.at[pack], g1_out.at[pack])
        yield
        wait(*got_attend[pack])
        rows = pl.ds(pack * tokens, tokens)
        yield from attend_backward_steps(
            qkv.at[pack], p.at[pack], go.at[pack], gqkv.at[rows], gp.at[pack], gs.at[pack]
        )
        copies.send(gqkv.at[rows], gqkv_out.at[pack])

    together([run(pack) for pack in range(packs)])
    if hierarchical:
        wait(*got_rest)
        one = Halves(copies, ids, scratch[19:21], outs[:2], x_high=True)
        two = Halves(copies, ids, scratch[21:23], outs[2:])
        up_tiles(one, z1, eu, 0)
        down_tiles(two, e2, h, 0)
        attend_tiles([one, one, two, two], z0, o, gqkv, e1, [64, 80, 64, 80], gqkv.shape[0])
    else:
        for source, target in zip((eu, e2, e1), outs):
            copies.send(source, target)
    copies.finish()


def to_send(labels, ids, grad, *rest):
    *outs, held = rest
    slots, places, patches, _ = held.shape
    for place in range(places):
        rows = grad[pack_at(labels, place), 0].astype(F32)
        held[:, place] = rows.reshape(slots, patches, -1).astype(BF)
    if len(outs) == 1:
        outs[0][...] = held[...]
        return
    for d in range(4):
        at = 2 * (ids[1] ^ d)
        outs[0][d] = held[at + ids[0]]
        outs[1][d] = held[at + 1 - ids[0]]


def pack_at(labels, place):
    packs, slots = labels.shape
    alone = packs - 1
    for pack in range(packs - 2, -1, -1):
        alone = jnp.where(labels[pack, slots - 1] == slots - 1, pack, alone)
    return jnp.where(place == packs - 1, alone, place + (place >= alone).astype(jnp.int32))


def without(kernel, first, count):
    def call(*refs):
        return kernel(*refs[:first], *refs[first + count :])

    return call


class Packs:
    def __init__(self, labels, first, count):
        self.labels, self.first, self.count = labels, first, count

    def call(self, kernel, args, outs, scratch=(), flops=0, after=()):
        first, last = self.first, self.labels.shape[0] - 2
        scalars = (self.labels,)

        def spec(kind, shape):
            rank = len(shape)
            if kind == "whole":
                return pl.BlockSpec(shape, lambda i, *s: (0,) * rank)
            if kind == "pack":
                return pl.BlockSpec(
                    (1,) + tuple(shape[1:]), lambda i, s: (pack_at(s, first + i),) + (0,) * (rank - 1)
                )
            if kind == "place":
                return pl.BlockSpec(
                    (1,) + tuple(shape[1:]), lambda i, *s: (first + i,) + (0,) * (rank - 1)
                )
            if kind == "step":
                return pl.BlockSpec(
                    (1,) + tuple(shape[1:]), lambda i, *s: (i,) + (0,) * (rank - 1)
                )
            if kind == "moved":
                return pl.BlockSpec(
                    (shape[0], 1, shape[2], shape[3]),
                    lambda i, *s: (0, jnp.minimum(i, last), 0, 0),
                )
            return pl.BlockSpec(memory_space=pl.ANY)

        in_specs = [spec(kind, array.shape) for kind, array in args]
        operands = [array for _, array in args]
        aliases = {}
        for index, (kind, shape, dtype, into) in enumerate(outs):
            if into is not None:
                aliases[len(scalars) + len(operands)] = index
                operands.append(into)
                in_specs.append(pl.BlockSpec(memory_space=pl.ANY))
        for array in after:
            operands.append(array)
            in_specs.append(pl.BlockSpec(memory_space=pl.ANY))
        moved = sum(a.size * a.dtype.itemsize for a in operands)
        unread = len(operands) - len(args)
        return pl.pallas_call(
            without(kernel, len(scalars) + len(args), unread),
            out_shape=[jax.ShapeDtypeStruct(shape, dtype) for _, shape, dtype, _ in outs],
            grid_spec=pltpu.PrefetchScalarGridSpec(
                num_scalar_prefetch=len(scalars),
                grid=(self.count,),
                in_specs=in_specs,
                out_specs=[spec(kind, shape) for kind, shape, _, _ in outs],
                scratch_shapes=list(scratch),
            ),
            input_output_aliases=aliases,
            compiler_params=pltpu.CompilerParams(
                vmem_limit_bytes=VMEM, dimension_semantics=("arbitrary",)
            ),
            cost_estimate=pl.CostEstimate(
                flops=int(flops * self.count * COST), bytes_accessed=int(moved * COST), transcendentals=0
            ),
        )(*scalars, *operands)


class Halves:
    def __init__(self, copies, ids, held, outs, x_high=False):
        self.copies, self.held, self.outs = copies, held, outs
        self.first, self.z, self.s, self.x_high = ids[0] == 0, ids[1], ids[2], x_high

    def part(self, s):
        if s is None:
            return slice(None)
        part = s ^ self.s
        return (part & 1) * 2 + (part >> 1) if self.x_high else part

    def put(self, s, z, at, even, odd):
        rows = slice(at, at + even.shape[0])
        self.held[0][self.part(s), z ^ self.z, rows] = jnp.where(self.first, even, odd)
        self.held[1][self.part(s), z ^ self.z, rows] = jnp.where(self.first, odd, even)

    def send(self, s, z, at, rows):
        index = self.part(s), slice(None) if z is None else z ^ self.z, pl.ds(at, rows)
        for ref, out in zip(self.held, self.outs):
            self.copies.send(ref.at[index], out.at[index])


def up_tiles(place, z1, eu, at):
    for step in range(4):
        tile = tn(z1[...], eu[:, step * CHUNK : (step + 1) * CHUNK]).astype(BF)
        for z in range(4):
            row = 128 * z
            place.put(step, z, at, tile[row : row + 64], tile[row + 64 : row + 128])
        place.send(step, None, at, 64)


def down_tiles(place, e2, h, at):
    for step in range(4):
        tile = tn(e2[...], h[:, step * CHUNK : (step + 1) * CHUNK]).astype(BF)
        for s in range(4):
            upper, lower = tile[128 * s : 128 * s + 64], tile[128 * s + 64 : 128 * s + 128]
            even = jnp.concatenate([upper[:, :256], lower[:, :256]], axis=1)
            odd = jnp.concatenate([upper[:, 256:], lower[:, 256:]], axis=1)
            place.put(s, step, at, even, odd)
        place.send(None, step, at, 64)


def attend_tiles(places, z0, o, gqkv, e1, ats, depth):
    for step, (place, at) in enumerate(zip(places, ats)):
        if step == 3:
            tile = tn(o[...], e1[...])
        else:
            rows = gqkv.shape[0] if step == 2 else depth
            tile = tn(z0[:rows], gqkv[:rows, step * CHUNK : (step + 1) * CHUNK])
        tile = tile.astype(BF)
        for z in range(4):
            for s in range(4):
                row = 128 * z + 16 * s
                place.put(s, z, at, tile[row : row + 16], tile[row + 64 : row + 80])
        if step % 2:
            place.send(None, None, at - 16, 32)


def time_weights_kernel(ids, *rest):
    names = 8
    shared, single, outs, scratch = rest[:names], rest[names : 2 * names], rest[16:20], rest[20:]
    z1, eu, e2, h, z0, gqkv, o, e1 = scratch[:names]
    copies = Copies(scratch[-1])
    one = Halves(copies, ids, scratch[8:10], outs[:2], x_high=True)
    two = Halves(copies, ids, scratch[10:12], outs[2:])
    packs, tokens, _ = shared[0].shape
    have = packs * tokens
    got = []
    for source, last, target in zip(shared, single, scratch):
        wide_target = target.at[pl.ds(have, tokens)]
        if last.shape[2] < target.shape[1]:
            wide_target = target.at[pl.ds(have, tokens), pl.ds(target.shape[1] - last.shape[2], last.shape[2])]
        got.append(
            [copies.fetch(source.at[pack], target.at[pl.ds(pack * tokens, tokens)]) for pack in range(packs)]
            + [copies.fetch(last.at[0], wide_target)]
        )
    wait(*got[0], *got[1], *got[2], *got[3])
    up_tiles(one, z1, eu, 0)
    down_tiles(two, e2, h, 0)
    wait(*got[4], *got[5], *got[6], *got[7])
    attend_tiles([one, one, two, two], z0, o, gqkv, e1, [64, 80, 64, 80], have)
    copies.finish()


def manual_call(kernel, ids, args, outs, scratch, semaphores, small=0, after=(), flops=0):
    anywhere = pl.BlockSpec(memory_space=pl.ANY)
    scalars = ids if isinstance(ids, tuple) else (ids,)
    return pl.pallas_call(
        without(kernel, len(scalars) + len(args), len(after)),
        out_shape=[jax.ShapeDtypeStruct(shape, dtype) for shape, dtype in outs],
        in_specs=[pl.BlockSpec(memory_space=pltpu.SMEM)] * len(scalars)
        + [pl.BlockSpec(memory_space=pltpu.VMEM)] * small
        + [anywhere] * (len(args) - small + len(after)),
        out_specs=[anywhere] * len(outs),
        scratch_shapes=[pltpu.VMEM(shape, dtype) for shape, dtype in scratch]
        + [pltpu.SemaphoreType.DMA((semaphores,))],
        compiler_params=pltpu.CompilerParams(vmem_limit_bytes=VMEM),
        cost_estimate=pl.CostEstimate(
            flops=int(flops * COST), bytes_accessed=0, transcendentals=0
        ),
    )(*scalars, *args, *after)


def swap(array, axis, size, mask):
    return lax.ppermute(array, axis, [(i, i ^ mask) for i in range(size)])


def add(*terms):
    total = terms[0].astype(F32)
    for term in terms[1:]:
        total = total + term.astype(F32)
    return total.astype(BF)


def far_parts(mine, got, note):
    return [add(a[2:], b[2:], note) for a, b in zip(mine, got)]


def near_parts(mine, got, far):
    halves = [swap(far[0], "stream", 4, 1), swap(far[1], "stream", 4, 2)]
    return halves, [add(a[1], b[1], half[1]) for a, b, half in zip(mine, got, halves)]


def stream_rows(mine, got, halves, near, *note):
    last = [swap(near[0], "stream", 4, 2), swap(near[1], "stream", 4, 1)]
    terms = list(zip(mine, got, halves, last))
    return [
        jnp.concatenate([add(a[0][d], b[0][d], half[0][d], end[d], *note) for a, b, half, end in terms])
        for d in range(4)
    ]


def z_got(rows):
    return [swap(rows[d], "tm", 8, 2 * d) for d in range(1, 4)]


def z_sum(rows):
    return add(rows[0], *[swap(rows[d], "tm", 8, 2 * d) for d in range(1, 4)])


def gather_parts(final):
    return [final] + [swap(final, "stream", 4, d) for d in range(1, 4)]


def marker(*arrays):
    def kernel(*refs):
        refs[-1][...] = jnp.zeros_like(refs[-1])

    return pl.pallas_call(
        kernel,
        out_shape=jax.ShapeDtypeStruct((1, CHUNK), F32),
        in_specs=[pl.BlockSpec(memory_space=pl.ANY)] * len(arrays),
        out_specs=pl.BlockSpec(memory_space=pltpu.VMEM),
        cost_estimate=pl.CostEstimate(flops=10**12, bytes_accessed=10**8, transcendentals=0),
    )(*arrays)


def as_row(col):
    size = col.shape[0]
    eye = lax.broadcasted_iota(jnp.int32, (size, size), 0) == lax.broadcasted_iota(
        jnp.int32, (size, size), 1
    )
    return jnp.sum(jnp.where(eye, col, 0.0), axis=0, keepdims=True)


def own_rows(ids, vector):
    shape = 64, vector.shape[1]
    row = lax.broadcasted_iota(jnp.int32, shape, 0) + 64 * (2 * ids[1] + ids[0])
    lane = lax.broadcasted_iota(jnp.int32, shape, 1)
    return jnp.sum(jnp.where(row == lane, vector[...], 0.0), axis=1, keepdims=True)


def finish_kernel(ids, p0, p1, p2, p3, w_up, scale, w_in, gain, *outs):
    scale_grad, up_grad, down_grad, gain_grad, in_grad, out_grad = outs
    up_at, down_at, *in_at, out_at = ROWS
    for d, piece in enumerate((p0, p1, p2, p3)):
        s = ids[2] ^ d
        up_grad[:, pl.ds(pl.multiple_of(512 * s, 512), 512)] = piece[up_at : up_at + 64].astype(F32)
        lower = piece[down_at : down_at + 64].astype(F32)
        whole = jnp.concatenate([lower[:, :256], lower[:, 256:]], axis=0)
        down_grad[:, pl.ds(pl.multiple_of(128 * s, 128), 128)] = whole.T
        rows = pl.ds(pl.multiple_of(16 * s, 16), 16)
        for third, at in enumerate(in_at):
            in_grad[rows, 512 * third : 512 * third + 512] = piece[at : at + 16].astype(F32)
        out_grad[rows, :] = piece[out_at : out_at + 16].astype(F32)
    for grad, weight, factor, vector_grad in (
        (up_grad, w_up, scale, scale_grad),
        (in_grad, w_in, gain, gain_grad),
    ):
        total = grad[...]
        vector_grad[...] = as_row(jnp.sum(total * weight[...].astype(F32), axis=1, keepdims=True))
        grad[...] = total * own_rows(ids, factor)


def finish_call(kernel, ids, pieces, pairs, outs):
    whole = pl.BlockSpec(pieces[0].shape, lambda i, *s: (0, 0))
    specs, operands = [], []
    for weight, vector in pairs:
        height = weight.shape[0] // 8
        specs += [
            pl.BlockSpec((height, weight.shape[1]), lambda i, s: (2 * s[1] + s[0], 0)),
            pl.BlockSpec((1, vector.size), lambda i, *s: (0, 0)),
        ]
        operands += [weight, vector.reshape(1, -1)]
    results = pl.pallas_call(
        kernel,
        out_shape=[jax.ShapeDtypeStruct(shape, F32) for shape in outs],
        grid_spec=pltpu.PrefetchScalarGridSpec(
            num_scalar_prefetch=1,
            grid=(1,),
            in_specs=[whole] * 4 + specs,
            out_specs=[pl.BlockSpec(shape, lambda i, *s: (0, 0)) for shape in outs],
        ),
        compiler_params=pltpu.CompilerParams(vmem_limit_bytes=SMALL_VMEM),
    )(ids, *pieces, *operands)
    return [a.reshape(-1) if a.shape[0] == 1 else a for a in results]


def plain_grads(z, grads, left, right, weight, vector):
    product = tn(z, grads)
    vector_grad = jnp.sum(product * weight.astype(F32), axis=1)
    sums = []
    for term in (vector_grad, product * vector[:, None], tn(left, right)):
        share = lax.psum_scatter(term.astype(BF), "tm", scatter_dimension=0, tiled=True)
        sums.append(lax.psum(share, "stream").astype(F32))
    return sums


def grad_to_send(labels, ids, grad, shape, outs):
    space = pl.BlockSpec(memory_space=pltpu.VMEM)
    return pl.pallas_call(
        to_send,
        out_shape=[jax.ShapeDtypeStruct(shape, dtype) for shape, dtype in outs],
        in_specs=[pl.BlockSpec(memory_space=pltpu.SMEM)] * 2 + [space],
        out_specs=[space] * len(outs),
        scratch_shapes=[pltpu.VMEM(shape, BF)],
        compiler_params=pltpu.CompilerParams(vmem_limit_bytes=VMEM),
    )(labels, ids, grad)


def per_device(
    ranks,
    streams,
    frames,
    space_gain,
    space_input,
    space_output,
    space_scale,
    space_up,
    space_down,
    time_gain,
    time_input,
    time_output,
    time_scale,
    time_up,
    time_down,
    clip_labels,
    output_grad,
):
    packs, _, tokens, width = frames.shape
    slots = clip_labels.shape[1]
    patches = tokens // ranks
    hidden = space_up.shape[1]
    some = packs - 1
    hierarchical = (ranks, streams) == (8, 4)
    tm = lax.axis_index("tm")
    ids = jnp.stack([tm % 2, tm // 2, lax.axis_index("stream")]).astype(jnp.int32)
    shared = Packs(clip_labels, 0, some)
    single = Packs(clip_labels, some, 1)

    def row(vector):
        return vector.reshape(1, -1)

    def exchange(array):
        return lax.all_to_all(array, "tm", split_axis=0, concat_axis=0, tiled=True)

    def steps(count, *tails):
        return [("step", (count,) + tail, BF, None) for tail in tails]

    moved = ("moved", (slots, some, patches, width), BF, None)
    whole = ("pack", frames.shape, F32, None)
    flops = 2 * tokens * width * (4 * width + 2 * hidden)

    shape = moved[1]
    halves = (slots // 2,) + shape[1:]
    moved_outs = [(halves, BF)] * 2 if hierarchical else [(shape, BF)]
    sent = grad_to_send(clip_labels, ids, output_grad, shape, moved_outs)
    grad_moved = exchange_pieces(sent)

    space_args = [
        ("whole", row(space_gain)),
        ("whole", space_input),
        ("whole", space_output),
        ("whole", row(space_scale)),
        ("whole", space_up),
        ("whole", space_down),
    ]
    time_args = [
        ("whole", row(time_gain)),
        ("whole", time_input),
        ("whole", time_output),
        ("whole", row(time_scale)),
        ("whole", time_up),
        ("whole", time_down),
    ]
    rows_w, rows_3, rows_h = (tokens, width), (tokens, 3 * width), (tokens, hidden)
    shared_w, shared_3, shared_h = [(some,) + tail for tail in (rows_w, rows_3, rows_h)]
    square, spread = (some, HEADS, tokens, tokens), (some, tokens, LANES)
    space_outs = [
        (shape, BF),
        (shared_w, BF),
        (spread, F32),
        (shared_3, BF),
        (square, BF),
        (shared_w, BF),
        (shared_w, BF),
        (spread, F32),
        (shared_h, BF),
        (shared_h, BF),
    ]
    x2, sz0, sinv0, sqkv, sp, so, sz1, sinv1, sh, sslope = manual_call(
        space_forward,
        clip_labels,
        [row(space_gain), row(space_scale), frames]
        + [space_input, space_output, space_up, space_down],
        space_outs,
        [(shared_w, BF)]
        + [(w.shape, BF) for w in (space_input, space_output, space_up, space_down)]
        + space_outs
        + [((some, 4, tokens, tokens), F32), ((some, 2, tokens, CHUNK), BF)],
        5 + 10 * some,
        small=2,
        after=sent,
        flops=some * flops,
    )
    x2_moved = exchange(x2)
    held_back = grad_moved
    if hierarchical:
        held_back = [marker(*grad_moved[2:])]

    block_tails = [rows_w, rows_w, rows_w, rows_3, rows_w, rows_h, rows_h, rows_w]
    time_tails = [rows_w, rows_w, rows_w, rows_w, rows_w, rows_h, rows_h, rows_w]
    input_grad, result, *alone = single.call(
        alone_both,
        [("pack", frames), ("pack", output_grad)] + space_args + time_args,
        [whole, whole] + steps(1, *block_tails) + steps(1, *time_tails),
        scratch=[
            pltpu.VMEM((tokens, LANES), F32),
            pltpu.VMEM((tokens, LANES), F32),
            pltpu.VMEM(rows_3, BF),
            pltpu.VMEM((HEADS, tokens, tokens), BF),
            pltpu.VMEM(rows_h, BF),
            pltpu.VMEM(rows_h, BF),
            pltpu.VMEM(rows_w, BF),
        ]
        + work_shapes(tokens),
        flops=6 * flops,
        after=(x2, *held_back),
    )
    sz0_one, so_one, se1_one, sgqkv_one, sz1_one, seu_one, sh_one, se2_one = alone[:8]
    tz0_one, to_one, te1_one, tgv_one, tz1_one, teu_one, th_one, te2_one = alone[8:]

    time_outs = [(x2.shape, BF)] * 2 + [
        (shape, BF)
        for shape in (shared_w, shared_3, shared_w, shared_w, shared_w, shared_h, shared_h, shared_w)
    ]
    *g0, out, tz0, tgqkv, to, te1, tz1, teu, th, te2 = manual_call(
        functools.partial(time_kernel, len(grad_moved), len(moved_outs)),
        (clip_labels, ids),
        [row(time_gain), row(time_scale), x2_moved, *grad_moved]
        + [time_input, time_output, time_up, time_down],
        moved_outs + time_outs[1:],
        [(x2.shape, BF)] * 2
        + [(w.shape, BF) for w in (time_input, time_output, time_up, time_down)]
        + time_outs
        + [
            (shared_3, BF),
            (square, BF),
            (shared_h, BF),
            ((some, tokens, tokens), F32),
            (shared_w, BF),
            ((some, 4, tokens, tokens), F32),
            ((some, 2, tokens, CHUNK), BF),
            ((some, 4, tokens, tokens), BF),
            (square, BF),
        ],
        14 + 8 * some + 9,
        small=2,
        after=(sz0_one,),
        flops=3 * some * flops,
    )
    g0_moved = exchange_pieces(g0)
    out, g0_moved = lax.optimization_barrier((out, g0_moved))
    out_moved = exchange(out)

    held_back = ()
    everything = packs * tokens
    feed_shapes = [(1, width // 8), (width // 8, hidden), (hidden // 8, width)]
    attend_shapes = [(1, width // 8), (width // 8, 3 * width), (width // 8, width)]
    time_shared = [tz1, teu, te2, th, tz0, tgqkv, to, te1]
    time_one = [tz1_one, teu_one, te2_one, th_one, tz0_one, tgv_one, to_one, te1_one]
    if hierarchical:
        parts_shapes = [((4, 4, 96, CHUNK), BF)] * 4
        time_terms = manual_call(
            time_weights_kernel,
            ids,
            time_shared + time_one,
            parts_shapes,
            [((everything, a.shape[2]), BF) for a in time_shared] + parts_shapes,
            8 * packs + 20,
            flops=packs * flops,
        )
        time_got = [swap(other, "tm", 8, 1) for other in time_terms[1::2]]
        time_far = far_parts(time_terms[::2], time_got, marker(*g0_moved[2:]))
        held_back = time_far
    else:
        grad_one = jnp.pad(tgv_one, ((0, 0), (0, 0), (2 * width, 0)))
        joined = [joint(a, b) for a, b in zip(time_shared, time_one[:5] + [grad_one] + time_one[6:])]
        time_grads = plain_grads(joined[0], joined[1], joined[3], joined[2], time_up, time_scale)
        time_grads += plain_grads(joined[4], joined[5], joined[6], joined[7], time_input, time_gain)

    space_one = [sz1_one, seu_one, sh_one, se2_one, sz0_one, sgqkv_one, so_one, se1_one]
    whole_shapes = [((everything, a.shape[2]), BF) for a in space_one]
    parts_shapes = [((4, 4, 96, CHUNK), BF)] * 4
    sg1, sgqkv, *weights = manual_call(
        functools.partial(space_kernel, hierarchical, len(g0_moved)),
        ids,
        [row(space_scale), sinv1, *g0_moved, sslope, sz1, space_output, space_up, space_down]
        + [sqkv, sp, sh, sz0, so]
        + space_one,
        [(shared_w, F32), (shared_3, BF)]
        + (parts_shapes if hierarchical else [whole_shapes[i] for i in (1, 3, 7)]),
        [
            (x2.shape, BF),
            (sslope.shape, BF),
            (space_output.shape, BF),
            (space_up.shape, BF),
            (space_down.shape, BF),
            (sqkv.shape, BF),
            (sp.shape, BF),
            (shared_w, BF),
            (shared_w, F32),
            ((some, 4, tokens, tokens), BF),
            (square, BF),
        ]
        + whole_shapes
        + (parts_shapes if hierarchical else []),
        96,
        small=2,
        after=held_back,
        flops=2 * packs * flops,
    )
    held_back = ()
    if hierarchical:
        time_got, sgqkv = lax.optimization_barrier((time_got, sgqkv))
        time_mine = time_terms[::2]
        time_halves, time_near = near_parts(time_mine, time_got, time_far)
        mine = weights[::2]
        got = [swap(other, "tm", 8, 1) for other in weights[1::2]]
        far = far_parts(mine, got, marker(time_near[1]))
        held_back = far
    input_grad, result = shared.call(
        space_back_in,
        [
            ("step", sgqkv),
            ("whole", space_input),
            ("whole", row(space_gain)),
            ("step", sz0),
            ("step", sinv0),
            ("step", sg1),
            ("moved", out_moved),
        ],
        [("pack", frames.shape, F32, input_grad), ("pack", frames.shape, F32, result)],
        flops=flops // 4,
        after=held_back,
    )
    if hierarchical:
        time_halves, input_grad = lax.optimization_barrier((time_halves, input_grad))
        time_rows = stream_rows(time_mine, time_got, time_halves, time_near)
        time_last = z_got(time_rows)
        time_final = add(time_rows[0], *time_last)
        final = z_sum(stream_rows(mine, got, *near_parts(mine, got, far), marker(*time_last)))
        grads = finish_call(
            finish_kernel,
            ids,
            gather_parts(final),
            [(space_up, space_scale), (space_input, space_gain)],
            feed_shapes + attend_shapes,
        )
        feed_grads, attend_grads = grads[:3], grads[3:]
        time_grads = finish_call(
            finish_kernel,
            ids,
            gather_parts(time_final),
            [(time_up, time_scale), (time_input, time_gain)],
            feed_shapes + attend_shapes,
        )
    else:
        have = some * tokens
        seu, se2, se1 = [a[:have].reshape(some, tokens, -1) for a in weights]
        feed_grads = plain_grads(
            joint(sz1, sz1_one),
            joint(seu, seu_one),
            joint(sh, sh_one),
            joint(se2, se2_one),
            space_up,
            space_scale,
        )
        attend_grads = plain_grads(
            joint(sz0, sz0_one),
            joint(sgqkv, sgqkv_one),
            joint(so, so_one),
            joint(se1, se1_one),
            space_input,
            space_gain,
        )
    grads = attend_grads + feed_grads + time_grads[3:] + time_grads[:3]
    return (result, input_grad, *grads)


def joint(shared, one):
    return jnp.concatenate([shared, one]).reshape(-1, shared.shape[-1])


def solution(mesh):
    tokens = P("stream", "tm", None, None)
    vector, matrix = P("tm"), P("tm", None)
    return jax.shard_map(
        functools.partial(per_device, mesh.shape["tm"], mesh.shape["stream"]),
        mesh=mesh,
        in_specs=(tokens,) + (P(),) * 12 + (P("stream", None), tokens),
        out_specs=(tokens, tokens) + (vector, matrix, matrix, vector, matrix, matrix) * 2,
        check_vma=False,
    )
```

```python
import functools

import jax
import jax.numpy as jnp
from jax import lax
from jax.experimental import pallas as pl
from jax.experimental.pallas import tpu as pltpu
from jax.sharding import PartitionSpec as P

HEADS = 8
EPS = 1e-05
GELU_A = 0.7978845608028654
GELU_B = 0.044715
BF = jnp.bfloat16
F32 = jnp.float32
CHUNK = 512
LANES = 128
COST = 1
ROWS = (0, 96, 64, 80, 160, 176)
VMEM = 60 * 1024 * 1024
SMALL_VMEM = 24 * 1024 * 1024


def nn(a, b):
    return jnp.dot(a, b, preferred_element_type=F32)


def nt(a, b):
    return lax.dot_general(a, b, (((1,), (1,)), ((), ())), preferred_element_type=F32)


def tn(a, b):
    return lax.dot_general(a, b, (((0,), (0,)), ((), ())), preferred_element_type=F32)


def unit(values):
    average = jnp.mean(values, axis=-1, keepdims=True)
    centered = values - average
    inverse = lax.rsqrt(jnp.mean(centered * centered, axis=-1, keepdims=True) + EPS)
    return centered * inverse, inverse


def unit_backward(grad, unit_rows, inverse):
    first = jnp.mean(grad, axis=-1, keepdims=True)
    second = jnp.mean(grad * unit_rows, axis=-1, keepdims=True)
    return inverse * (grad - first - unit_rows * second)


def gelu_parts(u):
    square = u * u
    tangent = jnp.tanh(u * (BF(GELU_A) + BF(GELU_A * GELU_B) * square))
    half = BF(0.5) * u
    value = half + half * tangent
    slope = (BF(0.5) + BF(0.5) * tangent) + half * (BF(1.0) - tangent * tangent) * (
        BF(GELU_A) + BF(3.0 * GELU_A * GELU_B) * square
    )
    return value, slope


def head_masks(width):
    lane = lax.broadcasted_iota(jnp.int32, (1, 2 * width), 1)
    low = lane < width
    return low, (low.astype(F32).astype(BF), (1.0 - low.astype(F32)).astype(BF))


def attend_steps(qkv_ref, p_ref, o_ref, bias_ref, s_ref):
    width = qkv_ref.shape[1] // 3
    size = width // HEADS
    _, masks = head_masks(size)

    def lanes(part, head):
        at = part * width + (head // 2) * 2 * size
        return qkv_ref[:, at : at + 2 * size]

    def score(head):
        s_ref[head % 4] = nt(lanes(1, head) * masks[head % 2], lanes(0, head) * BF(size**-0.5))

    def soften(head):
        scores = s_ref[head % 4]
        if bias_ref is not None:
            scores = scores + bias_ref[...]
        e = jnp.exp(scores - jnp.max(scores, axis=0, keepdims=True))
        p_ref[head] = (e * (1.0 / jnp.sum(e, axis=0, keepdims=True))).astype(BF)

    for head in range(0, HEADS, 2):
        if head == 0:
            score(0)
            score(1)
        if head + 2 < HEADS:
            score(head + 2)
            score(head + 3)
        soften(head)
        soften(head + 1)
        yield
    for head in range(0, HEADS, 2):
        v = lanes(2, head).T
        both = jnp.concatenate([nn(v[:size], p_ref[head]), nn(v[size:], p_ref[head + 1])], axis=0)
        o_ref[:, head * size : (head + 2) * size] = both.T.astype(BF)
        yield


def attend_backward_steps(qkv_ref, p_ref, go_ref, out_ref, gp_ref, gs_ref):
    width = qkv_ref.shape[1] // 3
    size = width // HEADS
    _, masks = head_masks(size)

    def lanes(part, head):
        at = part * width + (head // 2) * 2 * size
        return qkv_ref[:, at : at + 2 * size]

    def gos(head):
        return go_ref[:, (head // 2) * 2 * size : (head // 2 + 1) * 2 * size]

    def put(part, head, value):
        at = part * width + head * size
        out_ref[:, at : at + 2 * size] = value.astype(BF)

    def start(head):
        for h in (head, head + 1):
            gp_ref[h % 4] = nt(lanes(2, h) * masks[h % 2], gos(h)).astype(BF)
        g = gos(head)
        put(2, head, nn(p_ref[head], g * masks[0]) + nn(p_ref[head + 1], g * masks[1]))

    def middle(head):
        p = p_ref[head]
        weighted = p * gp_ref[head % 4]
        total = jnp.sum(weighted.astype(F32), axis=0, keepdims=True).astype(BF)
        gs_ref[head] = weighted - p * total

    def finish(head):
        q = lanes(0, head) * BF(size**-0.5)
        k = (lanes(1, head) * BF(size**-0.5)).T
        put(1, head, nn(gs_ref[head], q * masks[0]) + nn(gs_ref[head + 1], q * masks[1]))
        both = jnp.concatenate([nn(k[:size], gs_ref[head]), nn(k[size:], gs_ref[head + 1])], axis=0)
        put(0, head, both.T)

    start(0)
    yield
    for head in range(0, HEADS, 2):
        middle(head)
        middle(head + 1)
        if head + 2 < HEADS:
            start(head + 2)
        if head > 0:
            finish(head - 2)
        yield
    finish(HEADS - 2)


def feed_up_steps(m, up_ref, down_ref, h_ref, slope_ref, u_ref):
    steps = up_ref.shape[1] // CHUNK

    def before(step):
        u_ref[step % 2] = nn(m, up_ref[:, step * CHUNK : (step + 1) * CHUNK]).astype(BF)

    before(0)
    for step in range(steps):
        if step + 1 < steps:
            before(step + 1)
        at = step * CHUNK
        h_ref[:, at : at + CHUNK], slope_ref[:, at : at + CHUNK] = gelu_parts(u_ref[step % 2])
        yield
    return nn(h_ref[...], down_ref[...])


def feed_back_steps(e2, up_ref, down_ref, slope_ref, eu_ref, up_copy=None):
    for at in range(0, up_ref.shape[1], CHUNK):
        gh = nt(e2, down_ref[at : at + CHUNK, :]).astype(BF)
        eu_ref[:, at : at + CHUNK] = gh * slope_ref[:, at : at + CHUNK]
        yield
    if up_copy is not None:
        wait(up_copy)
    return nt(eu_ref[...], up_ref[...])


def whole(steps):
    while True:
        try:
            next(steps)
        except StopIteration as end:
            return end.value


def together(runs):
    while runs:
        runs = [run for run in runs if next(run, "end") != "end"]


def attend_backward(*args):
    whole(attend_backward_steps(*args))


def feed_up(*args):
    return whole(feed_up_steps(*args))


def feed_back(*args):
    return whole(feed_back_steps(*args))


def rows_of(block):
    slots, _, patches, width = block.shape
    return block[:, 0].astype(F32).reshape(slots * patches, width)


def block_of(rows, ref):
    slots, _, patches, width = ref.shape
    ref[:, 0] = rows.reshape(slots, patches, width).astype(ref.dtype)


def work_shapes(tokens):
    return [
        pltpu.VMEM((4, tokens, tokens), F32),
        pltpu.VMEM((2, tokens, CHUNK), BF),
        pltpu.VMEM((4, tokens, tokens), BF),
        pltpu.VMEM((HEADS, tokens, tokens), BF),
    ]


def wide(column):
    return jnp.broadcast_to(column, (column.shape[0], LANES))


def space_steps(x, weights, state, work, arrive=lambda index: None, sent=lambda *indices: None):
    gain, w_in, w_out, scale, w_up, w_down = weights
    z0, inv0, qkv, p, o, z1, inv1, h, slope = state
    unit0, inverse0 = unit(x)
    z0[...] = unit0.astype(BF)
    inv0[...] = wide(inverse0)
    sent(0, 1)
    arrive(0)
    qkv[...] = nn((unit0 * gain[...]).astype(BF), w_in[...]).astype(BF)
    sent(2)
    yield
    yield from attend_steps(qkv, p, o, None, work[0])
    sent(3, 4)
    arrive(1)
    r1 = x + nn(o[...], w_out[...])
    unit1, inverse1 = unit(r1)
    z1[...] = unit1.astype(BF)
    inv1[...] = wide(inverse1)
    sent(5, 6)
    m = (unit1 * scale[...]).astype(BF)
    yield
    arrive(2)
    total = yield from feed_up_steps(m, w_up, w_down, h, slope, work[1])
    sent(7, 8)
    return r1 + total


def space_rows(x, weights, state, work):
    return whole(space_steps(x, weights, state, work))


def space_forward(labels, gain, scale, frames_in, w_in_in, w_out_in, w_up_in, w_down_in, *rest):
    outs, (frames, w_in, w_out, w_up, w_down), rest = rest[:10], rest[10:15], rest[15:]
    (x2, *state), (scores, u, semaphores) = rest[:10], rest[10:]
    copies = Copies(semaphores)
    packs = frames.shape[0]
    got = [
        copies.fetch(frames_in.at[pack_at(labels, pack), 0], frames.at[pack])
        for pack in range(packs)
    ]
    waits = [
        [copies.fetch(w_in_in, w_in)],
        [copies.fetch(w_out_in, w_out)],
        [copies.fetch(w_up_in, w_up), copies.fetch(w_down_in, w_down)],
    ]
    weights = gain, w_in, w_out, scale, w_up, w_down

    base = copies.count

    def leaving(index, pack):
        semaphore = semaphores.at[base + index * packs + pack]
        return pltpu.make_async_copy(state[index].at[pack], outs[1 + index].at[pack], semaphore)

    def first(pack, arrivals):
        pl.when(pack == 0)(lambda: wait(*arrivals))

    def run(pack, carry):
        def sent(*indices):
            for index in indices:
                leaving(index, pack).start()

        steps = space_steps(
            frames[pack].astype(F32),
            weights,
            [ref.at[pack] for ref in state],
            (scores, u),
            lambda index: first(pack, waits[index]),
            sent,
        )
        block_of(whole(steps), x2.at[:, pl.ds(pack, 1)])
        return carry

    wait(*got)
    lax.fori_loop(0, packs, run, 0)
    copies.count = base + len(state) * packs
    copies.send(x2, outs[0])
    for index in range(len(state)):
        for pack in range(packs):
            leaving(index, pack).wait()
    copies.finish()


def build_bias(labels, pack, slots, patches, bias):
    tokens = slots * patches
    row = lax.broadcasted_iota(jnp.int32, (1, tokens), 1)
    column = lax.broadcasted_iota(jnp.int32, (tokens, 1), 0)

    def label_of(position):
        slot = position // patches
        value = jnp.zeros_like(position)
        for f in range(slots):
            value = jnp.where(slot == f, labels[pack, f], value)
        return value

    same_patch = (row % patches) == (column % patches)
    allowed = same_patch & (column <= row) & (label_of(column) == label_of(row))
    bias[...] = jnp.where(allowed, 0.0, -1e30)


def send_moved(copies, ids, held, outs):
    if len(outs) == 1:
        copies.send(held, outs[0])
        return
    for d in range(4):
        at = 2 * (ids[1] ^ d)
        copies.send(held.at[at + ids[0]], outs[0].at[d])
        copies.send(held.at[at + 1 - ids[0]], outs[1].at[d])


def fetch_moved(copies, ids, pieces, held):
    if len(pieces) == 1:
        return [copies.fetch(pieces[0], held)]
    near, far, *others = pieces
    at = 2 * ids[1]
    got = [copies.fetch(near.at[0], held.at[at + ids[0]])]
    got.append(copies.fetch(far.at[0], held.at[at + 1 - ids[0]]))
    for d, piece in enumerate(others, 1):
        at = 2 * (ids[1] ^ d)
        got.append(copies.fetch(piece.at[0], held.at[at + ids[0]]))
        got.append(copies.fetch(piece.at[1], held.at[at + 1 - ids[0]]))
    return got


def exchange_pieces(arrays):
    if len(arrays) == 1:
        return [lax.all_to_all(arrays[0], "tm", split_axis=0, concat_axis=0, tiled=True)]
    near, far = arrays[0], swap(arrays[1], "tm", 8, 1)
    return [near, far] + [swap(jnp.stack([near[d], far[d]]), "tm", 8, 2 * d) for d in range(1, 4)]


def time_kernel(pieces, moved, labels, ids, gain, scale, x2_in, *rest):
    grad_in, rest = rest[:pieces], rest[pieces:]
    (w_in_in, w_out_in, w_up_in, w_down_in), rest = rest[:4], rest[4:]
    g0_outs, outs, rest = rest[:moved], (None,) + rest[moved : moved + 9], rest[moved + 9 :]
    x2, grad, w_in, w_out, w_up, w_down = rest[:6]
    held = rest[6:16]
    g0, out, z0, gqkv, o, e1, z1, eu, h, e2 = held
    qkv, p, slope, bias, go, scores, u, gp, gs = rest[16:25]
    copies = Copies(rest[-1])
    slots, packs, patches, _ = x2.shape
    got_x2, got_in = copies.fetch(x2_in, x2), copies.fetch(w_in_in, w_in)
    got_out, got_up = copies.fetch(w_out_in, w_out), copies.fetch(w_up_in, w_up)
    got_down, got_grad = copies.fetch(w_down_in, w_down), fetch_moved(copies, ids, grad_in, grad)

    def send(index, pack):
        copies.send(held[index].at[pack], outs[index].at[pack])

    def run(pack):
        if pack == 0:
            wait(got_x2)
        build_bias(labels, pack_at(labels, pack), slots, patches, bias.at[pack])
        x = rows_of(x2[:, pack : pack + 1])
        unit0, inverse0 = unit(x)
        z0[pack] = unit0.astype(BF)
        send(2, pack)
        if pack == 0:
            wait(got_in)
        qkv[pack] = nn((unit0 * gain[...]).astype(BF), w_in[...]).astype(BF)
        yield
        yield from attend_steps(qkv.at[pack], p.at[pack], o.at[pack], bias.at[pack], scores.at[pack])
        send(4, pack)
        if pack == 0:
            wait(got_out)
        r1 = x + nn(o[pack], w_out[...])
        unit1, inverse1 = unit(r1)
        z1[pack] = unit1.astype(BF)
        send(6, pack)
        m = (unit1 * scale[...]).astype(BF)
        yield
        if pack == 0:
            wait(got_up, got_down)
        total = yield from feed_up_steps(m, w_up, w_down, h.at[pack], slope.at[pack], u.at[pack])
        send(8, pack)
        block_of(r1 + total, out.at[:, pl.ds(pack, 1)])
        if pack == 0:
            wait(*got_grad)
        g2 = rows_of(grad[:, pack : pack + 1])
        e2[pack] = g2.astype(BF)
        send(9, pack)
        yield
        gm = yield from feed_back_steps(e2[pack], w_up, w_down, slope.at[pack], eu.at[pack])
        send(7, pack)
        g1 = g2 + unit_backward(gm * scale[...], unit1, inverse1)
        e1[pack] = g1.astype(BF)
        send(5, pack)
        go[pack] = nt(e1[pack], w_out[...]).astype(BF)
        yield
        yield from attend_backward_steps(
            qkv.at[pack], p.at[pack], go.at[pack], gqkv.at[pack], gp.at[pack], gs.at[pack]
        )
        send(3, pack)
        gn = nt(gqkv[pack], w_in[...])
        block_of(g1 + unit_backward(gn * gain[...], unit0, inverse0), g0.at[:, pl.ds(pack, 1)])

    together([run(pack) for pack in range(packs)])
    send_moved(copies, ids, g0, g0_outs)
    copies.send(out, outs[1])
    copies.finish()


def alone_both(labels, frames, grad, *rest):
    space, (gain, w_in, w_out, scale, w_up, w_down) = rest[:6], rest[6:12]
    input_grad, out = rest[12:14]
    sz0, so, se1, sgqkv, sz1, seu, sh, se2 = [ref.at[0] for ref in rest[14:22]]
    z0, o, e1, gv, z1, eu, h, e2 = [ref.at[0] for ref in rest[22:30]]
    inv0, inv1, qkv, p, sslope, slope, go, *work = rest[30:]
    state = sz0, inv0, qkv, p, so, sz1, inv1, sh, sslope
    x = space_rows(frames[0, 0].astype(F32), space, state, work)
    width = x.shape[1]
    unit0, inverse0 = unit(x)
    z0[...] = unit0.astype(BF)
    o[...] = nn((unit0 * gain[...]).astype(BF), w_in[:, 2 * width :]).astype(BF)
    r1 = x + nn(o[...], w_out[...])
    unit1, inverse1 = unit(r1)
    z1[...] = unit1.astype(BF)
    m = (unit1 * scale[...]).astype(BF)
    out[0, 0] = r1 + feed_up(m, w_up, w_down, h, slope, work[1])
    e2[...] = grad[0, 0]
    g2 = grad[0, 0].astype(F32)
    gm = feed_back(e2[...], w_up, w_down, slope, eu)
    g1 = g2 + unit_backward(gm * scale[...], unit1, inverse1)
    e1[...] = g1.astype(BF)
    gv[...] = nt(e1[...], w_out[...]).astype(BF)
    gn = nt(gv[...], w_in[:, 2 * width :])
    g2 = g1 + unit_backward(gn * gain[...], unit0, inverse0)
    gain, w_in, w_out, scale, w_up, w_down = space
    se2[...] = g2.astype(BF)
    gm = feed_back(se2[...], w_up, w_down, sslope, seu)
    g1 = g2 + unit_backward(gm * scale[...], sz1[...].astype(F32), inv1[:, :1])
    se1[...] = g1.astype(BF)
    go[...] = nt(se1[...], w_out[...]).astype(BF)
    attend_backward(qkv, p, go, sgqkv, work[2], work[3])
    gn = nt(sgqkv[...], w_in[...])
    input_grad[0, 0] = g1 + unit_backward(gn * gain[...], sz0[...].astype(F32), inv0[:, :1])


def space_back_in(labels, gqkv, w_in, gain, z0, inv0, g1, moved, input_grad, result):
    gn = nt(gqkv[0], w_in[...])
    grad = unit_backward(gn * gain[...], z0[0].astype(F32), inv0[0, :, :1])
    input_grad[0, 0] = g1[0] + grad
    result[0, 0] = rows_of(moved[...])


class Copies:
    def __init__(self, semaphores):
        self.semaphores, self.count, self.sent = semaphores, 0, []

    def fetch(self, source, target):
        copy = pltpu.make_async_copy(source, target, self.semaphores.at[self.count])
        self.count += 1
        copy.start()
        return copy

    def send(self, source, target):
        self.sent.append(self.fetch(source, target))

    def finish(self):
        for copy in self.sent:
            copy.wait()


def wait(*copies):
    for copy in copies:
        copy.wait()


def space_kernel(hierarchical, pieces, ids, scale, inv1, *rest):
    g2_in, rest = rest[:pieces], rest[pieces:]
    (slope_in, z1_in, w_out_in, w_up_in, w_down_in, qkv_in, p_in), rest = rest[:7], rest[7:]
    shared, one, rest = rest[:3], rest[3:11], rest[11:]
    (g1_out, gqkv_out), outs, scratch = rest[:2], rest[2 : 6 if hierarchical else 5], rest[6 if hierarchical else 5 :]
    g2, slope, w_out, w_up, w_down, qkv, p, go, g1, gp, gs = scratch[:11]
    z1, eu, h, e2, z0, gqkv, o, e1 = whole = scratch[11:19]
    copies = Copies(scratch[-1])
    packs, tokens, _ = g1.shape
    have = packs * tokens
    got_g2 = fetch_moved(copies, ids, g2_in, g2)
    got_down = copies.fetch(w_down_in, w_down)
    got_slope = [copies.fetch(slope_in.at[pack], slope.at[pack]) for pack in range(packs)]
    got_up = copies.fetch(w_up_in, w_up)
    got_z1 = [
        copies.fetch(z1_in.at[pack], z1.at[pl.ds(pack * tokens, tokens)]) for pack in range(packs)
    ]
    got_out = copies.fetch(w_out_in, w_out)
    got_attend = [
        (copies.fetch(qkv_in.at[pack], qkv.at[pack]), copies.fetch(p_in.at[pack], p.at[pack]))
        for pack in range(packs)
    ]
    got_rest = []
    if hierarchical:
        for source, target in zip(shared, (h, z0, o)):
            for pack in range(packs):
                rows = pl.ds(pack * tokens, tokens)
                got_rest.append(copies.fetch(source.at[pack], target.at[rows]))
        for source, target in zip(one, whole):
            got_rest.append(copies.fetch(source.at[0], target.at[pl.ds(have, tokens)]))
    wait(*got_g2)

    def run(pack):
        rows = slice(pack * tokens, (pack + 1) * tokens)
        e2[rows] = rows_of(g2[:, pack : pack + 1]).astype(BF)
        if pack == 0:
            wait(got_down)
        wait(got_slope[pack])
        gm = yield from feed_back_steps(e2[rows], w_up, w_down, slope.at[pack], eu.at[rows], got_up if pack == 0 else None)
        if pack == 0:
            wait(*got_z1, got_out)
        grad = unit_backward(gm * scale[...], z1[rows].astype(F32), inv1[pack, :, :1])
        total = rows_of(g2[:, pack : pack + 1]) + grad
        g1[pack] = total
        e1[rows] = total.astype(BF)
        go[pack] = nt(e1[rows], w_out[...]).astype(BF)
        copies.send(g1.at[pack], g1_out.at[pack])
        yield
        wait(*got_attend[pack])
        rows = pl.ds(pack * tokens, tokens)
        yield from attend_backward_steps(
            qkv.at[pack], p.at[pack], go.at[pack], gqkv.at[rows], gp.at[pack], gs.at[pack]
        )
        copies.send(gqkv.at[rows], gqkv_out.at[pack])

    together([run(pack) for pack in range(packs)])
    if hierarchical:
        wait(*got_rest)
        one = Halves(copies, ids, scratch[19:21], outs[:2], x_high=True)
        two = Halves(copies, ids, scratch[21:23], outs[2:])
        up_tiles(one, z1, eu, 0)
        down_tiles(two, e2, h, 0)
        attend_tiles([one, one, two, two], z0, o, gqkv, e1, [64, 80, 64, 80], gqkv.shape[0])
    else:
        for source, target in zip((eu, e2, e1), outs):
            copies.send(source, target)
    copies.finish()


def to_send(labels, ids, grad, *rest):
    *outs, held = rest
    slots, places, patches, _ = held.shape
    for place in range(places):
        rows = grad[pack_at(labels, place), 0].astype(F32)
        held[:, place] = rows.reshape(slots, patches, -1).astype(BF)
    if len(outs) == 1:
        outs[0][...] = held[...]
        return
    for d in range(4):
        at = 2 * (ids[1] ^ d)
        outs[0][d] = held[at + ids[0]]
        outs[1][d] = held[at + 1 - ids[0]]


def pack_at(labels, place):
    packs, slots = labels.shape
    alone = packs - 1
    for pack in range(packs - 2, -1, -1):
        alone = jnp.where(labels[pack, slots - 1] == slots - 1, pack, alone)
    return jnp.where(place == packs - 1, alone, place + (place >= alone).astype(jnp.int32))


def without(kernel, first, count):
    def call(*refs):
        return kernel(*refs[:first], *refs[first + count :])

    return call


class Packs:
    def __init__(self, labels, first, count):
        self.labels, self.first, self.count = labels, first, count

    def call(self, kernel, args, outs, scratch=(), flops=0, after=()):
        first, last = self.first, self.labels.shape[0] - 2
        scalars = (self.labels,)

        def spec(kind, shape):
            rank = len(shape)
            if kind == "whole":
                return pl.BlockSpec(shape, lambda i, *s: (0,) * rank)
            if kind == "pack":
                return pl.BlockSpec(
                    (1,) + tuple(shape[1:]), lambda i, s: (pack_at(s, first + i),) + (0,) * (rank - 1)
                )
            if kind == "place":
                return pl.BlockSpec(
                    (1,) + tuple(shape[1:]), lambda i, *s: (first + i,) + (0,) * (rank - 1)
                )
            if kind == "step":
                return pl.BlockSpec(
                    (1,) + tuple(shape[1:]), lambda i, *s: (i,) + (0,) * (rank - 1)
                )
            if kind == "moved":
                return pl.BlockSpec(
                    (shape[0], 1, shape[2], shape[3]),
                    lambda i, *s: (0, jnp.minimum(i, last), 0, 0),
                )
            return pl.BlockSpec(memory_space=pl.ANY)

        in_specs = [spec(kind, array.shape) for kind, array in args]
        operands = [array for _, array in args]
        aliases = {}
        for index, (kind, shape, dtype, into) in enumerate(outs):
            if into is not None:
                aliases[len(scalars) + len(operands)] = index
                operands.append(into)
                in_specs.append(pl.BlockSpec(memory_space=pl.ANY))
        for array in after:
            operands.append(array)
            in_specs.append(pl.BlockSpec(memory_space=pl.ANY))
        moved = sum(a.size * a.dtype.itemsize for a in operands)
        unread = len(operands) - len(args)
        return pl.pallas_call(
            without(kernel, len(scalars) + len(args), unread),
            out_shape=[jax.ShapeDtypeStruct(shape, dtype) for _, shape, dtype, _ in outs],
            grid_spec=pltpu.PrefetchScalarGridSpec(
                num_scalar_prefetch=len(scalars),
                grid=(self.count,),
                in_specs=in_specs,
                out_specs=[spec(kind, shape) for kind, shape, _, _ in outs],
                scratch_shapes=list(scratch),
            ),
            input_output_aliases=aliases,
            compiler_params=pltpu.CompilerParams(
                vmem_limit_bytes=VMEM, dimension_semantics=("arbitrary",)
            ),
            cost_estimate=pl.CostEstimate(
                flops=int(flops * self.count * COST), bytes_accessed=int(moved * COST), transcendentals=0
            ),
        )(*scalars, *operands)


class Halves:
    def __init__(self, copies, ids, held, outs, x_high=False):
        self.copies, self.held, self.outs = copies, held, outs
        self.first, self.z, self.s, self.x_high = ids[0] == 0, ids[1], ids[2], x_high

    def part(self, s):
        if s is None:
            return slice(None)
        part = s ^ self.s
        return (part & 1) * 2 + (part >> 1) if self.x_high else part

    def put(self, s, z, at, even, odd):
        rows = slice(at, at + even.shape[0])
        self.held[0][self.part(s), z ^ self.z, rows] = jnp.where(self.first, even, odd)
        self.held[1][self.part(s), z ^ self.z, rows] = jnp.where(self.first, odd, even)

    def send(self, s, z, at, rows):
        index = self.part(s), slice(None) if z is None else z ^ self.z, pl.ds(at, rows)
        for ref, out in zip(self.held, self.outs):
            self.copies.send(ref.at[index], out.at[index])


def up_tiles(place, z1, eu, at):
    for step in range(4):
        tile = tn(z1[...], eu[:, step * CHUNK : (step + 1) * CHUNK]).astype(BF)
        for z in range(4):
            row = 128 * z
            place.put(step, z, at, tile[row : row + 64], tile[row + 64 : row + 128])
        place.send(step, None, at, 64)


def down_tiles(place, e2, h, at):
    for step in range(4):
        tile = tn(e2[...], h[:, step * CHUNK : (step + 1) * CHUNK]).astype(BF)
        for s in range(4):
            upper, lower = tile[128 * s : 128 * s + 64], tile[128 * s + 64 : 128 * s + 128]
            even = jnp.concatenate([upper[:, :256], lower[:, :256]], axis=1)
            odd = jnp.concatenate([upper[:, 256:], lower[:, 256:]], axis=1)
            place.put(s, step, at, even, odd)
        place.send(None, step, at, 64)


def attend_tiles(places, z0, o, gqkv, e1, ats, depth):
    for step, (place, at) in enumerate(zip(places, ats)):
        if step == 3:
            tile = tn(o[...], e1[...])
        else:
            rows = gqkv.shape[0] if step == 2 else depth
            tile = tn(z0[:rows], gqkv[:rows, step * CHUNK : (step + 1) * CHUNK])
        tile = tile.astype(BF)
        for z in range(4):
            for s in range(4):
                row = 128 * z + 16 * s
                place.put(s, z, at, tile[row : row + 16], tile[row + 64 : row + 80])
        if step % 2:
            place.send(None, None, at - 16, 32)


def time_weights_kernel(ids, *rest):
    names = 8
    shared, single, outs, scratch = rest[:names], rest[names : 2 * names], rest[16:20], rest[20:]
    z1, eu, e2, h, z0, gqkv, o, e1 = scratch[:names]
    copies = Copies(scratch[-1])
    one = Halves(copies, ids, scratch[8:10], outs[:2], x_high=True)
    two = Halves(copies, ids, scratch[10:12], outs[2:])
    packs, tokens, _ = shared[0].shape
    have = packs * tokens
    got = []
    for source, last, target in zip(shared, single, scratch):
        wide_target = target.at[pl.ds(have, tokens)]
        if last.shape[2] < target.shape[1]:
            wide_target = target.at[pl.ds(have, tokens), pl.ds(target.shape[1] - last.shape[2], last.shape[2])]
        got.append(
            [copies.fetch(source.at[pack], target.at[pl.ds(pack * tokens, tokens)]) for pack in range(packs)]
            + [copies.fetch(last.at[0], wide_target)]
        )
    wait(*got[0], *got[1], *got[2], *got[3])
    up_tiles(one, z1, eu, 0)
    down_tiles(two, e2, h, 0)
    wait(*got[4], *got[5], *got[6], *got[7])
    attend_tiles([one, one, two, two], z0, o, gqkv, e1, [64, 80, 64, 80], have)
    copies.finish()


def manual_call(kernel, ids, args, outs, scratch, semaphores, small=0, after=(), flops=0):
    anywhere = pl.BlockSpec(memory_space=pl.ANY)
    scalars = ids if isinstance(ids, tuple) else (ids,)
    return pl.pallas_call(
        without(kernel, len(scalars) + len(args), len(after)),
        out_shape=[jax.ShapeDtypeStruct(shape, dtype) for shape, dtype in outs],
        in_specs=[pl.BlockSpec(memory_space=pltpu.SMEM)] * len(scalars)
        + [pl.BlockSpec(memory_space=pltpu.VMEM)] * small
        + [anywhere] * (len(args) - small + len(after)),
        out_specs=[anywhere] * len(outs),
        scratch_shapes=[pltpu.VMEM(shape, dtype) for shape, dtype in scratch]
        + [pltpu.SemaphoreType.DMA((semaphores,))],
        compiler_params=pltpu.CompilerParams(vmem_limit_bytes=VMEM),
        cost_estimate=pl.CostEstimate(
            flops=int(flops * COST), bytes_accessed=0, transcendentals=0
        ),
    )(*scalars, *args, *after)


def swap(array, axis, size, mask):
    return lax.ppermute(array, axis, [(i, i ^ mask) for i in range(size)])


def add(*terms):
    total = terms[0].astype(F32)
    for term in terms[1:]:
        total = total + term.astype(F32)
    return total.astype(BF)


def far_parts(mine, got, note):
    return [add(a[2:], b[2:], note) for a, b in zip(mine, got)]


def near_parts(mine, got, far):
    halves = [swap(far[0], "stream", 4, 1), swap(far[1], "stream", 4, 2)]
    return halves, [add(a[1], b[1], half[1]) for a, b, half in zip(mine, got, halves)]


def stream_rows(mine, got, halves, near, *note):
    last = [swap(near[0], "stream", 4, 2), swap(near[1], "stream", 4, 1)]
    terms = list(zip(mine, got, halves, last))
    return [
        jnp.concatenate([add(a[0][d], b[0][d], half[0][d], end[d], *note) for a, b, half, end in terms])
        for d in range(4)
    ]


def z_got(rows):
    return [swap(rows[d], "tm", 8, 2 * d) for d in range(1, 4)]


def z_sum(rows):
    return add(rows[0], *[swap(rows[d], "tm", 8, 2 * d) for d in range(1, 4)])


def gather_parts(final):
    return [final] + [swap(final, "stream", 4, d) for d in range(1, 4)]


def marker(*arrays):
    def kernel(*refs):
        refs[-1][...] = jnp.zeros_like(refs[-1])

    return pl.pallas_call(
        kernel,
        out_shape=jax.ShapeDtypeStruct((1, CHUNK), F32),
        in_specs=[pl.BlockSpec(memory_space=pl.ANY)] * len(arrays),
        out_specs=pl.BlockSpec(memory_space=pltpu.VMEM),
        cost_estimate=pl.CostEstimate(flops=10**12, bytes_accessed=10**8, transcendentals=0),
    )(*arrays)


def as_row(col):
    size = col.shape[0]
    eye = lax.broadcasted_iota(jnp.int32, (size, size), 0) == lax.broadcasted_iota(
        jnp.int32, (size, size), 1
    )
    return jnp.sum(jnp.where(eye, col, 0.0), axis=0, keepdims=True)


def own_rows(ids, vector):
    shape = 64, vector.shape[1]
    row = lax.broadcasted_iota(jnp.int32, shape, 0) + 64 * (2 * ids[1] + ids[0])
    lane = lax.broadcasted_iota(jnp.int32, shape, 1)
    return jnp.sum(jnp.where(row == lane, vector[...], 0.0), axis=1, keepdims=True)


def finish_kernel(ids, p0, p1, p2, p3, w_up, scale, w_in, gain, *outs):
    scale_grad, up_grad, down_grad, gain_grad, in_grad, out_grad = outs
    up_at, down_at, *in_at, out_at = ROWS
    for d, piece in enumerate((p0, p1, p2, p3)):
        s = ids[2] ^ d
        up_grad[:, pl.ds(pl.multiple_of(512 * s, 512), 512)] = piece[up_at : up_at + 64].astype(F32)
        lower = piece[down_at : down_at + 64].astype(F32)
        whole = jnp.concatenate([lower[:, :256], lower[:, 256:]], axis=0)
        down_grad[:, pl.ds(pl.multiple_of(128 * s, 128), 128)] = whole.T
        rows = pl.ds(pl.multiple_of(16 * s, 16), 16)
        for third, at in enumerate(in_at):
            in_grad[rows, 512 * third : 512 * third + 512] = piece[at : at + 16].astype(F32)
        out_grad[rows, :] = piece[out_at : out_at + 16].astype(F32)
    for grad, weight, factor, vector_grad in (
        (up_grad, w_up, scale, scale_grad),
        (in_grad, w_in, gain, gain_grad),
    ):
        total = grad[...]
        vector_grad[...] = as_row(jnp.sum(total * weight[...].astype(F32), axis=1, keepdims=True))
        grad[...] = total * own_rows(ids, factor)


def finish_call(kernel, ids, pieces, pairs, outs):
    whole = pl.BlockSpec(pieces[0].shape, lambda i, *s: (0, 0))
    specs, operands = [], []
    for weight, vector in pairs:
        height = weight.shape[0] // 8
        specs += [
            pl.BlockSpec((height, weight.shape[1]), lambda i, s: (2 * s[1] + s[0], 0)),
            pl.BlockSpec((1, vector.size), lambda i, *s: (0, 0)),
        ]
        operands += [weight, vector.reshape(1, -1)]
    results = pl.pallas_call(
        kernel,
        out_shape=[jax.ShapeDtypeStruct(shape, F32) for shape in outs],
        grid_spec=pltpu.PrefetchScalarGridSpec(
            num_scalar_prefetch=1,
            grid=(1,),
            in_specs=[whole] * 4 + specs,
            out_specs=[pl.BlockSpec(shape, lambda i, *s: (0, 0)) for shape in outs],
        ),
        compiler_params=pltpu.CompilerParams(vmem_limit_bytes=SMALL_VMEM),
    )(ids, *pieces, *operands)
    return [a.reshape(-1) if a.shape[0] == 1 else a for a in results]


def plain_grads(z, grads, left, right, weight, vector):
    product = tn(z, grads)
    vector_grad = jnp.sum(product * weight.astype(F32), axis=1)
    sums = []
    for term in (vector_grad, product * vector[:, None], tn(left, right)):
        share = lax.psum_scatter(term.astype(BF), "tm", scatter_dimension=0, tiled=True)
        sums.append(lax.psum(share, "stream").astype(F32))
    return sums


def grad_to_send(labels, ids, grad, shape, outs):
    space = pl.BlockSpec(memory_space=pltpu.VMEM)
    return pl.pallas_call(
        to_send,
        out_shape=[jax.ShapeDtypeStruct(shape, dtype) for shape, dtype in outs],
        in_specs=[pl.BlockSpec(memory_space=pltpu.SMEM)] * 2 + [space],
        out_specs=[space] * len(outs),
        scratch_shapes=[pltpu.VMEM(shape, BF)],
        compiler_params=pltpu.CompilerParams(vmem_limit_bytes=VMEM),
    )(labels, ids, grad)


def per_device(
    ranks,
    streams,
    frames,
    space_gain,
    space_input,
    space_output,
    space_scale,
    space_up,
    space_down,
    time_gain,
    time_input,
    time_output,
    time_scale,
    time_up,
    time_down,
    clip_labels,
    output_grad,
):
    packs, _, tokens, width = frames.shape
    slots = clip_labels.shape[1]
    patches = tokens // ranks
    hidden = space_up.shape[1]
    some = packs - 1
    hierarchical = (ranks, streams) == (8, 4)
    tm = lax.axis_index("tm")
    ids = jnp.stack([tm % 2, tm // 2, lax.axis_index("stream")]).astype(jnp.int32)
    shared = Packs(clip_labels, 0, some)
    single = Packs(clip_labels, some, 1)

    def row(vector):
        return vector.reshape(1, -1)

    def exchange(array):
        return lax.all_to_all(array, "tm", split_axis=0, concat_axis=0, tiled=True)

    def steps(count, *tails):
        return [("step", (count,) + tail, BF, None) for tail in tails]

    moved = ("moved", (slots, some, patches, width), BF, None)
    whole = ("pack", frames.shape, F32, None)
    flops = 2 * tokens * width * (4 * width + 2 * hidden)

    shape = moved[1]
    halves = (slots // 2,) + shape[1:]
    moved_outs = [(halves, BF)] * 2 if hierarchical else [(shape, BF)]
    sent = grad_to_send(clip_labels, ids, output_grad, shape, moved_outs)
    grad_moved = exchange_pieces(sent)

    space_args = [
        ("whole", row(space_gain)),
        ("whole", space_input),
        ("whole", space_output),
        ("whole", row(space_scale)),
        ("whole", space_up),
        ("whole", space_down),
    ]
    time_args = [
        ("whole", row(time_gain)),
        ("whole", time_input),
        ("whole", time_output),
        ("whole", row(time_scale)),
        ("whole", time_up),
        ("whole", time_down),
    ]
    rows_w, rows_3, rows_h = (tokens, width), (tokens, 3 * width), (tokens, hidden)
    shared_w, shared_3, shared_h = [(some,) + tail for tail in (rows_w, rows_3, rows_h)]
    square, spread = (some, HEADS, tokens, tokens), (some, tokens, LANES)
    space_outs = [
        (shape, BF),
        (shared_w, BF),
        (spread, F32),
        (shared_3, BF),
        (square, BF),
        (shared_w, BF),
        (shared_w, BF),
        (spread, F32),
        (shared_h, BF),
        (shared_h, BF),
    ]
    x2, sz0, sinv0, sqkv, sp, so, sz1, sinv1, sh, sslope = manual_call(
        space_forward,
        clip_labels,
        [row(space_gain), row(space_scale), frames]
        + [space_input, space_output, space_up, space_down],
        space_outs,
        [(shared_w, BF)]
        + [(w.shape, BF) for w in (space_input, space_output, space_up, space_down)]
        + space_outs
        + [((4, tokens, tokens), F32), ((2, tokens, CHUNK), BF)],
        5 + 10 * some,
        small=2,
        after=sent,
        flops=some * flops,
    )
    x2_moved = exchange(x2)
    held_back = grad_moved
    if hierarchical:
        held_back = [marker(*grad_moved[2:])]

    block_tails = [rows_w, rows_w, rows_w, rows_3, rows_w, rows_h, rows_h, rows_w]
    time_tails = [rows_w, rows_w, rows_w, rows_w, rows_w, rows_h, rows_h, rows_w]
    input_grad, result, *alone = single.call(
        alone_both,
        [("pack", frames), ("pack", output_grad)] + space_args + time_args,
        [whole, whole] + steps(1, *block_tails) + steps(1, *time_tails),
        scratch=[
            pltpu.VMEM((tokens, LANES), F32),
            pltpu.VMEM((tokens, LANES), F32),
            pltpu.VMEM(rows_3, BF),
            pltpu.VMEM((HEADS, tokens, tokens), BF),
            pltpu.VMEM(rows_h, BF),
            pltpu.VMEM(rows_h, BF),
            pltpu.VMEM(rows_w, BF),
        ]
        + work_shapes(tokens),
        flops=6 * flops,
        after=(x2, *held_back),
    )
    sz0_one, so_one, se1_one, sgqkv_one, sz1_one, seu_one, sh_one, se2_one = alone[:8]
    tz0_one, to_one, te1_one, tgv_one, tz1_one, teu_one, th_one, te2_one = alone[8:]

    time_outs = [(x2.shape, BF)] * 2 + [
        (shape, BF)
        for shape in (shared_w, shared_3, shared_w, shared_w, shared_w, shared_h, shared_h, shared_w)
    ]
    *g0, out, tz0, tgqkv, to, te1, tz1, teu, th, te2 = manual_call(
        functools.partial(time_kernel, len(grad_moved), len(moved_outs)),
        (clip_labels, ids),
        [row(time_gain), row(time_scale), x2_moved, *grad_moved]
        + [time_input, time_output, time_up, time_down],
        moved_outs + time_outs[1:],
        [(x2.shape, BF)] * 2
        + [(w.shape, BF) for w in (time_input, time_output, time_up, time_down)]
        + time_outs
        + [
            (shared_3, BF),
            (square, BF),
            (shared_h, BF),
            ((some, tokens, tokens), F32),
            (shared_w, BF),
            ((some, 4, tokens, tokens), F32),
            ((some, 2, tokens, CHUNK), BF),
            ((some, 4, tokens, tokens), BF),
            (square, BF),
        ],
        14 + 8 * some + 9,
        small=2,
        after=(sz0_one,),
        flops=3 * some * flops,
    )
    g0_moved = exchange_pieces(g0)
    out, g0_moved = lax.optimization_barrier((out, g0_moved))
    out_moved = exchange(out)

    held_back = ()
    everything = packs * tokens
    feed_shapes = [(1, width // 8), (width // 8, hidden), (hidden // 8, width)]
    attend_shapes = [(1, width // 8), (width // 8, 3 * width), (width // 8, width)]
    time_shared = [tz1, teu, te2, th, tz0, tgqkv, to, te1]
    time_one = [tz1_one, teu_one, te2_one, th_one, tz0_one, tgv_one, to_one, te1_one]
    if hierarchical:
        parts_shapes = [((4, 4, 96, CHUNK), BF)] * 4
        time_terms = manual_call(
            time_weights_kernel,
            ids,
            time_shared + time_one,
            parts_shapes,
            [((everything, a.shape[2]), BF) for a in time_shared] + parts_shapes,
            8 * packs + 20,
            flops=packs * flops,
        )
        time_got = [swap(other, "tm", 8, 1) for other in time_terms[1::2]]
        time_far = far_parts(time_terms[::2], time_got, marker(*g0_moved[2:]))
        held_back = time_far
    else:
        grad_one = jnp.pad(tgv_one, ((0, 0), (0, 0), (2 * width, 0)))
        joined = [joint(a, b) for a, b in zip(time_shared, time_one[:5] + [grad_one] + time_one[6:])]
        time_grads = plain_grads(joined[0], joined[1], joined[3], joined[2], time_up, time_scale)
        time_grads += plain_grads(joined[4], joined[5], joined[6], joined[7], time_input, time_gain)

    space_one = [sz1_one, seu_one, sh_one, se2_one, sz0_one, sgqkv_one, so_one, se1_one]
    whole_shapes = [((everything, a.shape[2]), BF) for a in space_one]
    parts_shapes = [((4, 4, 96, CHUNK), BF)] * 4
    sg1, sgqkv, *weights = manual_call(
        functools.partial(space_kernel, hierarchical, len(g0_moved)),
        ids,
        [row(space_scale), sinv1, *g0_moved, sslope, sz1, space_output, space_up, space_down]
        + [sqkv, sp, sh, sz0, so]
        + space_one,
        [(shared_w, F32), (shared_3, BF)]
        + (parts_shapes if hierarchical else [whole_shapes[i] for i in (1, 3, 7)]),
        [
            (x2.shape, BF),
            (sslope.shape, BF),
            (space_output.shape, BF),
            (space_up.shape, BF),
            (space_down.shape, BF),
            (sqkv.shape, BF),
            (sp.shape, BF),
            (shared_w, BF),
            (shared_w, F32),
            ((some, 4, tokens, tokens), BF),
            (square, BF),
        ]
        + whole_shapes
        + (parts_shapes if hierarchical else []),
        96,
        small=2,
        after=held_back,
        flops=2 * packs * flops,
    )
    held_back = ()
    if hierarchical:
        time_got, sgqkv = lax.optimization_barrier((time_got, sgqkv))
        time_mine = time_terms[::2]
        time_halves, time_near = near_parts(time_mine, time_got, time_far)
        mine = weights[::2]
        got = [swap(other, "tm", 8, 1) for other in weights[1::2]]
        far = far_parts(mine, got, marker(time_near[1]))
        held_back = far
    input_grad, result = shared.call(
        space_back_in,
        [
            ("step", sgqkv),
            ("whole", space_input),
            ("whole", row(space_gain)),
            ("step", sz0),
            ("step", sinv0),
            ("step", sg1),
            ("moved", out_moved),
        ],
        [("pack", frames.shape, F32, input_grad), ("pack", frames.shape, F32, result)],
        flops=flops // 4,
        after=held_back,
    )
    if hierarchical:
        time_halves, input_grad = lax.optimization_barrier((time_halves, input_grad))
        time_rows = stream_rows(time_mine, time_got, time_halves, time_near)
        time_last = z_got(time_rows)
        time_final = add(time_rows[0], *time_last)
        final = z_sum(stream_rows(mine, got, *near_parts(mine, got, far), marker(*time_last)))
        grads = finish_call(
            finish_kernel,
            ids,
            gather_parts(final),
            [(space_up, space_scale), (space_input, space_gain)],
            feed_shapes + attend_shapes,
        )
        feed_grads, attend_grads = grads[:3], grads[3:]
        time_grads = finish_call(
            finish_kernel,
            ids,
            gather_parts(time_final),
            [(time_up, time_scale), (time_input, time_gain)],
            feed_shapes + attend_shapes,
        )
    else:
        have = some * tokens
        seu, se2, se1 = [a[:have].reshape(some, tokens, -1) for a in weights]
        feed_grads = plain_grads(
            joint(sz1, sz1_one),
            joint(seu, seu_one),
            joint(sh, sh_one),
            joint(se2, se2_one),
            space_up,
            space_scale,
        )
        attend_grads = plain_grads(
            joint(sz0, sz0_one),
            joint(sgqkv, sgqkv_one),
            joint(so, so_one),
            joint(se1, se1_one),
            space_input,
            space_gain,
        )
    grads = attend_grads + feed_grads + time_grads[3:] + time_grads[:3]
    return (result, input_grad, *grads)


def joint(shared, one):
    return jnp.concatenate([shared, one]).reshape(-1, shared.shape[-1])


def solution(mesh):
    tokens = P("stream", "tm", None, None)
    vector, matrix = P("tm"), P("tm", None)
    return jax.shard_map(
        functools.partial(per_device, mesh.shape["tm"], mesh.shape["stream"]),
        mesh=mesh,
        in_specs=(tokens,) + (P(),) * 12 + (P("stream", None), tokens),
        out_specs=(tokens, tokens) + (vector, matrix, matrix, vector, matrix, matrix) * 2,
        check_vma=False,
    )
```

```python
import functools

import jax
import jax.numpy as jnp
from jax import lax
from jax.experimental import pallas as pl
from jax.experimental.pallas import tpu as pltpu
from jax.sharding import PartitionSpec as P

HEADS = 8
EPS = 1e-05
GELU_A = 0.7978845608028654
GELU_B = 0.044715
BF = jnp.bfloat16
F32 = jnp.float32
CHUNK = 512
LANES = 128
COST = 1
ROWS = (0, 96, 64, 80, 160, 176)
VMEM = 60 * 1024 * 1024
SMALL_VMEM = 24 * 1024 * 1024


def nn(a, b):
    return jnp.dot(a, b, preferred_element_type=F32)


def nt(a, b):
    return lax.dot_general(a, b, (((1,), (1,)), ((), ())), preferred_element_type=F32)


def tn(a, b):
    return lax.dot_general(a, b, (((0,), (0,)), ((), ())), preferred_element_type=F32)


def unit(values):
    average = jnp.mean(values, axis=-1, keepdims=True)
    centered = values - average
    inverse = lax.rsqrt(jnp.mean(centered * centered, axis=-1, keepdims=True) + EPS)
    return centered * inverse, inverse


def unit_backward(grad, unit_rows, inverse):
    first = jnp.mean(grad, axis=-1, keepdims=True)
    second = jnp.mean(grad * unit_rows, axis=-1, keepdims=True)
    return inverse * (grad - first - unit_rows * second)


def gelu_parts(u):
    square = u * u
    tangent = jnp.tanh(u * (BF(GELU_A) + BF(GELU_A * GELU_B) * square))
    half = BF(0.5) * u
    value = half + half * tangent
    slope = (BF(0.5) + BF(0.5) * tangent) + half * (BF(1.0) - tangent * tangent) * (
        BF(GELU_A) + BF(3.0 * GELU_A * GELU_B) * square
    )
    return value, slope


def head_masks(width):
    lane = lax.broadcasted_iota(jnp.int32, (1, 2 * width), 1)
    low = lane < width
    return low, (low.astype(F32).astype(BF), (1.0 - low.astype(F32)).astype(BF))


def attend_steps(qkv_ref, p_ref, o_ref, bias_ref, s_ref):
    width = qkv_ref.shape[1] // 3
    size = width // HEADS
    _, masks = head_masks(size)

    def lanes(part, head):
        at = part * width + (head // 2) * 2 * size
        return qkv_ref[:, at : at + 2 * size]

    def score(head):
        s_ref[head % 4] = nt(lanes(1, head) * masks[head % 2], lanes(0, head) * BF(size**-0.5))

    def soften(head):
        scores = s_ref[head % 4]
        if bias_ref is not None:
            scores = scores + bias_ref[...]
        e = jnp.exp(scores - jnp.max(scores, axis=0, keepdims=True))
        p_ref[head] = (e * (1.0 / jnp.sum(e, axis=0, keepdims=True))).astype(BF)

    for head in range(0, HEADS, 2):
        if head == 0:
            score(0)
            score(1)
        if head + 2 < HEADS:
            score(head + 2)
            score(head + 3)
        soften(head)
        soften(head + 1)
        yield
    for head in range(0, HEADS, 2):
        v = lanes(2, head).T
        both = jnp.concatenate([nn(v[:size], p_ref[head]), nn(v[size:], p_ref[head + 1])], axis=0)
        o_ref[:, head * size : (head + 2) * size] = both.T.astype(BF)
        yield


def attend_backward_steps(qkv_ref, p_ref, go_ref, out_ref, gp_ref, gs_ref):
    width = qkv_ref.shape[1] // 3
    size = width // HEADS
    _, masks = head_masks(size)

    def lanes(part, head):
        at = part * width + (head // 2) * 2 * size
        return qkv_ref[:, at : at + 2 * size]

    def gos(head):
        return go_ref[:, (head // 2) * 2 * size : (head // 2 + 1) * 2 * size]

    def put(part, head, value):
        at = part * width + head * size
        out_ref[:, at : at + 2 * size] = value.astype(BF)

    def start(head):
        for h in (head, head + 1):
            gp_ref[h % 4] = nt(lanes(2, h) * masks[h % 2], gos(h)).astype(BF)
        g = gos(head)
        put(2, head, nn(p_ref[head], g * masks[0]) + nn(p_ref[head + 1], g * masks[1]))

    def middle(head):
        p = p_ref[head]
        weighted = p * gp_ref[head % 4]
        total = jnp.sum(weighted.astype(F32), axis=0, keepdims=True).astype(BF)
        gs_ref[head] = weighted - p * total

    def finish(head):
        q = lanes(0, head) * BF(size**-0.5)
        k = (lanes(1, head) * BF(size**-0.5)).T
        put(1, head, nn(gs_ref[head], q * masks[0]) + nn(gs_ref[head + 1], q * masks[1]))
        both = jnp.concatenate([nn(k[:size], gs_ref[head]), nn(k[size:], gs_ref[head + 1])], axis=0)
        put(0, head, both.T)

    start(0)
    yield
    for head in range(0, HEADS, 2):
        middle(head)
        middle(head + 1)
        if head + 2 < HEADS:
            start(head + 2)
        if head > 0:
            finish(head - 2)
        yield
    finish(HEADS - 2)


def feed_up_steps(m, up_ref, down_ref, h_ref, slope_ref, u_ref):
    steps = up_ref.shape[1] // CHUNK

    def before(step):
        u_ref[step % 2] = nn(m, up_ref[:, step * CHUNK : (step + 1) * CHUNK]).astype(BF)

    before(0)
    for step in range(steps):
        if step + 1 < steps:
            before(step + 1)
        at = step * CHUNK
        h_ref[:, at : at + CHUNK], slope_ref[:, at : at + CHUNK] = gelu_parts(u_ref[step % 2])
        yield
    return nn(h_ref[...], down_ref[...])


def feed_back_steps(e2, up_ref, down_ref, slope_ref, eu_ref, up_copy=None):
    for at in range(0, up_ref.shape[1], CHUNK):
        gh = nt(e2, down_ref[at : at + CHUNK, :]).astype(BF)
        eu_ref[:, at : at + CHUNK] = gh * slope_ref[:, at : at + CHUNK]
        yield
    if up_copy is not None:
        wait(up_copy)
    return nt(eu_ref[...], up_ref[...])


def whole(steps):
    while True:
        try:
            next(steps)
        except StopIteration as end:
            return end.value


def together(runs):
    while runs:
        runs = [run for run in runs if next(run, "end") != "end"]


def attend_backward(*args):
    whole(attend_backward_steps(*args))


def feed_up(*args):
    return whole(feed_up_steps(*args))


def feed_back(*args):
    return whole(feed_back_steps(*args))


def rows_of(block):
    slots, _, patches, width = block.shape
    return block[:, 0].astype(F32).reshape(slots * patches, width)


def block_of(rows, ref):
    slots, _, patches, width = ref.shape
    ref[:, 0] = rows.reshape(slots, patches, width).astype(ref.dtype)


def work_shapes(tokens):
    return [
        pltpu.VMEM((4, tokens, tokens), F32),
        pltpu.VMEM((2, tokens, CHUNK), BF),
        pltpu.VMEM((4, tokens, tokens), BF),
        pltpu.VMEM((HEADS, tokens, tokens), BF),
    ]


def wide(column):
    return jnp.broadcast_to(column, (column.shape[0], LANES))


def space_steps(x, weights, state, work, arrive=lambda index: None, sent=lambda *indices: None):
    gain, w_in, w_out, scale, w_up, w_down = weights
    z0, inv0, qkv, p, o, z1, inv1, h, slope = state
    unit0, inverse0 = unit(x)
    z0[...] = unit0.astype(BF)
    inv0[...] = wide(inverse0)
    sent(0, 1)
    arrive(0)
    qkv[...] = nn((unit0 * gain[...]).astype(BF), w_in[...]).astype(BF)
    sent(2)
    yield
    yield from attend_steps(qkv, p, o, None, work[0])
    sent(3, 4)
    arrive(1)
    r1 = x + nn(o[...], w_out[...])
    unit1, inverse1 = unit(r1)
    z1[...] = unit1.astype(BF)
    inv1[...] = wide(inverse1)
    sent(5, 6)
    m = (unit1 * scale[...]).astype(BF)
    yield
    arrive(2)
    total = yield from feed_up_steps(m, w_up, w_down, h, slope, work[1])
    sent(7, 8)
    return r1 + total


def space_rows(x, weights, state, work):
    return whole(space_steps(x, weights, state, work))


def space_forward(labels, gain, scale, frames_in, w_in_in, w_out_in, w_up_in, w_down_in, *rest):
    outs, (frames, w_in, w_out, w_up, w_down), rest = rest[:10], rest[10:15], rest[15:]
    (x2, *state), (scores, u, semaphores) = rest[:10], rest[10:]
    copies = Copies(semaphores)
    packs = frames.shape[0]
    got = [
        copies.fetch(frames_in.at[pack_at(labels, pack), 0], frames.at[pack])
        for pack in range(packs)
    ]
    waits = [
        [copies.fetch(w_in_in, w_in)],
        [copies.fetch(w_out_in, w_out)],
        [copies.fetch(w_up_in, w_up), copies.fetch(w_down_in, w_down)],
    ]
    weights = gain, w_in, w_out, scale, w_up, w_down

    base = copies.count

    def leaving(index, pack):
        semaphore = semaphores.at[base + index * packs + pack]
        return pltpu.make_async_copy(state[index].at[pack], outs[1 + index].at[pack], semaphore)

    def sending(pack):
        part, semaphore = (slice(None), pl.ds(pack, 1)), semaphores.at[base + len(state) * packs + pack]
        return pltpu.make_async_copy(x2.at[part], outs[0].at[part], semaphore)

    def first(pack, arrivals):
        pl.when(pack == 0)(lambda: wait(*arrivals))

    def run(pack, carry):
        def sent(*indices):
            for index in indices:
                leaving(index, pack).start()

        steps = space_steps(
            frames[pack].astype(F32),
            weights,
            [ref.at[pack] for ref in state],
            (scores, u),
            lambda index: first(pack, waits[index]),
            sent,
        )
        block_of(whole(steps), x2.at[:, pl.ds(pack, 1)])
        sending(pack).start()
        return carry

    wait(*got)
    lax.fori_loop(0, packs, run, 0)
    for pack in range(packs):
        sending(pack).wait()
        for index in range(len(state)):
            leaving(index, pack).wait()


def build_bias(labels, pack, slots, patches, bias):
    tokens = slots * patches
    row = lax.broadcasted_iota(jnp.int32, (1, tokens), 1)
    column = lax.broadcasted_iota(jnp.int32, (tokens, 1), 0)

    def label_of(position):
        slot = position // patches
        value = jnp.zeros_like(position)
        for f in range(slots):
            value = jnp.where(slot == f, labels[pack, f], value)
        return value

    same_patch = (row % patches) == (column % patches)
    allowed = same_patch & (column <= row) & (label_of(column) == label_of(row))
    bias[...] = jnp.where(allowed, 0.0, -1e30)


def send_moved(copies, ids, held, outs):
    if len(outs) == 1:
        copies.send(held, outs[0])
        return
    for d in range(4):
        at = 2 * (ids[1] ^ d)
        copies.send(held.at[at + ids[0]], outs[0].at[d])
        copies.send(held.at[at + 1 - ids[0]], outs[1].at[d])


def fetch_moved(copies, ids, pieces, held):
    if len(pieces) == 1:
        return [copies.fetch(pieces[0], held)]
    near, far, *others = pieces
    at = 2 * ids[1]
    got = [copies.fetch(near.at[0], held.at[at + ids[0]])]
    got.append(copies.fetch(far.at[0], held.at[at + 1 - ids[0]]))
    for d, piece in enumerate(others, 1):
        at = 2 * (ids[1] ^ d)
        got.append(copies.fetch(piece.at[0], held.at[at + ids[0]]))
        got.append(copies.fetch(piece.at[1], held.at[at + 1 - ids[0]]))
    return got


def exchange_pieces(arrays):
    if len(arrays) == 1:
        return [lax.all_to_all(arrays[0], "tm", split_axis=0, concat_axis=0, tiled=True)]
    near, far = arrays[0], swap(arrays[1], "tm", 8, 1)
    return [near, far] + [swap(jnp.stack([near[d], far[d]]), "tm", 8, 2 * d) for d in range(1, 4)]


def time_kernel(pieces, moved, labels, ids, gain, scale, x2_in, *rest):
    grad_in, rest = rest[:pieces], rest[pieces:]
    (w_in_in, w_out_in, w_up_in, w_down_in), rest = rest[:4], rest[4:]
    g0_outs, outs, rest = rest[:moved], (None,) + rest[moved : moved + 9], rest[moved + 9 :]
    x2, grad, w_in, w_out, w_up, w_down = rest[:6]
    held = rest[6:16]
    g0, out, z0, gqkv, o, e1, z1, eu, h, e2 = held
    qkv, p, slope, bias, go, scores, u, gp, gs = rest[16:25]
    copies = Copies(rest[-1])
    slots, packs, patches, _ = x2.shape
    got_x2, got_in = copies.fetch(x2_in, x2), copies.fetch(w_in_in, w_in)
    got_out, got_up = copies.fetch(w_out_in, w_out), copies.fetch(w_up_in, w_up)
    got_down, got_grad = copies.fetch(w_down_in, w_down), fetch_moved(copies, ids, grad_in, grad)

    def send(index, pack):
        copies.send(held[index].at[pack], outs[index].at[pack])

    def run(pack):
        if pack == 0:
            wait(got_x2)
        build_bias(labels, pack_at(labels, pack), slots, patches, bias.at[pack])
        x = rows_of(x2[:, pack : pack + 1])
        unit0, inverse0 = unit(x)
        z0[pack] = unit0.astype(BF)
        send(2, pack)
        if pack == 0:
            wait(got_in)
        qkv[pack] = nn((unit0 * gain[...]).astype(BF), w_in[...]).astype(BF)
        yield
        yield from attend_steps(qkv.at[pack], p.at[pack], o.at[pack], bias.at[pack], scores.at[pack])
        send(4, pack)
        if pack == 0:
            wait(got_out)
        r1 = x + nn(o[pack], w_out[...])
        unit1, inverse1 = unit(r1)
        z1[pack] = unit1.astype(BF)
        send(6, pack)
        m = (unit1 * scale[...]).astype(BF)
        yield
        if pack == 0:
            wait(got_up, got_down)
        total = yield from feed_up_steps(m, w_up, w_down, h.at[pack], slope.at[pack], u.at[pack])
        send(8, pack)
        block_of(r1 + total, out.at[:, pl.ds(pack, 1)])
        if pack == 0:
            wait(*got_grad)
        g2 = rows_of(grad[:, pack : pack + 1])
        e2[pack] = g2.astype(BF)
        send(9, pack)
        yield
        gm = yield from feed_back_steps(e2[pack], w_up, w_down, slope.at[pack], eu.at[pack])
        send(7, pack)
        g1 = g2 + unit_backward(gm * scale[...], unit1, inverse1)
        e1[pack] = g1.astype(BF)
        send(5, pack)
        go[pack] = nt(e1[pack], w_out[...]).astype(BF)
        yield
        yield from attend_backward_steps(
            qkv.at[pack], p.at[pack], go.at[pack], gqkv.at[pack], gp.at[pack], gs.at[pack]
        )
        send(3, pack)
        gn = nt(gqkv[pack], w_in[...])
        block_of(g1 + unit_backward(gn * gain[...], unit0, inverse0), g0.at[:, pl.ds(pack, 1)])

    together([run(pack) for pack in range(packs)])
    send_moved(copies, ids, g0, g0_outs)
    copies.send(out, outs[1])
    copies.finish()


def alone_both(labels, frames, grad, *rest):
    space, (gain, w_in, w_out, scale, w_up, w_down) = rest[:6], rest[6:12]
    input_grad, out = rest[12:14]
    sz0, so, se1, sgqkv, sz1, seu, sh, se2 = [ref.at[0] for ref in rest[14:22]]
    z0, o, e1, gv, z1, eu, h, e2 = [ref.at[0] for ref in rest[22:30]]
    inv0, inv1, qkv, p, sslope, slope, go, *work = rest[30:]
    state = sz0, inv0, qkv, p, so, sz1, inv1, sh, sslope
    x = space_rows(frames[0, 0].astype(F32), space, state, work)
    width = x.shape[1]
    unit0, inverse0 = unit(x)
    z0[...] = unit0.astype(BF)
    o[...] = nn((unit0 * gain[...]).astype(BF), w_in[:, 2 * width :]).astype(BF)
    r1 = x + nn(o[...], w_out[...])
    unit1, inverse1 = unit(r1)
    z1[...] = unit1.astype(BF)
    m = (unit1 * scale[...]).astype(BF)
    out[0, 0] = r1 + feed_up(m, w_up, w_down, h, slope, work[1])
    e2[...] = grad[0, 0]
    g2 = grad[0, 0].astype(F32)
    gm = feed_back(e2[...], w_up, w_down, slope, eu)
    g1 = g2 + unit_backward(gm * scale[...], unit1, inverse1)
    e1[...] = g1.astype(BF)
    gv[...] = nt(e1[...], w_out[...]).astype(BF)
    gn = nt(gv[...], w_in[:, 2 * width :])
    g2 = g1 + unit_backward(gn * gain[...], unit0, inverse0)
    gain, w_in, w_out, scale, w_up, w_down = space
    se2[...] = g2.astype(BF)
    gm = feed_back(se2[...], w_up, w_down, sslope, seu)
    g1 = g2 + unit_backward(gm * scale[...], sz1[...].astype(F32), inv1[:, :1])
    se1[...] = g1.astype(BF)
    go[...] = nt(se1[...], w_out[...]).astype(BF)
    attend_backward(qkv, p, go, sgqkv, work[2], work[3])
    gn = nt(sgqkv[...], w_in[...])
    input_grad[0, 0] = g1 + unit_backward(gn * gain[...], sz0[...].astype(F32), inv0[:, :1])


def space_back_in(labels, gqkv, w_in, gain, z0, inv0, g1, moved, input_grad, result):
    gn = nt(gqkv[0], w_in[...])
    grad = unit_backward(gn * gain[...], z0[0].astype(F32), inv0[0, :, :1])
    input_grad[0, 0] = g1[0] + grad
    result[0, 0] = rows_of(moved[...])


class Copies:
    def __init__(self, semaphores):
        self.semaphores, self.count, self.sent = semaphores, 0, []

    def fetch(self, source, target):
        copy = pltpu.make_async_copy(source, target, self.semaphores.at[self.count])
        self.count += 1
        copy.start()
        return copy

    def send(self, source, target):
        self.sent.append(self.fetch(source, target))

    def finish(self):
        for copy in self.sent:
            copy.wait()


def wait(*copies):
    for copy in copies:
        copy.wait()


def space_kernel(hierarchical, pieces, ids, scale, inv1, *rest):
    g2_in, rest = rest[:pieces], rest[pieces:]
    (slope_in, z1_in, w_out_in, w_up_in, w_down_in, qkv_in, p_in), rest = rest[:7], rest[7:]
    shared, one, rest = rest[:3], rest[3:11], rest[11:]
    (g1_out, gqkv_out), outs, scratch = rest[:2], rest[2 : 6 if hierarchical else 5], rest[6 if hierarchical else 5 :]
    g2, slope, w_out, w_up, w_down, qkv, p, go, g1, gp, gs = scratch[:11]
    z1, eu, h, e2, z0, gqkv, o, e1 = whole = scratch[11:19]
    copies = Copies(scratch[-1])
    packs, tokens, _ = g1.shape
    have = packs * tokens
    got_g2 = fetch_moved(copies, ids, g2_in, g2)
    got_down = copies.fetch(w_down_in, w_down)
    got_slope = [copies.fetch(slope_in.at[pack], slope.at[pack]) for pack in range(packs)]
    got_up = copies.fetch(w_up_in, w_up)
    got_z1 = [
        copies.fetch(z1_in.at[pack], z1.at[pl.ds(pack * tokens, tokens)]) for pack in range(packs)
    ]
    got_out = copies.fetch(w_out_in, w_out)
    got_attend = [
        (copies.fetch(qkv_in.at[pack], qkv.at[pack]), copies.fetch(p_in.at[pack], p.at[pack]))
        for pack in range(packs)
    ]
    got_rest = []
    if hierarchical:
        for source, target in zip(shared, (h, z0, o)):
            for pack in range(packs):
                rows = pl.ds(pack * tokens, tokens)
                got_rest.append(copies.fetch(source.at[pack], target.at[rows]))
        for source, target in zip(one, whole):
            got_rest.append(copies.fetch(source.at[0], target.at[pl.ds(have, tokens)]))
    wait(*got_g2)

    def run(pack):
        rows = slice(pack * tokens, (pack + 1) * tokens)
        e2[rows] = rows_of(g2[:, pack : pack + 1]).astype(BF)
        if pack == 0:
            wait(got_down)
        wait(got_slope[pack])
        gm = yield from feed_back_steps(e2[rows], w_up, w_down, slope.at[pack], eu.at[rows], got_up if pack == 0 else None)
        if pack == 0:
            wait(*got_z1, got_out)
        grad = unit_backward(gm * scale[...], z1[rows].astype(F32), inv1[pack, :, :1])
        total = rows_of(g2[:, pack : pack + 1]) + grad
        g1[pack] = total
        e1[rows] = total.astype(BF)
        go[pack] = nt(e1[rows], w_out[...]).astype(BF)
        copies.send(g1.at[pack], g1_out.at[pack])
        yield
        wait(*got_attend[pack])
        rows = pl.ds(pack * tokens, tokens)
        yield from attend_backward_steps(
            qkv.at[pack], p.at[pack], go.at[pack], gqkv.at[rows], gp.at[pack], gs.at[pack]
        )
        copies.send(gqkv.at[rows], gqkv_out.at[pack])

    together([run(pack) for pack in range(packs)])
    if hierarchical:
        wait(*got_rest)
        one = Halves(copies, ids, scratch[19:21], outs[:2], x_high=True)
        two = Halves(copies, ids, scratch[21:23], outs[2:])
        up_tiles(one, z1, eu, 0)
        down_tiles(two, e2, h, 0)
        attend_tiles([one, one, two, two], z0, o, gqkv, e1, [64, 80, 64, 80], gqkv.shape[0])
    else:
        for source, target in zip((eu, e2, e1), outs):
            copies.send(source, target)
    copies.finish()


def to_send(labels, ids, grad, *rest):
    *outs, held = rest
    slots, places, patches, _ = held.shape
    for place in range(places):
        rows = grad[pack_at(labels, place), 0].astype(F32)
        held[:, place] = rows.reshape(slots, patches, -1).astype(BF)
    if len(outs) == 1:
        outs[0][...] = held[...]
        return
    for d in range(4):
        at = 2 * (ids[1] ^ d)
        outs[0][d] = held[at + ids[0]]
        outs[1][d] = held[at + 1 - ids[0]]


def pack_at(labels, place):
    packs, slots = labels.shape
    alone = packs - 1
    for pack in range(packs - 2, -1, -1):
        alone = jnp.where(labels[pack, slots - 1] == slots - 1, pack, alone)
    return jnp.where(place == packs - 1, alone, place + (place >= alone).astype(jnp.int32))


def without(kernel, first, count):
    def call(*refs):
        return kernel(*refs[:first], *refs[first + count :])

    return call


class Packs:
    def __init__(self, labels, first, count):
        self.labels, self.first, self.count = labels, first, count

    def call(self, kernel, args, outs, scratch=(), flops=0, after=()):
        first, last = self.first, self.labels.shape[0] - 2
        scalars = (self.labels,)

        def spec(kind, shape):
            rank = len(shape)
            if kind == "whole":
                return pl.BlockSpec(shape, lambda i, *s: (0,) * rank)
            if kind == "pack":
                return pl.BlockSpec(
                    (1,) + tuple(shape[1:]), lambda i, s: (pack_at(s, first + i),) + (0,) * (rank - 1)
                )
            if kind == "place":
                return pl.BlockSpec(
                    (1,) + tuple(shape[1:]), lambda i, *s: (first + i,) + (0,) * (rank - 1)
                )
            if kind == "step":
                return pl.BlockSpec(
                    (1,) + tuple(shape[1:]), lambda i, *s: (i,) + (0,) * (rank - 1)
                )
            if kind == "moved":
                return pl.BlockSpec(
                    (shape[0], 1, shape[2], shape[3]),
                    lambda i, *s: (0, jnp.minimum(i, last), 0, 0),
                )
            return pl.BlockSpec(memory_space=pl.ANY)

        in_specs = [spec(kind, array.shape) for kind, array in args]
        operands = [array for _, array in args]
        aliases = {}
        for index, (kind, shape, dtype, into) in enumerate(outs):
            if into is not None:
                aliases[len(scalars) + len(operands)] = index
                operands.append(into)
                in_specs.append(pl.BlockSpec(memory_space=pl.ANY))
        for array in after:
            operands.append(array)
            in_specs.append(pl.BlockSpec(memory_space=pl.ANY))
        moved = sum(a.size * a.dtype.itemsize for a in operands)
        unread = len(operands) - len(args)
        return pl.pallas_call(
            without(kernel, len(scalars) + len(args), unread),
            out_shape=[jax.ShapeDtypeStruct(shape, dtype) for _, shape, dtype, _ in outs],
            grid_spec=pltpu.PrefetchScalarGridSpec(
                num_scalar_prefetch=len(scalars),
                grid=(self.count,),
                in_specs=in_specs,
                out_specs=[spec(kind, shape) for kind, shape, _, _ in outs],
                scratch_shapes=list(scratch),
            ),
            input_output_aliases=aliases,
            compiler_params=pltpu.CompilerParams(
                vmem_limit_bytes=VMEM, dimension_semantics=("arbitrary",)
            ),
            cost_estimate=pl.CostEstimate(
                flops=int(flops * self.count * COST), bytes_accessed=int(moved * COST), transcendentals=0
            ),
        )(*scalars, *operands)


class Halves:
    def __init__(self, copies, ids, held, outs, x_high=False):
        self.copies, self.held, self.outs = copies, held, outs
        self.first, self.z, self.s, self.x_high = ids[0] == 0, ids[1], ids[2], x_high

    def part(self, s):
        if s is None:
            return slice(None)
        part = s ^ self.s
        return (part & 1) * 2 + (part >> 1) if self.x_high else part

    def put(self, s, z, at, even, odd):
        rows = slice(at, at + even.shape[0])
        self.held[0][self.part(s), z ^ self.z, rows] = jnp.where(self.first, even, odd)
        self.held[1][self.part(s), z ^ self.z, rows] = jnp.where(self.first, odd, even)

    def send(self, s, z, at, rows):
        index = self.part(s), slice(None) if z is None else z ^ self.z, pl.ds(at, rows)
        for ref, out in zip(self.held, self.outs):
            self.copies.send(ref.at[index], out.at[index])


def up_tiles(place, z1, eu, at):
    for step in range(4):
        tile = tn(z1[...], eu[:, step * CHUNK : (step + 1) * CHUNK]).astype(BF)
        for z in range(4):
            row = 128 * z
            place.put(step, z, at, tile[row : row + 64], tile[row + 64 : row + 128])
        place.send(step, None, at, 64)


def down_tiles(place, e2, h, at):
    for step in range(4):
        tile = tn(e2[...], h[:, step * CHUNK : (step + 1) * CHUNK]).astype(BF)
        for s in range(4):
            upper, lower = tile[128 * s : 128 * s + 64], tile[128 * s + 64 : 128 * s + 128]
            even = jnp.concatenate([upper[:, :256], lower[:, :256]], axis=1)
            odd = jnp.concatenate([upper[:, 256:], lower[:, 256:]], axis=1)
            place.put(s, step, at, even, odd)
        place.send(None, step, at, 64)


def attend_tiles(places, z0, o, gqkv, e1, ats, depth):
    for step, (place, at) in enumerate(zip(places, ats)):
        if step == 3:
            tile = tn(o[...], e1[...])
        else:
            rows = gqkv.shape[0] if step == 2 else depth
            tile = tn(z0[:rows], gqkv[:rows, step * CHUNK : (step + 1) * CHUNK])
        tile = tile.astype(BF)
        for z in range(4):
            for s in range(4):
                row = 128 * z + 16 * s
                place.put(s, z, at, tile[row : row + 16], tile[row + 64 : row + 80])
        if step % 2:
            place.send(None, None, at - 16, 32)


def time_weights_kernel(ids, *rest):
    names = 8
    shared, single, outs, scratch = rest[:names], rest[names : 2 * names], rest[16:20], rest[20:]
    z1, eu, e2, h, z0, gqkv, o, e1 = scratch[:names]
    copies = Copies(scratch[-1])
    one = Halves(copies, ids, scratch[8:10], outs[:2], x_high=True)
    two = Halves(copies, ids, scratch[10:12], outs[2:])
    packs, tokens, _ = shared[0].shape
    have = packs * tokens
    got = []
    for source, last, target in zip(shared, single, scratch):
        wide_target = target.at[pl.ds(have, tokens)]
        if last.shape[2] < target.shape[1]:
            wide_target = target.at[pl.ds(have, tokens), pl.ds(target.shape[1] - last.shape[2], last.shape[2])]
        got.append(
            [copies.fetch(source.at[pack], target.at[pl.ds(pack * tokens, tokens)]) for pack in range(packs)]
            + [copies.fetch(last.at[0], wide_target)]
        )
    wait(*got[0], *got[1], *got[2], *got[3])
    up_tiles(one, z1, eu, 0)
    down_tiles(two, e2, h, 0)
    wait(*got[4], *got[5], *got[6], *got[7])
    attend_tiles([one, one, two, two], z0, o, gqkv, e1, [64, 80, 64, 80], have)
    copies.finish()


def manual_call(kernel, ids, args, outs, scratch, semaphores, small=0, after=(), flops=0):
    anywhere = pl.BlockSpec(memory_space=pl.ANY)
    scalars = ids if isinstance(ids, tuple) else (ids,)
    return pl.pallas_call(
        without(kernel, len(scalars) + len(args), len(after)),
        out_shape=[jax.ShapeDtypeStruct(shape, dtype) for shape, dtype in outs],
        in_specs=[pl.BlockSpec(memory_space=pltpu.SMEM)] * len(scalars)
        + [pl.BlockSpec(memory_space=pltpu.VMEM)] * small
        + [anywhere] * (len(args) - small + len(after)),
        out_specs=[anywhere] * len(outs),
        scratch_shapes=[pltpu.VMEM(shape, dtype) for shape, dtype in scratch]
        + [pltpu.SemaphoreType.DMA((semaphores,))],
        compiler_params=pltpu.CompilerParams(vmem_limit_bytes=VMEM),
        cost_estimate=pl.CostEstimate(
            flops=int(flops * COST), bytes_accessed=0, transcendentals=0
        ),
    )(*scalars, *args, *after)


def swap(array, axis, size, mask):
    return lax.ppermute(array, axis, [(i, i ^ mask) for i in range(size)])


def add(*terms):
    total = terms[0].astype(F32)
    for term in terms[1:]:
        total = total + term.astype(F32)
    return total.astype(BF)


def far_parts(mine, got, note):
    return [add(a[2:], b[2:], note) for a, b in zip(mine, got)]


def near_parts(mine, got, far):
    halves = [swap(far[0], "stream", 4, 1), swap(far[1], "stream", 4, 2)]
    return halves, [add(a[1], b[1], half[1]) for a, b, half in zip(mine, got, halves)]


def stream_rows(mine, got, halves, near, *note):
    last = [swap(near[0], "stream", 4, 2), swap(near[1], "stream", 4, 1)]
    terms = list(zip(mine, got, halves, last))
    return [
        jnp.concatenate([add(a[0][d], b[0][d], half[0][d], end[d], *note) for a, b, half, end in terms])
        for d in range(4)
    ]


def z_got(rows):
    return [swap(rows[d], "tm", 8, 2 * d) for d in range(1, 4)]


def z_sum(rows):
    return add(rows[0], *[swap(rows[d], "tm", 8, 2 * d) for d in range(1, 4)])


def gather_parts(final):
    return [final] + [swap(final, "stream", 4, d) for d in range(1, 4)]


def marker(*arrays):
    def kernel(*refs):
        refs[-1][...] = jnp.zeros_like(refs[-1])

    return pl.pallas_call(
        kernel,
        out_shape=jax.ShapeDtypeStruct((1, CHUNK), F32),
        in_specs=[pl.BlockSpec(memory_space=pl.ANY)] * len(arrays),
        out_specs=pl.BlockSpec(memory_space=pltpu.VMEM),
        cost_estimate=pl.CostEstimate(flops=10**12, bytes_accessed=10**8, transcendentals=0),
    )(*arrays)


def as_row(col):
    size = col.shape[0]
    eye = lax.broadcasted_iota(jnp.int32, (size, size), 0) == lax.broadcasted_iota(
        jnp.int32, (size, size), 1
    )
    return jnp.sum(jnp.where(eye, col, 0.0), axis=0, keepdims=True)


def own_rows(ids, vector):
    shape = 64, vector.shape[1]
    row = lax.broadcasted_iota(jnp.int32, shape, 0) + 64 * (2 * ids[1] + ids[0])
    lane = lax.broadcasted_iota(jnp.int32, shape, 1)
    return jnp.sum(jnp.where(row == lane, vector[...], 0.0), axis=1, keepdims=True)


def finish_kernel(ids, p0, p1, p2, p3, w_up, scale, w_in, gain, *outs):
    scale_grad, up_grad, down_grad, gain_grad, in_grad, out_grad = outs
    up_at, down_at, *in_at, out_at = ROWS
    for d, piece in enumerate((p0, p1, p2, p3)):
        s = ids[2] ^ d
        up_grad[:, pl.ds(pl.multiple_of(512 * s, 512), 512)] = piece[up_at : up_at + 64].astype(F32)
        lower = piece[down_at : down_at + 64].astype(F32)
        whole = jnp.concatenate([lower[:, :256], lower[:, 256:]], axis=0)
        down_grad[:, pl.ds(pl.multiple_of(128 * s, 128), 128)] = whole.T
        rows = pl.ds(pl.multiple_of(16 * s, 16), 16)
        for third, at in enumerate(in_at):
            in_grad[rows, 512 * third : 512 * third + 512] = piece[at : at + 16].astype(F32)
        out_grad[rows, :] = piece[out_at : out_at + 16].astype(F32)
    for grad, weight, factor, vector_grad in (
        (up_grad, w_up, scale, scale_grad),
        (in_grad, w_in, gain, gain_grad),
    ):
        total = grad[...]
        vector_grad[...] = as_row(jnp.sum(total * weight[...].astype(F32), axis=1, keepdims=True))
        grad[...] = total * own_rows(ids, factor)


def finish_call(kernel, ids, pieces, pairs, outs):
    whole = pl.BlockSpec(pieces[0].shape, lambda i, *s: (0, 0))
    specs, operands = [], []
    for weight, vector in pairs:
        height = weight.shape[0] // 8
        specs += [
            pl.BlockSpec((height, weight.shape[1]), lambda i, s: (2 * s[1] + s[0], 0)),
            pl.BlockSpec((1, vector.size), lambda i, *s: (0, 0)),
        ]
        operands += [weight, vector.reshape(1, -1)]
    results = pl.pallas_call(
        kernel,
        out_shape=[jax.ShapeDtypeStruct(shape, F32) for shape in outs],
        grid_spec=pltpu.PrefetchScalarGridSpec(
            num_scalar_prefetch=1,
            grid=(1,),
            in_specs=[whole] * 4 + specs,
            out_specs=[pl.BlockSpec(shape, lambda i, *s: (0, 0)) for shape in outs],
        ),
        compiler_params=pltpu.CompilerParams(vmem_limit_bytes=SMALL_VMEM),
    )(ids, *pieces, *operands)
    return [a.reshape(-1) if a.shape[0] == 1 else a for a in results]


def plain_grads(z, grads, left, right, weight, vector):
    product = tn(z, grads)
    vector_grad = jnp.sum(product * weight.astype(F32), axis=1)
    sums = []
    for term in (vector_grad, product * vector[:, None], tn(left, right)):
        share = lax.psum_scatter(term.astype(BF), "tm", scatter_dimension=0, tiled=True)
        sums.append(lax.psum(share, "stream").astype(F32))
    return sums


def grad_to_send(labels, ids, grad, shape, outs):
    space = pl.BlockSpec(memory_space=pltpu.VMEM)
    return pl.pallas_call(
        to_send,
        out_shape=[jax.ShapeDtypeStruct(shape, dtype) for shape, dtype in outs],
        in_specs=[pl.BlockSpec(memory_space=pltpu.SMEM)] * 2 + [space],
        out_specs=[space] * len(outs),
        scratch_shapes=[pltpu.VMEM(shape, BF)],
        compiler_params=pltpu.CompilerParams(vmem_limit_bytes=VMEM),
    )(labels, ids, grad)


def per_device(
    ranks,
    streams,
    frames,
    space_gain,
    space_input,
    space_output,
    space_scale,
    space_up,
    space_down,
    time_gain,
    time_input,
    time_output,
    time_scale,
    time_up,
    time_down,
    clip_labels,
    output_grad,
):
    packs, _, tokens, width = frames.shape
    slots = clip_labels.shape[1]
    patches = tokens // ranks
    hidden = space_up.shape[1]
    some = packs - 1
    hierarchical = (ranks, streams) == (8, 4)
    tm = lax.axis_index("tm")
    ids = jnp.stack([tm % 2, tm // 2, lax.axis_index("stream")]).astype(jnp.int32)
    shared = Packs(clip_labels, 0, some)
    single = Packs(clip_labels, some, 1)

    def row(vector):
        return vector.reshape(1, -1)

    def exchange(array):
        return lax.all_to_all(array, "tm", split_axis=0, concat_axis=0, tiled=True)

    def steps(count, *tails):
        return [("step", (count,) + tail, BF, None) for tail in tails]

    moved = ("moved", (slots, some, patches, width), BF, None)
    whole = ("pack", frames.shape, F32, None)
    flops = 2 * tokens * width * (4 * width + 2 * hidden)

    shape = moved[1]
    halves = (slots // 2,) + shape[1:]
    moved_outs = [(halves, BF)] * 2 if hierarchical else [(shape, BF)]
    sent = grad_to_send(clip_labels, ids, output_grad, shape, moved_outs)
    grad_moved = exchange_pieces(sent)

    space_args = [
        ("whole", row(space_gain)),
        ("whole", space_input),
        ("whole", space_output),
        ("whole", row(space_scale)),
        ("whole", space_up),
        ("whole", space_down),
    ]
    time_args = [
        ("whole", row(time_gain)),
        ("whole", time_input),
        ("whole", time_output),
        ("whole", row(time_scale)),
        ("whole", time_up),
        ("whole", time_down),
    ]
    rows_w, rows_3, rows_h = (tokens, width), (tokens, 3 * width), (tokens, hidden)
    shared_w, shared_3, shared_h = [(some,) + tail for tail in (rows_w, rows_3, rows_h)]
    square, spread = (some, HEADS, tokens, tokens), (some, tokens, LANES)
    space_outs = [
        (shape, BF),
        (shared_w, BF),
        (spread, F32),
        (shared_3, BF),
        (square, BF),
        (shared_w, BF),
        (shared_w, BF),
        (spread, F32),
        (shared_h, BF),
        (shared_h, BF),
    ]
    x2, sz0, sinv0, sqkv, sp, so, sz1, sinv1, sh, sslope = manual_call(
        space_forward,
        clip_labels,
        [row(space_gain), row(space_scale), frames]
        + [space_input, space_output, space_up, space_down],
        space_outs,
        [(shared_w, BF)]
        + [(w.shape, BF) for w in (space_input, space_output, space_up, space_down)]
        + space_outs
        + [((4, tokens, tokens), F32), ((2, tokens, CHUNK), BF)],
        5 + 11 * some,
        small=2,
        after=sent,
        flops=some * flops,
    )
    x2_moved = exchange(x2)
    held_back = grad_moved
    if hierarchical:
        held_back = [marker(*grad_moved[2:])]

    block_tails = [rows_w, rows_w, rows_w, rows_3, rows_w, rows_h, rows_h, rows_w]
    time_tails = [rows_w, rows_w, rows_w, rows_w, rows_w, rows_h, rows_h, rows_w]
    input_grad, result, *alone = single.call(
        alone_both,
        [("pack", frames), ("pack", output_grad)] + space_args + time_args,
        [whole, whole] + steps(1, *block_tails) + steps(1, *time_tails),
        scratch=[
            pltpu.VMEM((tokens, LANES), F32),
            pltpu.VMEM((tokens, LANES), F32),
            pltpu.VMEM(rows_3, BF),
            pltpu.VMEM((HEADS, tokens, tokens), BF),
            pltpu.VMEM(rows_h, BF),
            pltpu.VMEM(rows_h, BF),
            pltpu.VMEM(rows_w, BF),
        ]
        + work_shapes(tokens),
        flops=6 * flops,
        after=(x2, *held_back),
    )
    sz0_one, so_one, se1_one, sgqkv_one, sz1_one, seu_one, sh_one, se2_one = alone[:8]
    tz0_one, to_one, te1_one, tgv_one, tz1_one, teu_one, th_one, te2_one = alone[8:]

    time_outs = [(x2.shape, BF)] * 2 + [
        (shape, BF)
        for shape in (shared_w, shared_3, shared_w, shared_w, shared_w, shared_h, shared_h, shared_w)
    ]
    *g0, out, tz0, tgqkv, to, te1, tz1, teu, th, te2 = manual_call(
        functools.partial(time_kernel, len(grad_moved), len(moved_outs)),
        (clip_labels, ids),
        [row(time_gain), row(time_scale), x2_moved, *grad_moved]
        + [time_input, time_output, time_up, time_down],
        moved_outs + time_outs[1:],
        [(x2.shape, BF)] * 2
        + [(w.shape, BF) for w in (time_input, time_output, time_up, time_down)]
        + time_outs
        + [
            (shared_3, BF),
            (square, BF),
            (shared_h, BF),
            ((some, tokens, tokens), F32),
            (shared_w, BF),
            ((some, 4, tokens, tokens), F32),
            ((some, 2, tokens, CHUNK), BF),
            ((some, 4, tokens, tokens), BF),
            (square, BF),
        ],
        14 + 8 * some + 9,
        small=2,
        after=(sz0_one,),
        flops=3 * some * flops,
    )
    g0_moved = exchange_pieces(g0)
    out, g0_moved = lax.optimization_barrier((out, g0_moved))
    out_moved = exchange(out)

    held_back = ()
    everything = packs * tokens
    feed_shapes = [(1, width // 8), (width // 8, hidden), (hidden // 8, width)]
    attend_shapes = [(1, width // 8), (width // 8, 3 * width), (width // 8, width)]
    time_shared = [tz1, teu, te2, th, tz0, tgqkv, to, te1]
    time_one = [tz1_one, teu_one, te2_one, th_one, tz0_one, tgv_one, to_one, te1_one]
    if hierarchical:
        parts_shapes = [((4, 4, 96, CHUNK), BF)] * 4
        time_terms = manual_call(
            time_weights_kernel,
            ids,
            time_shared + time_one,
            parts_shapes,
            [((everything, a.shape[2]), BF) for a in time_shared] + parts_shapes,
            8 * packs + 20,
            flops=packs * flops,
        )
        time_got = [swap(other, "tm", 8, 1) for other in time_terms[1::2]]
        time_far = far_parts(time_terms[::2], time_got, marker(*g0_moved[2:]))
        held_back = time_far
    else:
        grad_one = jnp.pad(tgv_one, ((0, 0), (0, 0), (2 * width, 0)))
        joined = [joint(a, b) for a, b in zip(time_shared, time_one[:5] + [grad_one] + time_one[6:])]
        time_grads = plain_grads(joined[0], joined[1], joined[3], joined[2], time_up, time_scale)
        time_grads += plain_grads(joined[4], joined[5], joined[6], joined[7], time_input, time_gain)

    space_one = [sz1_one, seu_one, sh_one, se2_one, sz0_one, sgqkv_one, so_one, se1_one]
    whole_shapes = [((everything, a.shape[2]), BF) for a in space_one]
    parts_shapes = [((4, 4, 96, CHUNK), BF)] * 4
    sg1, sgqkv, *weights = manual_call(
        functools.partial(space_kernel, hierarchical, len(g0_moved)),
        ids,
        [row(space_scale), sinv1, *g0_moved, sslope, sz1, space_output, space_up, space_down]
        + [sqkv, sp, sh, sz0, so]
        + space_one,
        [(shared_w, F32), (shared_3, BF)]
        + (parts_shapes if hierarchical else [whole_shapes[i] for i in (1, 3, 7)]),
        [
            (x2.shape, BF),
            (sslope.shape, BF),
            (space_output.shape, BF),
            (space_up.shape, BF),
            (space_down.shape, BF),
            (sqkv.shape, BF),
            (sp.shape, BF),
            (shared_w, BF),
            (shared_w, F32),
            ((some, 4, tokens, tokens), BF),
            (square, BF),
        ]
        + whole_shapes
        + (parts_shapes if hierarchical else []),
        96,
        small=2,
        after=held_back,
        flops=2 * packs * flops,
    )
    held_back = ()
    if hierarchical:
        time_got, sgqkv = lax.optimization_barrier((time_got, sgqkv))
        time_mine = time_terms[::2]
        time_halves, time_near = near_parts(time_mine, time_got, time_far)
        mine = weights[::2]
        got = [swap(other, "tm", 8, 1) for other in weights[1::2]]
        far = far_parts(mine, got, marker(time_near[1]))
        held_back = far
    input_grad, result = shared.call(
        space_back_in,
        [
            ("step", sgqkv),
            ("whole", space_input),
            ("whole", row(space_gain)),
            ("step", sz0),
            ("step", sinv0),
            ("step", sg1),
            ("moved", out_moved),
        ],
        [("pack", frames.shape, F32, input_grad), ("pack", frames.shape, F32, result)],
        flops=flops // 4,
        after=held_back,
    )
    if hierarchical:
        time_halves, input_grad = lax.optimization_barrier((time_halves, input_grad))
        time_rows = stream_rows(time_mine, time_got, time_halves, time_near)
        time_last = z_got(time_rows)
        time_final = add(time_rows[0], *time_last)
        final = z_sum(stream_rows(mine, got, *near_parts(mine, got, far), marker(*time_last)))
        grads = finish_call(
            finish_kernel,
            ids,
            gather_parts(final),
            [(space_up, space_scale), (space_input, space_gain)],
            feed_shapes + attend_shapes,
        )
        feed_grads, attend_grads = grads[:3], grads[3:]
        time_grads = finish_call(
            finish_kernel,
            ids,
            gather_parts(time_final),
            [(time_up, time_scale), (time_input, time_gain)],
            feed_shapes + attend_shapes,
        )
    else:
        have = some * tokens
        seu, se2, se1 = [a[:have].reshape(some, tokens, -1) for a in weights]
        feed_grads = plain_grads(
            joint(sz1, sz1_one),
            joint(seu, seu_one),
            joint(sh, sh_one),
            joint(se2, se2_one),
            space_up,
            space_scale,
        )
        attend_grads = plain_grads(
            joint(sz0, sz0_one),
            joint(sgqkv, sgqkv_one),
            joint(so, so_one),
            joint(se1, se1_one),
            space_input,
            space_gain,
        )
    grads = attend_grads + feed_grads + time_grads[3:] + time_grads[:3]
    return (result, input_grad, *grads)


def joint(shared, one):
    return jnp.concatenate([shared, one]).reshape(-1, shared.shape[-1])


def solution(mesh):
    tokens = P("stream", "tm", None, None)
    vector, matrix = P("tm"), P("tm", None)
    return jax.shard_map(
        functools.partial(per_device, mesh.shape["tm"], mesh.shape["stream"]),
        mesh=mesh,
        in_specs=(tokens,) + (P(),) * 12 + (P("stream", None), tokens),
        out_specs=(tokens, tokens) + (vector, matrix, matrix, vector, matrix, matrix) * 2,
        check_vma=False,
    )
```
